512 devices in a mesh: inst: 64 (over x, y, z_hi, core), tensor: 8 (over z_lo).
Axes of the slice: x: 4, y: 4, z: 16 (z_hi: 2, z_lo: 8; z = z_hi * 8 + z_lo), core: 2. Of those that a mesh axis runs over, the one named last changes fastest.
Arguments:
- hidden_rows: bfloat16 [32768, 8192], P('inst', 'tensor'), may hold values from -50 to 50
- kv_weight: bfloat16 [8192, 2048], P('tensor'), may hold values from -0.0625 to 0.0625
- norm_gain: float32 [8192], P('tensor'), may hold values from 0.5 to 2
- resident_cache: bfloat16 [2048, 16384], P('tensor', 'inst'), may hold values from -12 to 12
- queries: bfloat16 [2, 1024, 8192], P(None, 'inst', 'tensor'), may hold values from -160 to 160
- fresh_hidden: bfloat16 [2, 1024, 8192], P(None, 'inst', 'tensor'), may hold values from -50 to 50
- move_dest: int32 [2048], P('inst'), may hold values from 0 to 63, as said below
- move_len: int32 [2048], P('inst'), may hold values from 1 to 16
- resident_len: int32 [1024], P('inst'), may hold values from 1 to 16
- decode_ids: int32 [1024], P('inst'), may hold values from 0 to 47, as said below
Outputs:
- rebuilt: bfloat16 [2048, 32768], P('tensor', 'inst')
- attended: bfloat16 [2, 1024, 8192], P(None, 'inst', 'tensor')
The draws below stay inside these ranges and needn't reach their ends.
Inputs may be any that keep to these rules, and one draw needn't show every extreme that they name: `move_dest`: each instance sends its 32 requests to 32 different instances, never to itself, and receives exactly 32 requests, each from a different instance. `decode_ids`: the 16 entries of one instance are different; 0 to 15 name its staying requests, 16 + a its arrived request a.
All inputs are finite; a program needn't handle non-finite values.
Results may differ from the reference program's by a relative error of at most 0.019.
Values may be sent and summed in bfloat16 or wider, within the bound.
No kernel may reach another device: no remote copies, remote signals or barrier semaphores. Data moves between devices by JAX's collectives and lax.ppermute only.
A program may use at most 64 MiB of HBM per device.

```python
import math
import jax
import jax.numpy as jnp
from jax import lax

D = 8192
KVH = 8
GROUP = 8
HD = 128
QHEADS = 64
CTX = 16
SLOTS = 16
BATCH = 16
STEPS = 2
N_INST = 64
N_TENSOR = 8


def draw_hidden_rows(key, part):
    key = jax.random.fold_in(key, 11)
    first, second = jax.random.split(key, 2)
    count = N_INST * (N_INST // 2) * CTX
    column = jnp.arange(D, dtype=jnp.float32) / D
    base = jnp.clip(jax.random.normal(first, (count, D), jnp.float32), -4.0, 4.0)
    row_scale = jnp.exp(jax.random.uniform(second, (count, 1), jnp.float32, math.log(0.3), math.log(3.0)))
    column_scale = 10.0 ** (column - 0.5)
    return (base * row_scale * column_scale[None, :]).astype(jnp.bfloat16)


def draw_fresh_hidden(key, part):
    key = jax.random.fold_in(key, 12)
    first, second = jax.random.split(key, 2)
    shape = (STEPS, N_INST * BATCH, D)
    column = jnp.arange(D, dtype=jnp.float32) / D
    base = jnp.clip(jax.random.normal(first, shape, jnp.float32), -4.0, 4.0)
    row_scale = jnp.exp(jax.random.uniform(second, (STEPS, N_INST * BATCH, 1), jnp.float32, math.log(0.3), math.log(3.0)))
    column_scale = 10.0 ** (column - 0.5)
    return (base * row_scale * column_scale).astype(jnp.bfloat16)


def draw_queries(key, part):
    key = jax.random.fold_in(key, 13)
    first = jax.random.fold_in(key, 0)
    base = jnp.clip(jax.random.normal(first, (STEPS, N_INST * BATCH, QHEADS * HD), jnp.float32), -4.0, 4.0)
    return base.astype(jnp.bfloat16)


def draw_move_dest(key, part):
    key = jax.random.fold_in(key, 21)
    moving = N_INST // 2
    half = N_INST // 2
    others = jax.random.permutation(key, N_INST - 3).astype(jnp.int32) + 2
    others = jnp.where(others >= half, others + 1, others)
    offsets = jnp.concatenate([jnp.array([1, half], dtype=jnp.int32), others[:moving - 2]])
    source = jnp.arange(N_INST, dtype=jnp.int32)[:, None]
    within = jnp.arange(moving, dtype=jnp.int32)[None, :]
    target = (source + jnp.take(offsets, (within + source) % moving)) % N_INST
    return target.reshape(-1).astype(jnp.int32)


def draw_move_len(key, part):
    key = jax.random.fold_in(key, 22)
    first, second = jax.random.split(key)
    moving = N_INST // 2
    values = jax.random.randint(first, (N_INST, moving), 1, CTX + 1)
    longest = jax.random.randint(second, (N_INST, 1), 0, moving)
    values = jnp.where(jnp.arange(moving)[None, :] == longest, CTX, values)
    return values.reshape(-1).astype(jnp.int32)


def draw_resident_len(key, part):
    key = jax.random.fold_in(key, 23)
    first, second = jax.random.split(key)
    values = jax.random.randint(first, (N_INST, SLOTS), 1, CTX + 1)
    longest = jax.random.randint(second, (N_INST, 1), 0, SLOTS)
    values = jnp.where(jnp.arange(SLOTS)[None, :] == longest, CTX, values)
    return values.reshape(-1).astype(jnp.int32)


def draw_decode_ids(key, part):
    key = jax.random.fold_in(key, 24)
    keys = jax.random.split(key, N_INST)
    total = SLOTS + N_INST // 2
    picks = jax.vmap(lambda single: jax.random.permutation(single, total)[:BATCH])(keys)
    return picks.reshape(-1).astype(jnp.int32)


def steps_of(key, shape, cuts, least, largest):
    gain = 1.0
    for position, blocks in cuts:
        steps = jax.random.uniform(jax.random.fold_in(jax.random.fold_in(key, 6), position), (blocks,), jnp.float32, least / len(cuts), largest / len(cuts))
        gain = gain * jnp.repeat(jnp.exp(steps), shape[position] // blocks).reshape((-1,) + (1,) * (len(shape) - 1 - position))
    return gain


def scatter_about(rng, shape, spread, limit, cuts=(), kind=jnp.bfloat16):
    factor_of = steps_of(rng, shape, cuts, -0.22, 0.18) if cuts else 1.0
    entries = jax.random.normal(rng, shape, jnp.float32) * spread * factor_of
    return jnp.minimum(jnp.maximum(entries, -limit), limit).astype(kind)


def setup_inputs(seed: int = 0) -> dict:
    splits = jax.random.split(jax.random.key(seed), 11)
    return {
        "hidden_rows": draw_hidden_rows(jax.random.fold_in(splits[10], 71), 0),
        "kv_weight": scatter_about(splits[1], (D, 2 * KVH * HD), D ** -0.5, 0.0625, ((0, 8),)),
        "norm_gain": jnp.clip(jnp.exp(math.log(2.0) - 1.3862944 * jax.random.uniform(splits[2], (D,), jnp.float32) ** steps_of(splits[2], (D,), ((0, 8),), -0.2, 0.2)), 0.5, 2.0),
        "resident_cache": scatter_about(splits[3], (2 * KVH * HD, N_INST * SLOTS * CTX), 2.0, 12.0, ((0, 8), (1, 64))),
        "queries": draw_queries(jax.random.fold_in(splits[10], 71), 0),
        "fresh_hidden": draw_fresh_hidden(jax.random.fold_in(splits[10], 71), 0),
        "move_dest": draw_move_dest(jax.random.fold_in(splits[10], 71), 0),
        "move_len": draw_move_len(jax.random.fold_in(splits[10], 71), 0),
        "resident_len": draw_resident_len(jax.random.fold_in(splits[10], 71), 0),
        "decode_ids": draw_decode_ids(jax.random.fold_in(splits[10], 71), 0),
    }


def round_trip(values):
    return lax.optimization_barrier(values.astype(jnp.bfloat16)).astype(jnp.float32)

def project_rows(source_rows, kv_weight, norm_gain):
    count = source_rows.shape[0]
    width = kv_weight.shape[1]
    widened = source_rows.astype(jnp.float32)
    squares = lax.optimization_barrier(jnp.sum(widened * widened, axis=1))
    scaled = (widened * norm_gain).astype(jnp.bfloat16)
    blocks = scaled.reshape(count, N_TENSOR, D // N_TENSOR).astype(jnp.float32)
    weight_blocks = kv_weight.reshape(N_TENSOR, D // N_TENSOR, width).astype(jnp.float32)
    terms = jnp.einsum('rtf,tfc->trc', blocks, weight_blocks)
    total = lax.optimization_barrier(jnp.sum(round_trip(terms), axis=0))
    return (total * lax.rsqrt(squares / D + 1e-06)[:, None]).astype(jnp.bfloat16)

def attend(query_step, cache_keys, cache_values, fresh_keys, fresh_values, valid):
    scale = 1.0 / HD ** 0.5
    query_wide = query_step.astype(jnp.float32)
    cached = jnp.einsum('bhgd,hdbp->bhgp', query_wide, cache_keys.astype(jnp.float32)) * scale
    recent = jnp.einsum('bhgd,tbhd->bhgt', query_wide, fresh_keys.astype(jnp.float32)) * scale
    mask = valid[:, None, None, :]
    cached = jnp.where(mask, cached, -1e+30)
    top = jnp.maximum(lax.optimization_barrier(jnp.max(cached, axis=-1)), lax.optimization_barrier(jnp.max(recent, axis=-1)))
    cached_exp = jnp.where(mask, jnp.exp(cached - top[..., None]), 0.0)
    recent_exp = jnp.exp(recent - top[..., None])
    total = lax.optimization_barrier(jnp.sum(cached_exp, axis=-1)) + lax.optimization_barrier(jnp.sum(recent_exp, axis=-1))
    cached_prob = round_trip(cached_exp / total[..., None])
    recent_prob = round_trip(recent_exp / total[..., None])
    output = jnp.einsum('bhgp,hdbp->bhgd', cached_prob, cache_values.astype(jnp.float32))
    output = output + jnp.einsum('bhgt,tbhd->bhgd', recent_prob, fresh_values.astype(jnp.float32))
    return output.astype(jnp.bfloat16).reshape(query_step.shape[0], -1)

def reference(hidden_rows, kv_weight, norm_gain, resident_cache, queries, fresh_hidden, move_dest, move_len, resident_len, decode_ids):
    width = 2 * KVH * HD
    moving = N_INST // 2
    projected = lax.map(lambda rows: project_rows(rows, kv_weight, norm_gain), hidden_rows.reshape(N_INST, moving * CTX, D))
    projected = projected.reshape(N_INST, moving, CTX, width)
    targets = move_dest.reshape(N_INST, moving)
    lengths = move_len.reshape(N_INST, moving)
    instances = jnp.arange(N_INST, dtype=jnp.int32)
    matched = (targets[None, :, :] == instances[:, None, None]).astype(jnp.int32)
    present = lax.optimization_barrier(jnp.sum(matched, axis=2))
    which = lax.optimization_barrier(jnp.sum(matched * jnp.arange(moving, dtype=jnp.int32)[None, None, :], axis=2))
    sizes = lax.optimization_barrier(jnp.sum(matched * lengths[None, :, :], axis=2))
    order = jnp.cumsum(present, axis=1) - 1
    picked = present[:, None, :] * (order[:, None, :] == jnp.arange(moving, dtype=jnp.int32)[None, :, None]).astype(jnp.int32)
    source = lax.optimization_barrier(jnp.sum(picked * instances[None, None, :], axis=2))
    chosen = lax.optimization_barrier(jnp.sum(picked * which[:, None, :], axis=2))
    arrived_len = lax.optimization_barrier(jnp.sum(picked * sizes[:, None, :], axis=2))
    blocks = projected[source, chosen]
    keep = jnp.arange(CTX, dtype=jnp.int32)[None, None, :] < arrived_len[:, :, None]
    blocks = jnp.where(keep[..., None], blocks, jnp.zeros((), jnp.bfloat16))
    rebuilt = jnp.transpose(blocks, (3, 0, 1, 2)).reshape(width, N_INST * moving * CTX)
    fresh_wide = fresh_hidden.astype(jnp.float32)
    fresh_squares = lax.optimization_barrier(jnp.sum(fresh_wide * fresh_wide, axis=2))
    fresh_scaled = (fresh_wide * norm_gain).astype(jnp.bfloat16).astype(jnp.float32)
    fresh_raw = jnp.einsum('sbf,fc->sbc', fresh_scaled, kv_weight.astype(jnp.float32))
    fresh_kv = (fresh_raw * lax.rsqrt(fresh_squares / D + 1e-06)[..., None]).astype(jnp.bfloat16)
    resident_by = jnp.transpose(resident_cache.reshape(width, N_INST, SLOTS * CTX), (1, 0, 2))
    arrived_by = jnp.transpose(rebuilt.reshape(width, N_INST, moving * CTX), (1, 0, 2))
    lengths_by = jnp.concatenate([resident_len.reshape(N_INST, SLOTS), arrived_len], axis=1)
    ids_by = decode_ids.reshape(N_INST, BATCH)
    query_by = jnp.transpose(queries.reshape(STEPS, N_INST, BATCH, KVH, GROUP, HD), (1, 0, 2, 3, 4, 5))
    fresh_by = jnp.transpose(fresh_kv.reshape(STEPS, N_INST, BATCH, KVH, 2, HD), (1, 0, 2, 3, 4, 5))

    def one_instance(packed):
        resident_here, arrived_here, lengths_here, ids_here, query_here, fresh_here = packed
        combined = jnp.concatenate([resident_here, arrived_here], axis=1)
        positions = (ids_here[:, None] * CTX + jnp.arange(CTX, dtype=jnp.int32)[None, :]).reshape(-1)
        gathered = jnp.take(combined, positions, axis=1).reshape(KVH, 2, HD, BATCH, CTX)
        valid = jnp.arange(CTX, dtype=jnp.int32)[None, :] < jnp.take(lengths_here, ids_here)[:, None]
        outputs = []
        for step in range(STEPS):
            outputs.append(attend(query_here[step], gathered[:, 0], gathered[:, 1], fresh_here[:step + 1, :, :, 0], fresh_here[:step + 1, :, :, 1], valid))
        return jnp.stack(outputs)
    attended = lax.map(one_instance, (resident_by, arrived_by, lengths_by, ids_by, query_by, fresh_by))
    attended = jnp.transpose(attended, (1, 0, 2, 3)).reshape(STEPS, N_INST * BATCH, QHEADS * HD)
    return (rebuilt, attended)
```

```python
import jax
import jax.numpy as jnp
from jax import lax
from jax.sharding import PartitionSpec as P

D = 8192
GROUP = 8
HD = 128
STEPS = 2


def partial_sums(rows, kv_weight, norm_gain):
    widened = rows.astype(jnp.float32)
    squares = jnp.sum(widened * widened, axis=1)
    scaled = (widened * norm_gain).astype(jnp.bfloat16)
    partial_value = jnp.dot(scaled, kv_weight, preferred_element_type=jnp.float32)
    return partial_value.astype(jnp.bfloat16), squares


def sum_over_tensor(values):
    tensors = lax.axis_size("tensor")
    distance = 1
    while distance < tensors:
        pairs = [(i, i ^ distance) for i in range(tensors)]
        values = values + lax.ppermute(values, "tensor", pairs)
        distance *= 2
    return values


def arrivals(arrived_len, requests):
    senders = arrived_len.shape[0]
    living = (arrived_len > 0).astype(jnp.int32)
    ranking = jnp.cumsum(living) - 1
    picked = living[None, :] * (
        ranking[None, :] == jnp.arange(requests, dtype=jnp.int32)[:, None]
    ).astype(jnp.int32)
    source = jnp.sum(picked * jnp.arange(senders, dtype=jnp.int32)[None, :], axis=1)
    return (source, jnp.sum(picked * arrived_len[None, :], axis=1))


def attend(query_step, cache_keys, cache_values, fresh_keys, fresh_values, valid):
    scale = 1.0 / HD**0.5
    cached = (
        jnp.einsum("bhgd,hdbp->bhgp", query_step, cache_keys, preferred_element_type=jnp.float32)
        * scale
    )
    recent = (
        jnp.einsum("bhgd,tbhd->bhgt", query_step, fresh_keys, preferred_element_type=jnp.float32)
        * scale
    )
    masking = valid[:, None, None, :]
    cached = jnp.where(masking, cached, -1e30)
    highest = jnp.maximum(jnp.max(cached, axis=-1), jnp.max(recent, axis=-1))
    cached_exp = jnp.where(masking, jnp.exp(cached - highest[..., None]), 0.0)
    recent_exp = jnp.exp(recent - highest[..., None])
    denominator = jnp.sum(cached_exp, axis=-1) + jnp.sum(recent_exp, axis=-1)
    cached_prob = (cached_exp / denominator[..., None]).astype(jnp.bfloat16)
    recent_prob = (recent_exp / denominator[..., None]).astype(jnp.bfloat16)
    output = jnp.einsum(
        "bhgp,hdbp->bhgd", cached_prob, cache_values, preferred_element_type=jnp.float32
    )
    output = output + jnp.einsum(
        "bhgt,tbhd->bhgd", recent_prob, fresh_values, preferred_element_type=jnp.float32
    )
    return output.astype(jnp.bfloat16).reshape(query_step.shape[0], -1)


def shards(
    hidden_rows,
    kv_weight,
    norm_gain,
    resident_cache,
    queries,
    fresh_hidden,
    move_dest,
    move_len,
    resident_len,
    decode_ids,
):
    requests = move_dest.shape[0]
    context = hidden_rows.shape[0] // requests
    leaving = hidden_rows.shape[0]
    instances = lax.axis_size("inst")
    owned = kv_weight.shape[1] // lax.axis_size("tensor")
    heads_here = owned // (2 * HD)
    batch_rows = decode_ids.shape[0]
    nothing = jnp.zeros((), jnp.bfloat16)
    targets = jnp.arange(instances, dtype=jnp.int32)
    matched = (move_dest[None, :] == targets[:, None]).astype(jnp.int32)
    chosen = jnp.sum(matched * jnp.arange(requests, dtype=jnp.int32)[None, :], axis=1)
    sent_len = jnp.sum(matched * move_len[None, :], axis=1)
    sending = (sent_len > 0)[:, None, None]

    all_rows = jnp.concatenate(
        [hidden_rows, fresh_hidden.reshape(STEPS * batch_rows, -1)], axis=0
    )
    partial_value, squares = partial_sums(all_rows, kv_weight, norm_gain)
    raw = lax.psum_scatter(partial_value, "tensor", scatter_dimension=1, tiled=True)
    squares = sum_over_tensor(squares)
    arrived_len = lax.all_to_all(sent_len, "inst", split_axis=0, concat_axis=0, tiled=True)
    source, kept_len = arrivals(arrived_len, requests)
    kv_rows = (
        raw.astype(jnp.float32) * lax.rsqrt(squares / D + 1e-06)[:, None]
    ).astype(jnp.bfloat16)
    fresh_kv = kv_rows[leaving:].reshape(STEPS, batch_rows, heads_here, 2, HD)

    blocks = kv_rows[:leaving].reshape(requests, context, owned)
    outgoing = jnp.where(sending, jnp.take(blocks, chosen, axis=0), nothing)
    arrived = lax.all_to_all(outgoing, "inst", split_axis=0, concat_axis=0, tiled=True)
    gathered_rows = jnp.take(arrived, source, axis=0)
    keeping = jnp.arange(context, dtype=jnp.int32)[None, :] < kept_len[:, None]
    rebuilt = jnp.where(keeping[:, :, None], gathered_rows, nothing)
    rebuilt = rebuilt.reshape(requests * context, owned).T
    combined = jnp.concatenate([resident_cache, rebuilt], axis=1)
    lengths = jnp.concatenate([resident_len, kept_len])
    positions = (
        decode_ids[:, None] * context + jnp.arange(context, dtype=jnp.int32)[None, :]
    ).reshape(-1)
    gathered = jnp.take(combined, positions, axis=1).reshape(heads_here, 2, HD, batch_rows, context)
    valid = jnp.arange(context, dtype=jnp.int32)[None, :] < jnp.take(lengths, decode_ids)[:, None]
    query_heads = queries.reshape(STEPS, batch_rows, heads_here, GROUP, HD)
    outputs = []
    for step in range(STEPS):
        outputs.append(
            attend(
                query_heads[step],
                gathered[:, 0],
                gathered[:, 1],
                fresh_kv[: step + 1, :, :, 0],
                fresh_kv[: step + 1, :, :, 1],
                valid,
            )
        )
    return (rebuilt, jnp.stack(outputs))


def solution(mesh):
    in_specs = (
        P("inst", "tensor"),
        P("tensor", None),
        P("tensor"),
        P("tensor", "inst"),
        P(None, "inst", "tensor"),
        P(None, "inst", "tensor"),
        P("inst"),
        P("inst"),
        P("inst"),
        P("inst"),
    )
    out_specs = (P("tensor", "inst"), P(None, "inst", "tensor"))
    return jax.shard_map(shards, mesh=mesh, in_specs=in_specs, out_specs=out_specs, check_vma=False)
```

```python
import jax
import jax.numpy as jnp
from jax import lax
from jax.experimental import pallas as pl
from jax.experimental.pallas import tpu as pltpu
from jax.sharding import PartitionSpec as P

D = 8192
GROUP = 8
HD = 128
STEPS = 2
TILE = 128
EXTRA = 16
ABSENT = 2.0**100
BF = jnp.bfloat16
F32 = jnp.float32
VMEM_BYTES = 40 * 1024 * 1024


def ring_of(tensors):
    return list(range(0, tensors, 2)) + list(range(tensors - 1, 0, -2))


def iota(shape, axis):
    return lax.broadcasted_iota(jnp.int32, shape, axis)


def dot(a, b, contract=((1,), (0,))):
    return lax.dot_general(a, b, (contract, ((), ())), preferred_element_type=F32)


def first_chunks(order, hidden, fresh, gain, weight_a, weight_b, out_a, out_b, scaled, extra):
    rows = hidden.shape[0] + fresh.shape[0]
    wide = jnp.concatenate([hidden[...], fresh[...]], axis=0).astype(F32)
    scaled[...] = (wide * gain[...]).astype(BF)
    square = wide * wide
    high = square.astype(BF)
    low = (square - high.astype(F32)).astype(BF)
    lanes = out_a.shape[1]
    ones = jnp.ones((EXTRA, wide.shape[1]), BF)
    total = jnp.zeros((EXTRA, lanes), F32)
    for index, start in enumerate(range(0, rows, lanes)):
        stop = min(start + lanes, rows)
        part = dot(ones, high[start:stop], ((1,), (1,))) + dot(ones, low[start:stop], ((1,), (1,)))
        if stop - start < lanes:
            part = jnp.concatenate([part, jnp.zeros((EXTRA, lanes - stop + start), F32)], axis=1)
        total = jnp.where(iota((EXTRA, lanes), 0) == index, part, total)
    extra[...] = total.astype(BF)
    for weight, out in ((weight_a, out_a), (weight_b, out_b)):
        out[:rows, :] = dot(scaled[...], weight[...]).astype(BF)
        out[rows:, :] = extra[...]


def later_chunks(order, scaled, extra, *refs):
    count = len(refs) // 2
    rows = scaled.shape[0]
    for weight, out in zip(refs[:count], refs[count:]):
        out[:rows, :] = dot(scaled[...], weight[...]).astype(BF)
        out[rows:, :] = extra[...]


def whole(shape):
    return pl.BlockSpec(shape, lambda i, *_: (0,) * len(shape))


def project_chunks(hidden, fresh, gain, weight, order, lanes):
    rows, depth = hidden.shape[0] + fresh.shape[0], hidden.shape[1]
    chunk = jax.ShapeDtypeStruct((rows + EXTRA, lanes), BF)
    chunk_spec = whole((rows + EXTRA, lanes))
    scaled_type = jax.ShapeDtypeStruct((rows, depth), BF)
    extra_type = jax.ShapeDtypeStruct((EXTRA, lanes), BF)
    tensors = order.shape[0]

    def column_block(place):
        return pl.BlockSpec((depth, lanes), lambda i, order: (0, order[place]))

    params = pltpu.CompilerParams(vmem_limit_bytes=VMEM_BYTES)
    cost = lambda count: pl.CostEstimate(
        flops=2 * rows * depth * lanes * count,
        bytes_accessed=2 * (rows * depth + count * (depth + rows) * lanes),
        transcendentals=0,
    )
    out_a, out_b, scaled, extra = pl.pallas_call(
        first_chunks,
        grid_spec=pltpu.PrefetchScalarGridSpec(
            num_scalar_prefetch=1,
            grid=(1,),
            in_specs=[
                whole(hidden.shape),
                whole(fresh.shape),
                whole(gain.shape),
                column_block(0),
                column_block(1),
            ],
            out_specs=[chunk_spec, chunk_spec, whole(scaled_type.shape), whole(extra_type.shape)],
        ),
        out_shape=[chunk, chunk, scaled_type, extra_type],
        compiler_params=params,
        cost_estimate=cost(2),
        name="first_chunks",
    )(order, hidden, fresh, gain, weight, weight)
    rest = tensors - 2
    later = pl.pallas_call(
        later_chunks,
        grid_spec=pltpu.PrefetchScalarGridSpec(
            num_scalar_prefetch=1,
            grid=(1,),
            in_specs=[whole(scaled.shape), whole(extra.shape)]
            + [column_block(2 + i) for i in range(rest)],
            out_specs=[chunk_spec] * rest,
        ),
        out_shape=[chunk] * rest,
        compiler_params=params,
        cost_estimate=cost(rest),
        name="later_chunks",
    )(order, scaled, extra, *([weight] * rest))
    return [out_a, out_b, *later]


def ring_sums(hidden, fresh, gain, weight, lanes):
    tensors = lax.axis_size("tensor")
    ring = ring_of(tensors)
    ahead, behind = tensors // 2, tensors - 1 - tensors // 2
    offsets = []
    for step in range(ahead):
        offsets.append(ahead - step)
        if step < behind:
            offsets.append(step - behind)
    offsets.append(0)
    table = [
        [ring[(ring.index(device) + offset) % tensors] for offset in offsets]
        for device in range(tensors)
    ]
    order = jnp.array(table, jnp.int32)[lax.axis_index("tensor")]
    chunks = project_chunks(hidden, fresh, gain, weight, order, lanes)
    forward = [(ring[i], ring[(i + 1) % tensors]) for i in range(tensors)]
    backward = [(b, a) for a, b in forward]
    sums = {True: None, False: None}
    for offset, chunk in zip(offsets[:-1], chunks[:-1]):
        way = offset > 0
        if sums[way] is not None:
            chunk = (sums[way].astype(F32) + chunk.astype(F32)).astype(BF)
        sums[way] = lax.ppermute(chunk, "tensor", forward if way else backward)
    return sums[True], sums[False], chunks[-1]


def finish_rows(chosen, sent_len, ahead, behind, own, outgoing, fresh_kv, kept):
    total = ahead[...].astype(F32) + behind[...].astype(F32) + own[...].astype(F32)
    rows, lanes = total.shape[0] - EXTRA, total.shape[1]
    leaving = rows - fresh_kv.shape[0]
    squares = total[rows:]
    for start in range(0, rows, TILE):
        size = min(TILE, rows - start)
        across = squares[start // lanes : start // lanes + 1, start % lanes : start % lanes + TILE]
        diagonal = iota((size, TILE), 0) == iota((size, TILE), 1)
        column = jnp.sum(jnp.where(diagonal, across, 0.0), axis=1, keepdims=True)
        kept[start : start + size, :] = (
            total[start : start + size] * lax.rsqrt(column / D + 1e-06)
        ).astype(BF)
    fresh_kv[...] = kept[leaving:, :]
    context = outgoing.shape[1]

    def place(index, carry):
        start = pl.multiple_of(chosen[index] * context, context)
        block = kept[pl.ds(start, context), :]
        present = iota((context, lanes), 0) < sent_len[index]
        outgoing[index] = jnp.where(present, block, jnp.full((), ABSENT, BF))
        return carry

    lax.fori_loop(0, outgoing.shape[0], place, 0, unroll=8)


def finish(chosen, sent_len, ahead, behind, own, fresh_rows, context):
    rows, lanes = own.shape[0] - EXTRA, own.shape[1]
    slots = chosen.shape[0]
    return pl.pallas_call(
        finish_rows,
        grid_spec=pltpu.PrefetchScalarGridSpec(
            num_scalar_prefetch=2,
            grid=(1,),
            in_specs=[whole(own.shape)] * 3,
            out_specs=[whole((slots, context, lanes)), whole((fresh_rows, lanes))],
            scratch_shapes=[pltpu.VMEM((rows, lanes), BF)],
        ),
        out_shape=[
            jax.ShapeDtypeStruct((slots, context, lanes), BF),
            jax.ShapeDtypeStruct((fresh_rows, lanes), BF),
        ],
        compiler_params=pltpu.CompilerParams(vmem_limit_bytes=VMEM_BYTES),
        name="finish_rows",
    )(chosen, sent_len, ahead, behind, own)


def rebuild_and_attend(
    arrived, resident, resident_valid, queries, fresh, wanted, rebuilt, attended
):
    slots, context, lanes = arrived.shape
    steps, batch, width = queries.shape
    rows = slots * context
    columns = rebuilt.shape[1]
    held = resident.shape[1]
    heads = width // HD
    blocks = arrived[...].reshape(rows, lanes)
    valid = blocks[:, :TILE].astype(F32) < ABSENT / 2
    flags = jnp.where(valid, 1.0, 0.0).astype(BF)
    opening = jnp.where(iota((slots, rows), 1) == iota((slots, rows), 0) * context, 1.0, 0.0)
    living = dot(opening.astype(BF), flags).astype(BF)
    before = jnp.where(iota((rows, slots), 1) < iota((rows, slots), 0) // context, 1.0, 0.0)
    ranking = dot(before.astype(BF), living)
    target = ranking.astype(jnp.int32) * context + iota((rows, TILE), 0) % context
    target = jnp.where(valid, target, -1)
    routes = jnp.concatenate(
        [
            jnp.where(target == iota((rows, TILE), 1) + start, 1.0, 0.0).astype(BF)
            for start in range(0, columns, TILE)
        ],
        axis=1,
    )[:, :columns]
    moved = dot(blocks, routes, ((0,), (0,))).astype(BF)
    rebuilt[...] = moved
    filled = dot(jnp.ones((EXTRA, rows), BF), routes)[:1] > 0.5

    query = jnp.concatenate(
        [queries[s, :, h * HD : (h + 1) * HD] for s in range(steps) for h in range(heads)], axis=0
    )
    count = query.shape[0]
    scale = 1.0 / HD**0.5
    want = wanted[...]

    def request_of(size):
        return iota((count, size), 1) // context

    mask_held = (want == request_of(held)) & (resident_valid[...] > 0)
    mask_moved = (want == request_of(columns) + held // context) & filled
    line, mark = iota((count, steps * batch), 0), iota((count, steps * batch), 1)
    mask_fresh = (line % batch == mark % batch) & (mark // batch <= line // (heads * batch))
    lowest = -1e30
    score_held = jnp.where(mask_held, dot(query, resident[:HD, :]) * scale, lowest)
    score_moved = jnp.where(mask_moved, dot(query, moved[:HD]) * scale, lowest)
    score_fresh = jnp.where(
        mask_fresh, dot(query, fresh[:, :HD], ((1,), (1,))) * scale, lowest
    )
    top = jnp.maximum(
        jnp.maximum(
            jnp.max(score_held, axis=1, keepdims=True), jnp.max(score_moved, axis=1, keepdims=True)
        ),
        jnp.max(score_fresh, axis=1, keepdims=True),
    )
    exp_held = jnp.where(mask_held, jnp.exp(score_held - top), 0.0)
    exp_moved = jnp.where(mask_moved, jnp.exp(score_moved - top), 0.0)
    exp_fresh = jnp.where(mask_fresh, jnp.exp(score_fresh - top), 0.0)
    total = (
        jnp.sum(exp_held, axis=1, keepdims=True)
        + jnp.sum(exp_moved, axis=1, keepdims=True)
        + jnp.sum(exp_fresh, axis=1, keepdims=True)
    )
    across = ((1,), (1,))
    out = dot((exp_held / total).astype(BF), resident[HD:, :], across)
    out = out + dot((exp_moved / total).astype(BF), moved[HD:], across)
    out = out + dot((exp_fresh / total).astype(BF), fresh[:, HD:])
    out = out.astype(BF)
    for s in range(steps):
        for h in range(heads):
            start = (s * heads + h) * batch
            attended[s, :, h * HD : (h + 1) * HD] = out[start : start + batch]


def rebuild(arrived, resident, resident_valid, queries, fresh, wanted, columns):
    return pl.pallas_call(
        rebuild_and_attend,
        out_shape=[
            jax.ShapeDtypeStruct((arrived.shape[2], columns), BF),
            jax.ShapeDtypeStruct(queries.shape, BF),
        ],
        compiler_params=pltpu.CompilerParams(vmem_limit_bytes=VMEM_BYTES),
        name="rebuild_and_attend",
    )(arrived, resident, resident_valid, queries, fresh, wanted)


def shards(
    hidden_rows,
    kv_weight,
    norm_gain,
    resident_cache,
    queries,
    fresh_hidden,
    move_dest,
    move_len,
    resident_len,
    decode_ids,
):
    requests = move_dest.shape[0]
    context = hidden_rows.shape[0] // requests
    instances = lax.axis_size("inst")
    owned = kv_weight.shape[1] // lax.axis_size("tensor")
    assert owned == 2 * HD
    steps, batch_rows, features = fresh_hidden.shape
    heads = queries.shape[2] // HD
    targets = jnp.arange(instances, dtype=jnp.int32)
    matched = (move_dest[None, :] == targets[:, None]).astype(jnp.int32)
    chosen = jnp.sum(matched * jnp.arange(requests, dtype=jnp.int32)[None, :], axis=1)
    sent_len = jnp.sum(matched * move_len[None, :], axis=1)
    resident_valid = (
        jnp.arange(context, dtype=jnp.int32)[None, :] < resident_len[:, None]
    ).astype(jnp.int32)
    resident_valid = resident_valid.reshape(1, -1)
    wanted = jnp.tile(decode_ids, steps * heads)[:, None]

    ahead, behind, own = ring_sums(
        hidden_rows,
        fresh_hidden.reshape(steps * batch_rows, features),
        norm_gain[None, :],
        kv_weight,
        owned,
    )
    outgoing, fresh_kv = finish(
        chosen, sent_len, ahead, behind, own, steps * batch_rows, context
    )
    arrived = lax.all_to_all(outgoing, "inst", split_axis=0, concat_axis=0, tiled=True)
    return tuple(
        rebuild(
            arrived,
            resident_cache,
            resident_valid,
            queries,
            fresh_kv,
            wanted,
            requests * context,
        )
    )


def solution(mesh):
    in_specs = (
        P("inst", "tensor"),
        P("tensor", None),
        P("tensor"),
        P("tensor", "inst"),
        P(None, "inst", "tensor"),
        P(None, "inst", "tensor"),
        P("inst"),
        P("inst"),
        P("inst"),
        P("inst"),
    )
    out_specs = (P("tensor", "inst"), P(None, "inst", "tensor"))
    return jax.shard_map(shards, mesh=mesh, in_specs=in_specs, out_specs=out_specs, check_vma=False)
```

```python
import jax
import jax.numpy as jnp
from jax import lax
from jax.experimental import pallas as pl
from jax.experimental.pallas import tpu as pltpu
from jax.sharding import PartitionSpec as P

D = 8192
GROUP = 8
HD = 128
STEPS = 2
TILE = 128
CONTEXT = 16
EXTRA = 16
NOWHERE = 63
ABSENT = 2.0**100
BF = jnp.bfloat16
F32 = jnp.float32
VMEM_BYTES = 60 * 1024 * 1024


def ring_of(tensors):
    return list(range(0, tensors, 2)) + list(range(tensors - 1, 0, -2))


def iota(shape, axis):
    return lax.broadcasted_iota(jnp.int32, shape, axis)


def dot(a, b, contract=((1,), (0,))):
    return lax.dot_general(a, b, (contract, ((), ())), preferred_element_type=F32)


def plane_of(instance):
    return (instance >> 2) * 2 + (instance & 1)


def half_of(instance):
    return (instance >> 1) & 1


def first_chunks(
    order, dest, length, me, hidden, fresh, gain, weight_a, weight_b, out_a, out_b, scaled, extra, codes
):
    requests = dest.shape[0]
    context = hidden.shape[0] // requests
    rows, capacity = scaled.shape[0], scaled.shape[0] - fresh.shape[0]
    half = half_of(me[0])

    def crosses(j):
        return half_of(dest[j]) != half

    def count(j, crossing):
        return crossing + jnp.where(crosses(j), length[j], 0)

    crossing = lax.fori_loop(0, requests, count, jnp.int32(0), unroll=8)
    lane = iota((1, hidden.shape[0]), 1)

    def place(j, carry):
        next_cross, next_stay, target, code = carry
        cross = crosses(j)
        start = jnp.where(cross, next_cross, next_stay)
        place_here = (lane // context == j) & (lane % context < length[j])
        target = jnp.where(place_here, start + lane % context, target)
        inside = (lane >= start) & (lane < start + length[j])
        code = jnp.where(inside, plane_of(dest[j]) * context + lane - start, code)
        return (
            next_cross + jnp.where(cross, length[j], 0),
            next_stay + jnp.where(cross, 0, length[j]),
            target,
            code,
        )

    nowhere = jnp.full(lane.shape, -1, jnp.int32)
    _, _, target, code = lax.fori_loop(
        0, requests, place, (jnp.int32(0), crossing, nowhere, nowhere), unroll=8
    )
    codes[...] = jnp.where(iota(codes.shape, 0) == 0, code, crossing)
    select = jnp.where(target == iota((capacity, hidden.shape[0]), 0), 1.0, 0.0).astype(BF)
    wide = jnp.concatenate([dot(select, hidden[...]), fresh[...].astype(F32)], axis=0)
    scaled[...] = (wide * gain[...]).astype(BF)
    square = wide * wide
    high = square.astype(BF)
    low = (square - high.astype(F32)).astype(BF)
    lanes = out_a.shape[1]
    ones = jnp.ones((EXTRA, wide.shape[1]), BF)
    total = jnp.zeros((EXTRA, lanes), F32)
    for index, start in enumerate(range(0, rows, lanes)):
        stop = min(start + lanes, rows)
        part = dot(ones, high[start:stop], ((1,), (1,))) + dot(ones, low[start:stop], ((1,), (1,)))
        if stop - start < lanes:
            part = jnp.concatenate([part, jnp.zeros((EXTRA, lanes - stop + start), F32)], axis=1)
        total = jnp.where(iota((EXTRA, lanes), 0) == index, part, total)
    extra[...] = total.astype(BF)
    for weight, out in ((weight_a, out_a), (weight_b, out_b)):
        out[:rows, :] = dot(scaled[...], weight[...]).astype(BF)
        out[rows:, :] = extra[...]


def later_chunks(order, scaled, extra, *refs):
    count = len(refs) // 2
    rows = scaled.shape[0]
    for weight, out in zip(refs[:count], refs[count:]):
        out[:rows, :] = dot(scaled[...], weight[...]).astype(BF)
        out[rows:, :] = extra[...]


def whole(shape):
    return pl.BlockSpec(shape, lambda i, *_: (0,) * len(shape))


def project_chunks(hidden, fresh, gain, weight, order, dest, length, me, capacity, lanes):
    rows, depth = capacity + fresh.shape[0], hidden.shape[1]
    chunk = jax.ShapeDtypeStruct((rows + EXTRA, lanes), BF)
    chunk_spec = whole((rows + EXTRA, lanes))
    scaled_type = jax.ShapeDtypeStruct((rows, depth), BF)
    extra_type = jax.ShapeDtypeStruct((EXTRA, lanes), BF)
    codes_type = jax.ShapeDtypeStruct((8, hidden.shape[0]), jnp.int32)
    tensors = order.shape[0]

    def column_block(place):
        return pl.BlockSpec((depth, lanes), lambda i, order, *_: (0, order[place]))

    params = pltpu.CompilerParams(vmem_limit_bytes=VMEM_BYTES)
    cost = lambda count: pl.CostEstimate(
        flops=2 * rows * depth * lanes * count,
        bytes_accessed=2 * (rows * depth + count * (depth + rows) * lanes),
        transcendentals=0,
    )
    out_a, out_b, scaled, extra, codes = pl.pallas_call(
        first_chunks,
        grid_spec=pltpu.PrefetchScalarGridSpec(
            num_scalar_prefetch=4,
            grid=(1,),
            in_specs=[
                whole(hidden.shape),
                whole(fresh.shape),
                whole(gain.shape),
                column_block(0),
                column_block(1),
            ],
            out_specs=[
                chunk_spec,
                chunk_spec,
                whole(scaled_type.shape),
                whole(extra_type.shape),
                whole(codes_type.shape),
            ],
        ),
        out_shape=[chunk, chunk, scaled_type, extra_type, codes_type],
        compiler_params=params,
        cost_estimate=cost(2),
        name="first_chunks",
    )(order, dest, length, me, hidden, fresh, gain, weight, weight)
    rest = tensors - 2
    later = pl.pallas_call(
        later_chunks,
        grid_spec=pltpu.PrefetchScalarGridSpec(
            num_scalar_prefetch=1,
            grid=(1,),
            in_specs=[whole(scaled.shape), whole(extra.shape)]
            + [column_block(2 + i) for i in range(rest)],
            out_specs=[chunk_spec] * rest,
        ),
        out_shape=[chunk] * rest,
        compiler_params=params,
        cost_estimate=cost(rest),
        name="later_chunks",
    )(order, scaled, extra, *([weight] * rest))
    return [out_a, out_b, *later], codes


def ring_offsets(tensors):
    ahead = tensors // 2
    behind = tensors - 1 - ahead
    offsets = []
    for step in range(ahead):
        offsets.append(ahead - step)
        if step < behind:
            offsets.append(step - behind)
    return offsets + [0]


def ring_order(tensors):
    ring = ring_of(tensors)
    table = [
        [ring[(ring.index(device) + offset) % tensors] for offset in ring_offsets(tensors)]
        for device in range(tensors)
    ]
    return jnp.array(table, jnp.int32)[lax.axis_index("tensor")]


def ring_sums(chunks):
    tensors = lax.axis_size("tensor")
    ring = ring_of(tensors)
    forward = [(ring[i], ring[(i + 1) % tensors]) for i in range(tensors)]
    backward = [(b, a) for a, b in forward]
    sums = {True: None, False: None}
    for offset, chunk in zip(ring_offsets(tensors), chunks[:-1]):
        way = offset > 0
        if sums[way] is not None:
            chunk = (sums[way].astype(F32) + chunk.astype(F32)).astype(BF)
        sums[way] = lax.ppermute(chunk, "tensor", forward if way else backward)
    return sums[True], sums[False], chunks[-1]


def finish_rows(codes, ahead, behind, own, crossing_rows, kept):
    total = ahead[...].astype(F32) + behind[...].astype(F32) + own[...].astype(F32)
    rows, lanes = kept.shape
    squares = total[rows:]
    for start in range(0, rows, TILE):
        size = min(TILE, rows - start)
        across = squares[start // lanes : start // lanes + 1, start % lanes : start % lanes + TILE]
        diagonal = iota((size, TILE), 0) == iota((size, TILE), 1)
        column = jnp.sum(jnp.where(diagonal, across, 0.0), axis=1, keepdims=True)
        kept[start : start + size, :] = (
            total[start : start + size] * lax.rsqrt(column / D + 1e-06)
        ).astype(BF)
    sent = crossing_rows.shape[0] - EXTRA
    crossing_rows[:sent, :] = kept[:sent, :]
    wide = min(lanes, codes.shape[1])
    code, count = codes[0:1, :wide], codes[1:2, :wide]
    if wide < lanes:
        code = jnp.concatenate([code, jnp.zeros((1, lanes - wide), jnp.int32)], axis=1)
        count = jnp.concatenate([count, jnp.zeros((1, lanes - wide), jnp.int32)], axis=1)
    lane, line = iota((EXTRA, lanes), 1), iota((EXTRA, lanes), 0)
    used = (lane < count) & (lane < sent)
    notes = jnp.where(used, code // CONTEXT, NOWHERE)
    notes = jnp.where(line == 1, code % CONTEXT, notes)
    notes = jnp.where(line == 2, count // CONTEXT, notes)
    notes = jnp.where(line == 3, count % CONTEXT, notes)
    crossing_rows[sent:, :] = notes.astype(F32).astype(BF)


def finish(codes, ahead, behind, own, sent):
    rows, lanes = own.shape[0] - EXTRA, own.shape[1]
    return pl.pallas_call(
        finish_rows,
        out_shape=[
            jax.ShapeDtypeStruct((sent + EXTRA, lanes), BF),
            jax.ShapeDtypeStruct((rows, lanes), BF),
        ],
        compiler_params=pltpu.CompilerParams(vmem_limit_bytes=VMEM_BYTES),
        name="finish_rows",
    )(codes, ahead, behind, own)


def routed(route, rows):
    found = jnp.sum(route, axis=1, keepdims=True) > 0.5
    return jnp.where(found, dot(route.astype(BF), rows), ABSENT).astype(BF)


def place_staying(codes, first, second, out):
    capacity = codes.shape[1] - second.shape[0]
    slots, context, lanes = out.shape
    shape = (slots * context, codes.shape[1])
    code, crossing = codes[0:1, :], codes[1:2, :]
    route = (iota(shape, 0) == code) & (iota(shape, 1) >= crossing)
    rows = jnp.concatenate([first[:capacity, :], second[...]], axis=0)
    out[...] = routed(jnp.where(route, 1.0, 0.0), rows).reshape(out.shape)


def place_crossing(received, out):
    slots, context, lanes = out.shape
    sent = received.shape[0] - EXTRA
    notes = received[sent:, :].astype(F32).astype(jnp.int32)
    code = notes[0:1, :sent] * context + notes[1:2, :sent]
    route = iota((slots * context, sent), 0) == code
    out[...] = routed(jnp.where(route, 1.0, 0.0), received[:sent, :]).reshape(out.shape)


def place(kernel, slots, lanes, *operands):
    return pl.pallas_call(
        kernel,
        out_shape=jax.ShapeDtypeStruct((slots, CONTEXT, lanes), BF),
        compiler_params=pltpu.CompilerParams(vmem_limit_bytes=VMEM_BYTES),
        name=kernel.__name__,
    )(*operands)


def rebuild_and_attend(
    me, near, far, resident, resident_valid, queries, kept, wanted, rebuilt, attended
):
    plane, context, lanes = near.shape
    slots = 2 * plane
    steps, batch, width = queries.shape
    rows = slots * context
    fresh = kept[kept.shape[0] - steps * batch :, :]
    columns = rebuilt.shape[1]
    held = resident.shape[1]
    heads = width // HD
    blocks = jnp.concatenate([near[...], far[...]], axis=0).reshape(rows, lanes)
    half = half_of(me[0])

    def instance_of(slot):
        place = slot % plane
        there = jnp.where(slot < plane, half, 1 - half)
        return (place >> 1) * 4 + there * 2 + (place & 1)

    valid = blocks[:, :TILE].astype(F32) < ABSENT / 2
    flags = jnp.where(valid, 1.0, 0.0).astype(BF)
    opening = jnp.where(iota((slots, rows), 1) == iota((slots, rows), 0) * context, 1.0, 0.0)
    living = dot(opening.astype(BF), flags).astype(BF)
    sooner = instance_of(iota((rows, slots), 1)) < instance_of(iota((rows, slots), 0) // context)
    before = jnp.where(sooner, 1.0, 0.0)
    ranking = dot(before.astype(BF), living)
    target = ranking.astype(jnp.int32) * context + iota((rows, TILE), 0) % context
    target = jnp.where(valid, target, -1)
    routes = jnp.concatenate(
        [
            jnp.where(target == iota((rows, TILE), 1) + start, 1.0, 0.0).astype(BF)
            for start in range(0, columns, TILE)
        ],
        axis=1,
    )[:, :columns]
    moved = dot(blocks, routes, ((0,), (0,))).astype(BF)
    rebuilt[...] = moved
    filled = dot(jnp.ones((EXTRA, rows), BF), routes)[:1] > 0.5

    query = jnp.concatenate(
        [queries[s, :, h * HD : (h + 1) * HD] for s in range(steps) for h in range(heads)], axis=0
    )
    count = query.shape[0]
    scale = 1.0 / HD**0.5
    want = wanted[...]

    def request_of(size):
        return iota((count, size), 1) // context

    mask_held = (want == request_of(held)) & (resident_valid[...] > 0)
    mask_moved = (want == request_of(columns) + held // context) & filled
    line, mark = iota((count, steps * batch), 0), iota((count, steps * batch), 1)
    mask_fresh = (line % batch == mark % batch) & (mark // batch <= line // (heads * batch))
    lowest = -1e30
    score_held = jnp.where(mask_held, dot(query, resident[:HD, :]) * scale, lowest)
    score_moved = jnp.where(mask_moved, dot(query, moved[:HD]) * scale, lowest)
    score_fresh = jnp.where(
        mask_fresh, dot(query, fresh[:, :HD], ((1,), (1,))) * scale, lowest
    )
    top = jnp.maximum(
        jnp.maximum(
            jnp.max(score_held, axis=1, keepdims=True), jnp.max(score_moved, axis=1, keepdims=True)
        ),
        jnp.max(score_fresh, axis=1, keepdims=True),
    )
    exp_held = jnp.where(mask_held, jnp.exp(score_held - top), 0.0)
    exp_moved = jnp.where(mask_moved, jnp.exp(score_moved - top), 0.0)
    exp_fresh = jnp.where(mask_fresh, jnp.exp(score_fresh - top), 0.0)
    total = (
        jnp.sum(exp_held, axis=1, keepdims=True)
        + jnp.sum(exp_moved, axis=1, keepdims=True)
        + jnp.sum(exp_fresh, axis=1, keepdims=True)
    )
    across = ((1,), (1,))
    out = dot((exp_held / total).astype(BF), resident[HD:, :], across)
    out = out + dot((exp_moved / total).astype(BF), moved[HD:], across)
    out = out + dot((exp_fresh / total).astype(BF), fresh[:, HD:])
    out = out.astype(BF)
    for s in range(steps):
        for h in range(heads):
            start = (s * heads + h) * batch
            attended[s, :, h * HD : (h + 1) * HD] = out[start : start + batch]


def rebuild(me, near, far, resident, resident_valid, queries, kept, wanted, columns):
    vmem = pl.BlockSpec(memory_space=pltpu.VMEM)
    return pl.pallas_call(
        rebuild_and_attend,
        in_specs=[pl.BlockSpec(memory_space=pltpu.SMEM)] + [vmem] * 7,
        out_shape=[
            jax.ShapeDtypeStruct((near.shape[2], columns), BF),
            jax.ShapeDtypeStruct(queries.shape, BF),
        ],
        compiler_params=pltpu.CompilerParams(vmem_limit_bytes=VMEM_BYTES),
        name="rebuild_and_attend",
    )(me, near, far, resident, resident_valid, queries, kept, wanted)


def remaining_rows(hidden, gain, weight, codes, target_of, capacity, lanes):
    tensors = lax.axis_size("tensor")
    left = hidden.shape[0] - capacity
    select = (target_of[None, :] == capacity + jnp.arange(left, dtype=jnp.int32)[:, None]).astype(BF)
    wide = jnp.dot(select, hidden, preferred_element_type=F32)
    squares = jnp.sum(wide * wide, axis=1)
    distance = 1
    while distance < tensors:
        pairs = [(i, i ^ distance) for i in range(tensors)]
        squares = squares + lax.ppermute(squares, "tensor", pairs)
        distance *= 2
    parts = jnp.dot((wide * gain).astype(BF), weight, preferred_element_type=F32).astype(BF)
    order = ring_order(tensors)
    chunks = [
        lax.dynamic_slice_in_dim(parts, order[i] * lanes, lanes, 1) for i in range(tensors)
    ]
    ahead, behind, own = ring_sums(chunks)
    total = ahead.astype(F32) + behind.astype(F32) + own.astype(F32)
    return (total * lax.rsqrt(squares / D + 1e-06)[:, None]).astype(BF)


def shards(
    hidden_rows,
    kv_weight,
    norm_gain,
    resident_cache,
    queries,
    fresh_hidden,
    move_dest,
    move_len,
    resident_len,
    decode_ids,
):
    requests = move_dest.shape[0]
    leaving = hidden_rows.shape[0]
    context = leaving // requests
    instances = lax.axis_size("inst")
    owned = kv_weight.shape[1] // lax.axis_size("tensor")
    assert owned == 2 * HD and context == CONTEXT
    steps, batch_rows, features = fresh_hidden.shape
    heads = queries.shape[2] // HD
    fresh_rows = steps * batch_rows
    capacity = max(leaving * 23 // 32 // 16, 1) * 16
    sent = max(leaving * 15 // 32 // 16, 1) * 16
    plane = instances // 2
    mine = lax.axis_index("inst").astype(jnp.int32)[None]
    fresh = fresh_hidden.reshape(fresh_rows, features)
    gain = norm_gain[None, :]
    resident_valid = (
        jnp.arange(context, dtype=jnp.int32)[None, :] < resident_len[:, None]
    ).astype(jnp.int32)
    resident_valid = resident_valid.reshape(1, -1)
    wanted = jnp.tile(decode_ids, steps * heads)[:, None]

    order = ring_order(lax.axis_size("tensor"))
    chunks, codes = project_chunks(
        hidden_rows, fresh, gain, kv_weight, order, move_dest, move_len, mine, capacity, owned
    )
    ahead, behind, own = ring_sums(chunks)
    crossing_rows, kept = finish(codes, ahead, behind, own, sent)

    def second_pass():
        cross = half_of(move_dest) != half_of(mine)
        index = jnp.arange(requests, dtype=jnp.int32)
        sooner = (cross[:, None] > cross[None, :]) | (
            (cross[:, None] == cross[None, :]) & (index[:, None] < index[None, :])
        )
        start = jnp.sum(jnp.where(sooner, move_len[:, None], 0), axis=0)
        position = jnp.arange(context, dtype=jnp.int32)[None, :]
        target = jnp.where(position < move_len[:, None], start[:, None] + position, -1)
        return remaining_rows(
            hidden_rows, gain, kv_weight, codes, target.reshape(-1), capacity, owned
        )

    rest = lax.cond(
        jnp.sum(move_len) > capacity,
        second_pass,
        lambda: jnp.zeros((leaving - capacity, owned), BF),
    )

    halves = [(i, i ^ 2) for i in range(instances)]
    planes = [[i for i in range(instances) if half_of(i) == half] for half in range(2)]

    def over_plane(rows):
        return lax.all_to_all(
            rows, "inst", split_axis=0, concat_axis=0, tiled=True, axis_index_groups=planes
        )

    received = lax.ppermute(crossing_rows, "inst", halves)
    near = over_plane(place(place_staying, plane, owned, codes, kept, rest))
    crossing = place(place_crossing, plane, owned, received)

    def all_crossing():
        rows = jnp.concatenate([kept[:capacity], rest], axis=0)
        rows = lax.ppermute(rows, "inst", halves)
        notes = lax.ppermute(codes, "inst", halves)
        lane = jnp.arange(leaving, dtype=jnp.int32)[None, :]
        slot = jnp.arange(plane * context, dtype=jnp.int32)[:, None]
        route = (slot == notes[0:1]) & (lane < notes[1:2])
        return routed(route.astype(F32), rows).reshape(crossing.shape)

    theirs = received[sent + 2, 0].astype(F32) * context + received[sent + 3, 0].astype(F32)
    most = jnp.maximum(theirs, codes[1, 0].astype(F32))
    crossing = lax.cond(most > sent, all_crossing, lambda: crossing)
    far = over_plane(crossing)
    return tuple(
        rebuild(
            mine,
            near,
            far,
            resident_cache,
            resident_valid,
            queries,
            kept,
            wanted,
            leaving,
        )
    )


def solution(mesh):
    in_specs = (
        P("inst", "tensor"),
        P("tensor", None),
        P("tensor"),
        P("tensor", "inst"),
        P(None, "inst", "tensor"),
        P(None, "inst", "tensor"),
        P("inst"),
        P("inst"),
        P("inst"),
        P("inst"),
    )
    out_specs = (P("tensor", "inst"), P(None, "inst", "tensor"))
    return jax.shard_map(shards, mesh=mesh, in_specs=in_specs, out_specs=out_specs, check_vma=False)
```

```python
import functools

import jax
import jax.numpy as jnp
from jax import lax
from jax.experimental import pallas as pl
from jax.experimental.pallas import tpu as pltpu
from jax.sharding import PartitionSpec as P

D = 8192
GROUP = 8
HD = 128
STEPS = 2
TILE = 128
CONTEXT = 16
EXTRA = 16
NOWHERE = 63
ABSENT = 2.0**100
BF = jnp.bfloat16
F32 = jnp.float32
VMEM_BYTES = 32 * 1024 * 1024


def ring_of(tensors):
    return list(range(0, tensors, 2)) + list(range(tensors - 1, 0, -2))


def iota(shape, axis):
    return lax.broadcasted_iota(jnp.int32, shape, axis)


def dot(a, b, contract=((1,), (0,))):
    return lax.dot_general(a, b, (contract, ((), ())), preferred_element_type=F32)


def plane_of(instance):
    return (instance >> 2) * 2 + (instance & 1)


def half_of(instance):
    return (instance >> 1) & 1


def weight_copy(weight, blocks, sems, offset, place):
    tensors, lanes = lax.axis_size("tensor"), blocks.shape[2]
    me = lax.axis_index("tensor")
    at = jnp.where(me % 2 == 0, me // 2, tensors - 1 - me // 2)
    at = (at + offset + tensors) % tensors
    owner = jnp.where(at < (tensors + 1) // 2, 2 * at, 2 * (tensors - at) - 1)
    columns = pl.ds(pl.multiple_of(owner * lanes, lanes), lanes)
    return pltpu.make_async_copy(weight.at[:, columns], blocks.at[place], sems.at[place])


def first_chunks(
    offsets, dest, length, hidden, fresh, gain, weight, out_a, out_b, scaled, extra, codes, blocks, sems
):
    copies = [weight_copy(weight, blocks, sems, offset, i) for i, offset in enumerate(offsets)]
    for copy in copies:
        copy.start()
    requests = dest.shape[0]
    context = hidden.shape[0] // requests
    rows, capacity = scaled.shape[0], scaled.shape[0] - fresh.shape[0]
    half = half_of(lax.axis_index("inst"))

    def crosses(j):
        return half_of(dest[j]) != half

    def count(j, crossing):
        return crossing + jnp.where(crosses(j), length[j], 0)

    crossing = lax.fori_loop(0, requests, count, jnp.int32(0), unroll=8)
    lane = iota((1, hidden.shape[0]), 1)

    def place(j, carry):
        next_cross, next_stay, target, code = carry
        cross = crosses(j)
        start = jnp.where(cross, next_cross, next_stay)
        place_here = (lane // context == j) & (lane % context < length[j])
        target = jnp.where(place_here, start + lane % context, target)
        inside = (lane >= start) & (lane < start + length[j])
        code = jnp.where(inside, plane_of(dest[j]) * context + lane - start, code)
        return (
            next_cross + jnp.where(cross, length[j], 0),
            next_stay + jnp.where(cross, 0, length[j]),
            target,
            code,
        )

    nowhere = jnp.full(lane.shape, -1, jnp.int32)
    _, _, target, code = lax.fori_loop(
        0, requests, place, (jnp.int32(0), crossing, nowhere, nowhere), unroll=8
    )
    codes[...] = jnp.where(iota(codes.shape, 0) == 0, code, crossing)
    select = jnp.where(target == iota((capacity, hidden.shape[0]), 0), 1.0, 0.0).astype(BF)
    wide = jnp.concatenate([dot(select, hidden[...]), fresh[...].astype(F32)], axis=0)
    scaled[...] = (wide * gain[...]).astype(BF)
    square = wide * wide
    high = square.astype(BF)
    low = (square - high.astype(F32)).astype(BF)
    lanes = out_a.shape[1]
    ones = jnp.ones((EXTRA, wide.shape[1]), BF)
    total = jnp.zeros((EXTRA, lanes), F32)
    for index, start in enumerate(range(0, rows, lanes)):
        stop = min(start + lanes, rows)
        part = dot(ones, high[start:stop], ((1,), (1,))) + dot(ones, low[start:stop], ((1,), (1,)))
        if stop - start < lanes:
            part = jnp.concatenate([part, jnp.zeros((EXTRA, lanes - stop + start), F32)], axis=1)
        total = jnp.where(iota((EXTRA, lanes), 0) == index, part, total)
    extra[...] = total.astype(BF)
    for place_here, out in enumerate((out_a, out_b)):
        copies[place_here].wait()
        out[:rows, :] = dot(scaled[...], blocks[place_here]).astype(BF)
        out[rows:, :] = extra[...]


def later_chunks(offsets, scaled, extra, weight, *refs):
    outs, (blocks, sems) = refs[:-2], refs[-2:]
    copies = [weight_copy(weight, blocks, sems, offset, i) for i, offset in enumerate(offsets)]
    for copy in copies:
        copy.start()
    rows = scaled.shape[0]
    for place_here, out in enumerate(outs):
        copies[place_here].wait()
        out[:rows, :] = dot(scaled[...], blocks[place_here]).astype(BF)
        out[rows:, :] = extra[...]


def project_chunks(hidden, fresh, gain, weight, dest, length, capacity, lanes):
    rows, depth = capacity + fresh.shape[0], hidden.shape[1]
    chunk = jax.ShapeDtypeStruct((rows + EXTRA, lanes), BF)
    offsets = ring_offsets(lax.axis_size("tensor"))
    vmem = pl.BlockSpec(memory_space=pltpu.VMEM)
    smem = pl.BlockSpec(memory_space=pltpu.SMEM)
    hbm = pl.BlockSpec(memory_space=pltpu.HBM)

    def options(count, name):
        return dict(
            scratch_shapes=[
                pltpu.VMEM((count, depth, lanes), BF),
                pltpu.SemaphoreType.DMA((count,)),
            ],
            compiler_params=pltpu.CompilerParams(vmem_limit_bytes=VMEM_BYTES),
            cost_estimate=pl.CostEstimate(
                flops=2 * rows * depth * lanes * count,
                bytes_accessed=2 * (rows * depth + count * (depth + rows) * lanes),
                transcendentals=0,
            ),
            name=name,
        )

    out_a, out_b, scaled, extra, codes = pl.pallas_call(
        functools.partial(first_chunks, offsets[:2]),
        in_specs=[smem, smem, vmem, vmem, vmem, hbm],
        out_shape=[
            chunk,
            chunk,
            jax.ShapeDtypeStruct((rows, depth), BF),
            jax.ShapeDtypeStruct((EXTRA, lanes), BF),
            jax.ShapeDtypeStruct((8, hidden.shape[0]), jnp.int32),
        ],
        **options(2, "first_chunks"),
    )(dest, length, hidden, fresh, gain, weight)
    rest = len(offsets) - 2
    later = pl.pallas_call(
        functools.partial(later_chunks, offsets[2:]),
        in_specs=[vmem, vmem, hbm],
        out_shape=[chunk] * rest,
        **options(rest, "later_chunks"),
    )(scaled, extra, weight)
    return [out_a, out_b, *later], codes


def ring_offsets(tensors):
    ahead = tensors // 2
    behind = tensors - 1 - ahead
    offsets = []
    for step in range(ahead):
        offsets.append(ahead - step)
        if step < behind:
            offsets.append(step - behind)
    return offsets + [0]


def ring_order(tensors):
    ring = ring_of(tensors)
    table = [
        [ring[(ring.index(device) + offset) % tensors] for offset in ring_offsets(tensors)]
        for device in range(tensors)
    ]
    return jnp.array(table, jnp.int32)[lax.axis_index("tensor")]


def ring_sums(chunks):
    tensors = lax.axis_size("tensor")
    ring = ring_of(tensors)
    forward = [(ring[i], ring[(i + 1) % tensors]) for i in range(tensors)]
    backward = [(b, a) for a, b in forward]
    sums = {True: None, False: None}
    for offset, chunk in zip(ring_offsets(tensors), chunks[:-1]):
        way = offset > 0
        if sums[way] is not None:
            chunk = (sums[way].astype(F32) + chunk.astype(F32)).astype(BF)
        sums[way] = lax.ppermute(chunk, "tensor", forward if way else backward)
    return sums[True], sums[False], chunks[-1]


def finish_rows(codes, ahead, behind, own, crossing_rows, kept):
    total = ahead[...].astype(F32) + behind[...].astype(F32) + own[...].astype(F32)
    rows, lanes = kept.shape
    squares = total[rows:]
    for start in range(0, rows, TILE):
        size = min(TILE, rows - start)
        across = squares[start // lanes : start // lanes + 1, start % lanes : start % lanes + TILE]
        diagonal = iota((size, TILE), 0) == iota((size, TILE), 1)
        column = jnp.sum(jnp.where(diagonal, across, 0.0), axis=1, keepdims=True)
        kept[start : start + size, :] = (
            total[start : start + size] * lax.rsqrt(column / D + 1e-06)
        ).astype(BF)
    sent = crossing_rows.shape[0] - EXTRA
    crossing_rows[:sent, :] = kept[:sent, :]
    wide = min(lanes, codes.shape[1])
    code, count = codes[0:1, :wide], codes[1:2, :wide]
    if wide < lanes:
        code = jnp.concatenate([code, jnp.zeros((1, lanes - wide), jnp.int32)], axis=1)
        count = jnp.concatenate([count, jnp.zeros((1, lanes - wide), jnp.int32)], axis=1)
    lane, line = iota((EXTRA, lanes), 1), iota((EXTRA, lanes), 0)
    used = (lane < count) & (lane < sent)
    notes = jnp.where(used, code // CONTEXT, NOWHERE)
    notes = jnp.where(line == 1, code % CONTEXT, notes)
    notes = jnp.where(line == 2, count // CONTEXT, notes)
    notes = jnp.where(line == 3, count % CONTEXT, notes)
    crossing_rows[sent:, :] = notes.astype(F32).astype(BF)


def finish(codes, ahead, behind, own, sent):
    rows, lanes = own.shape[0] - EXTRA, own.shape[1]
    return pl.pallas_call(
        finish_rows,
        out_shape=[
            jax.ShapeDtypeStruct((sent + EXTRA, lanes), BF),
            jax.ShapeDtypeStruct((rows, lanes), BF),
        ],
        compiler_params=pltpu.CompilerParams(vmem_limit_bytes=VMEM_BYTES),
        name="finish_rows",
    )(codes, ahead, behind, own)


def routed(route, rows):
    found = jnp.sum(route, axis=1, keepdims=True) > 0.5
    return jnp.where(found, dot(route.astype(BF), rows), ABSENT).astype(BF)


def place_staying(codes, first, second, out):
    capacity = codes.shape[1] - second.shape[0]
    slots, context, lanes = out.shape
    shape = (slots * context, codes.shape[1])
    code, crossing = codes[0:1, :], codes[1:2, :]
    route = (iota(shape, 0) == code) & (iota(shape, 1) >= crossing)
    rows = jnp.concatenate([first[:capacity, :], second[...]], axis=0)
    out[...] = routed(jnp.where(route, 1.0, 0.0), rows).reshape(out.shape)


def place_crossing(received, codes, near, out, most):
    slots, context, lanes = near.shape
    sent = received.shape[0] - EXTRA
    notes = received[sent:, :].astype(F32).astype(jnp.int32)
    code = notes[0:1, :sent] * context + notes[1:2, :sent]
    route = iota((slots * context, sent), 0) == code
    out[:, :context, :] = near[...]
    out[:, context:, :] = routed(jnp.where(route, 1.0, 0.0), received[:sent, :]).reshape(near.shape)
    theirs = notes[2:3, :TILE] * context + notes[3:4, :TILE]
    most[...] = jnp.broadcast_to(jnp.maximum(theirs, codes[1:2, :1]), most.shape)


def place(kernel, out_shape, *operands):
    return pl.pallas_call(
        kernel,
        out_shape=out_shape,
        compiler_params=pltpu.CompilerParams(vmem_limit_bytes=VMEM_BYTES),
        name=kernel.__name__,
    )(*operands)


def rebuild_and_attend(
    arrived, resident, resident_valid, queries, kept, wanted, rebuilt, attended
):
    plane, context, lanes = arrived.shape
    slots, context = 2 * plane, context // 2
    steps, batch, width = queries.shape
    rows = slots * context
    fresh = kept[kept.shape[0] - steps * batch :, :]
    columns = rebuilt.shape[1]
    held = resident.shape[1]
    heads = width // HD
    blocks = arrived[...].reshape(rows, lanes)
    half = half_of(lax.axis_index("inst"))

    def instance_of(slot):
        place = slot >> 1
        there = jnp.where(slot % 2 == 0, half, 1 - half)
        return (place >> 1) * 4 + there * 2 + (place & 1)

    valid = blocks[:, :TILE].astype(F32) < ABSENT / 2
    flags = jnp.where(valid, 1.0, 0.0).astype(BF)
    opening = jnp.where(iota((slots, rows), 1) == iota((slots, rows), 0) * context, 1.0, 0.0)
    living = dot(opening.astype(BF), flags).astype(BF)
    sooner = instance_of(iota((rows, slots), 1)) < instance_of(iota((rows, slots), 0) // context)
    before = jnp.where(sooner, 1.0, 0.0)
    ranking = dot(before.astype(BF), living)
    target = ranking.astype(jnp.int32) * context + iota((rows, TILE), 0) % context
    target = jnp.where(valid, target, -1)
    routes = jnp.concatenate(
        [
            jnp.where(target == iota((rows, TILE), 1) + start, 1.0, 0.0).astype(BF)
            for start in range(0, columns, TILE)
        ],
        axis=1,
    )[:, :columns]
    moved = dot(blocks, routes, ((0,), (0,))).astype(BF)
    rebuilt[...] = moved
    filled = dot(jnp.ones((EXTRA, rows), BF), routes)[:1] > 0.5

    query = jnp.concatenate(
        [queries[s, :, h * HD : (h + 1) * HD] for s in range(steps) for h in range(heads)], axis=0
    )
    count = query.shape[0]
    scale = 1.0 / HD**0.5
    want = wanted[...]

    def request_of(size):
        return iota((count, size), 1) // context

    mask_held = (want == request_of(held)) & (resident_valid[...] > 0)
    mask_moved = (want == request_of(columns) + held // context) & filled
    line, mark = iota((count, steps * batch), 0), iota((count, steps * batch), 1)
    mask_fresh = (line % batch == mark % batch) & (mark // batch <= line // (heads * batch))
    lowest = -1e30
    score_held = jnp.where(mask_held, dot(query, resident[:HD, :]) * scale, lowest)
    score_moved = jnp.where(mask_moved, dot(query, moved[:HD]) * scale, lowest)
    score_fresh = jnp.where(
        mask_fresh, dot(query, fresh[:, :HD], ((1,), (1,))) * scale, lowest
    )
    top = jnp.maximum(
        jnp.maximum(
            jnp.max(score_held, axis=1, keepdims=True), jnp.max(score_moved, axis=1, keepdims=True)
        ),
        jnp.max(score_fresh, axis=1, keepdims=True),
    )
    exp_held = jnp.where(mask_held, jnp.exp(score_held - top), 0.0)
    exp_moved = jnp.where(mask_moved, jnp.exp(score_moved - top), 0.0)
    exp_fresh = jnp.where(mask_fresh, jnp.exp(score_fresh - top), 0.0)
    total = (
        jnp.sum(exp_held, axis=1, keepdims=True)
        + jnp.sum(exp_moved, axis=1, keepdims=True)
        + jnp.sum(exp_fresh, axis=1, keepdims=True)
    )
    across = ((1,), (1,))
    out = dot((exp_held / total).astype(BF), resident[HD:, :], across)
    out = out + dot((exp_moved / total).astype(BF), moved[HD:], across)
    out = out + dot((exp_fresh / total).astype(BF), fresh[:, HD:])
    out = out.astype(BF)
    for s in range(steps):
        for h in range(heads):
            start = (s * heads + h) * batch
            attended[s, :, h * HD : (h + 1) * HD] = out[start : start + batch]


def rebuild(arrived, resident, resident_valid, queries, kept, wanted, columns):
    return pl.pallas_call(
        rebuild_and_attend,
        out_shape=[
            jax.ShapeDtypeStruct((arrived.shape[2], columns), BF),
            jax.ShapeDtypeStruct(queries.shape, BF),
        ],
        compiler_params=pltpu.CompilerParams(vmem_limit_bytes=VMEM_BYTES),
        name="rebuild_and_attend",
    )(arrived, resident, resident_valid, queries, kept, wanted)


def remaining_rows(hidden, gain, weight, codes, target_of, capacity, lanes):
    tensors = lax.axis_size("tensor")
    left = hidden.shape[0] - capacity
    select = (target_of[None, :] == capacity + jnp.arange(left, dtype=jnp.int32)[:, None]).astype(BF)
    wide = jnp.dot(select, hidden, preferred_element_type=F32)
    squares = jnp.sum(wide * wide, axis=1)
    distance = 1
    while distance < tensors:
        pairs = [(i, i ^ distance) for i in range(tensors)]
        squares = squares + lax.ppermute(squares, "tensor", pairs)
        distance *= 2
    parts = jnp.dot((wide * gain).astype(BF), weight, preferred_element_type=F32).astype(BF)
    order = ring_order(tensors)
    chunks = [
        lax.dynamic_slice_in_dim(parts, order[i] * lanes, lanes, 1) for i in range(tensors)
    ]
    ahead, behind, own = ring_sums(chunks)
    total = ahead.astype(F32) + behind.astype(F32) + own.astype(F32)
    return (total * lax.rsqrt(squares / D + 1e-06)[:, None]).astype(BF)


def shards(
    hidden_rows,
    kv_weight,
    norm_gain,
    resident_cache,
    queries,
    fresh_hidden,
    move_dest,
    move_len,
    resident_len,
    decode_ids,
):
    requests = move_dest.shape[0]
    leaving = hidden_rows.shape[0]
    context = leaving // requests
    instances = lax.axis_size("inst")
    owned = kv_weight.shape[1] // lax.axis_size("tensor")
    assert owned == 2 * HD and context == CONTEXT
    steps, batch_rows, features = fresh_hidden.shape
    heads = queries.shape[2] // HD
    fresh_rows = steps * batch_rows
    capacity = max(leaving * 23 // 32 // 16, 1) * 16
    sent = max(leaving * 15 // 32 // 16, 1) * 16
    plane = instances // 2
    mine = lax.axis_index("inst").astype(jnp.int32)[None]
    fresh = fresh_hidden.reshape(fresh_rows, features)
    gain = norm_gain[None, :]
    resident_valid = (
        jnp.arange(context, dtype=jnp.int32)[None, :] < resident_len[:, None]
    ).astype(jnp.int32)
    resident_valid = resident_valid.reshape(1, -1)
    wanted = jnp.tile(decode_ids, steps * heads)[:, None]

    chunks, codes = project_chunks(
        hidden_rows, fresh, gain, kv_weight, move_dest, move_len, capacity, owned
    )
    ahead, behind, own = ring_sums(chunks)
    crossing_rows, kept = finish(codes, ahead, behind, own, sent)

    def second_pass():
        cross = half_of(move_dest) != half_of(mine)
        index = jnp.arange(requests, dtype=jnp.int32)
        sooner = (cross[:, None] > cross[None, :]) | (
            (cross[:, None] == cross[None, :]) & (index[:, None] < index[None, :])
        )
        start = jnp.sum(jnp.where(sooner, move_len[:, None], 0), axis=0)
        position = jnp.arange(context, dtype=jnp.int32)[None, :]
        target = jnp.where(position < move_len[:, None], start[:, None] + position, -1)
        return remaining_rows(
            hidden_rows, gain, kv_weight, codes, target.reshape(-1), capacity, owned
        )

    rest = lax.cond(
        jnp.sum(move_len) > capacity,
        second_pass,
        lambda: jnp.zeros((leaving - capacity, owned), BF),
    )

    halves = [(i, i ^ 2) for i in range(instances)]
    planes = [[i for i in range(instances) if half_of(i) == half] for half in range(2)]

    received = lax.ppermute(crossing_rows, "inst", halves)
    near_type = jax.ShapeDtypeStruct((plane, context, owned), BF)
    near = place(place_staying, near_type, codes, kept, rest)
    both_type = jax.ShapeDtypeStruct((plane, 2 * context, owned), BF)
    most_type = jax.ShapeDtypeStruct((8, TILE), jnp.int32)
    outgoing, most = place(place_crossing, (both_type, most_type), received, codes, near)

    def all_crossing():
        rows = jnp.concatenate([kept[:capacity], rest], axis=0)
        rows = lax.ppermute(rows, "inst", halves)
        notes = lax.ppermute(codes, "inst", halves)
        lane = jnp.arange(leaving, dtype=jnp.int32)[None, :]
        slot = jnp.arange(plane * context, dtype=jnp.int32)[:, None]
        route = (slot == notes[0:1]) & (lane < notes[1:2])
        far = routed(route.astype(F32), rows).reshape(near.shape)
        return jnp.concatenate([near, far], axis=1)

    outgoing = lax.cond(most[0, 0] > sent, all_crossing, lambda: outgoing)
    arrived = lax.all_to_all(
        outgoing, "inst", split_axis=0, concat_axis=0, tiled=True, axis_index_groups=planes
    )
    return tuple(
        rebuild(arrived, resident_cache, resident_valid, queries, kept, wanted, leaving)
    )


def solution(mesh):
    in_specs = (
        P("inst", "tensor"),
        P("tensor", None),
        P("tensor"),
        P("tensor", "inst"),
        P(None, "inst", "tensor"),
        P(None, "inst", "tensor"),
        P("inst"),
        P("inst"),
        P("inst"),
        P("inst"),
    )
    out_specs = (P("tensor", "inst"), P(None, "inst", "tensor"))
    return jax.shard_map(shards, mesh=mesh, in_specs=in_specs, out_specs=out_specs, check_vma=False)
```

```python
import functools

import jax
import jax.numpy as jnp
from jax import lax
from jax.experimental import pallas as pl
from jax.experimental.pallas import tpu as pltpu
from jax.sharding import PartitionSpec as P

D = 8192
GROUP = 8
HD = 128
STEPS = 2
TILE = 128
CONTEXT = 16
EXTRA = 16
NOWHERE = 63
ABSENT = 2.0**100
BF = jnp.bfloat16
F32 = jnp.float32
VMEM_BYTES = 32 * 1024 * 1024


def ring_of(tensors):
    return list(range(0, tensors, 2)) + list(range(tensors - 1, 0, -2))


def iota(shape, axis):
    return lax.broadcasted_iota(jnp.int32, shape, axis)


def dot(a, b, contract=((1,), (0,))):
    return lax.dot_general(a, b, (contract, ((), ())), preferred_element_type=F32)


def plane_of(instance):
    return (instance >> 2) * 2 + (instance & 1)


def half_of(instance):
    return (instance >> 1) & 1


def weight_copy(weight, blocks, sems, offset, place):
    tensors, lanes = lax.axis_size("tensor"), blocks.shape[2]
    me = lax.axis_index("tensor")
    at = jnp.where(me % 2 == 0, me // 2, tensors - 1 - me // 2)
    at = (at + offset + tensors) % tensors
    owner = jnp.where(at < (tensors + 1) // 2, 2 * at, 2 * (tensors - at) - 1)
    columns = pl.ds(pl.multiple_of(owner * lanes, lanes), lanes)
    return pltpu.make_async_copy(weight.at[:, columns], blocks.at[place], sems.at[place])


def project(scaled, extra, block, top, bottom):
    rows, split = scaled.shape[0], top.shape[0]
    chunk = dot(scaled[...], block[...]).astype(BF)
    top[...] = chunk[:split]
    bottom[: rows - split, :] = chunk[split:]
    bottom[rows - split :, :] = extra[...]


def first_chunks(
    offsets, dest, length, hidden_hbm, fresh, gain, weight, *refs
):
    outs, (scaled, extra, codes, blocks, sems, hidden, hidden_sem) = refs[:4], refs[4:]
    lanes = blocks.shape[2]
    hidden_copy = pltpu.make_async_copy(hidden_hbm, hidden, hidden_sem)
    hidden_copy.start()
    copies = [weight_copy(weight, blocks, sems, offset, i) for i, offset in enumerate(offsets)]
    for copy in copies:
        copy.start()
    requests = dest.shape[0]
    context = hidden.shape[0] // requests
    rows, capacity = scaled.shape[0], scaled.shape[0] - fresh.shape[0]
    half = half_of(lax.axis_index("inst"))

    def crosses(j):
        return half_of(dest[j]) != half

    def count(j, crossing):
        return crossing + jnp.where(crosses(j), length[j], 0)

    crossing = lax.fori_loop(0, requests, count, jnp.int32(0), unroll=8)
    lane = iota((1, hidden.shape[0]), 1)

    def place(j, carry):
        next_cross, next_stay, target, code = carry
        cross = crosses(j)
        start = jnp.where(cross, next_cross, next_stay)
        place_here = (lane // context == j) & (lane % context < length[j])
        target = jnp.where(place_here, start + lane % context, target)
        inside = (lane >= start) & (lane < start + length[j])
        code = jnp.where(inside, plane_of(dest[j]) * context + lane - start, code)
        return (
            next_cross + jnp.where(cross, length[j], 0),
            next_stay + jnp.where(cross, 0, length[j]),
            target,
            code,
        )

    nowhere = jnp.full(lane.shape, -1, jnp.int32)
    _, _, target, code = lax.fori_loop(
        0, requests, place, (jnp.int32(0), crossing, nowhere, nowhere), unroll=8
    )
    codes[...] = jnp.where(iota(codes.shape, 0) == 0, code, crossing)
    select = jnp.where(target == iota((capacity, hidden.shape[0]), 0), 1.0, 0.0).astype(BF)
    hidden_copy.wait()
    wide = jnp.concatenate([dot(select, hidden[...]), fresh[...].astype(F32)], axis=0)
    scaled[...] = (wide * gain[...]).astype(BF)
    square = wide * wide
    high = square.astype(BF)
    low = (square - high.astype(F32)).astype(BF)
    ones = jnp.ones((EXTRA, wide.shape[1]), BF)
    total = jnp.zeros((EXTRA, lanes), F32)
    for index, start in enumerate(range(0, rows, lanes)):
        stop = min(start + lanes, rows)
        part = dot(ones, high[start:stop], ((1,), (1,))) + dot(ones, low[start:stop], ((1,), (1,)))
        if stop - start < lanes:
            part = jnp.concatenate([part, jnp.zeros((EXTRA, lanes - stop + start), F32)], axis=1)
        total = jnp.where(iota((EXTRA, lanes), 0) == index, part, total)
    extra[...] = total.astype(BF)
    for i, copy in enumerate(copies):
        copy.wait()
        project(scaled, extra, blocks.at[i], outs[2 * i], outs[2 * i + 1])


def later_chunks(offsets, scaled, extra, weight, *refs):
    outs, (blocks, sems) = refs[:-2], refs[-2:]
    copies = [weight_copy(weight, blocks, sems, offset, i) for i, offset in enumerate(offsets)]
    for copy in copies:
        copy.start()
    for i, copy in enumerate(copies):
        copy.wait()
        project(scaled, extra, blocks.at[i], outs[2 * i], outs[2 * i + 1])


def project_chunks(hidden, fresh, gain, weight, dest, length, capacity, lanes):
    rows, depth = capacity + fresh.shape[0], hidden.shape[1]
    split = (rows + EXTRA) // 32 * 16
    pieces = [
        jax.ShapeDtypeStruct((split, lanes), BF),
        jax.ShapeDtypeStruct((rows + EXTRA - split, lanes), BF),
    ]
    offsets = ring_offsets(lax.axis_size("tensor"))
    vmem = pl.BlockSpec(memory_space=pltpu.VMEM)
    smem = pl.BlockSpec(memory_space=pltpu.SMEM)
    hbm = pl.BlockSpec(memory_space=pltpu.HBM)

    def options(count, name, *more):
        return dict(
            scratch_shapes=[
                pltpu.VMEM((count, depth, lanes), BF),
                pltpu.SemaphoreType.DMA((count,)),
                *more,
            ],
            compiler_params=pltpu.CompilerParams(vmem_limit_bytes=VMEM_BYTES),
            cost_estimate=pl.CostEstimate(
                flops=2 * rows * depth * lanes * count,
                bytes_accessed=2 * (rows * depth + count * (depth + rows) * lanes),
                transcendentals=0,
            ),
            name=name,
        )

    *first, scaled, extra, codes = pl.pallas_call(
        functools.partial(first_chunks, offsets[:2]),
        in_specs=[smem, smem, hbm, vmem, vmem, hbm],
        out_shape=[
            *pieces,
            *pieces,
            jax.ShapeDtypeStruct((rows, depth), BF),
            jax.ShapeDtypeStruct((EXTRA, lanes), BF),
            jax.ShapeDtypeStruct((8, hidden.shape[0]), jnp.int32),
        ],
        **options(
            2, "first_chunks", pltpu.VMEM(hidden.shape, BF), pltpu.SemaphoreType.DMA(())
        ),
    )(dest, length, hidden, fresh, gain, weight)
    rest = len(offsets) - 2
    later = pl.pallas_call(
        functools.partial(later_chunks, offsets[2:]),
        in_specs=[vmem, vmem, hbm],
        out_shape=pieces * rest,
        **options(rest, "later_chunks"),
    )(scaled, extra, weight)
    every = [*first, *later]
    return [every[i : i + 2] for i in range(0, len(every), 2)], codes


def ring_offsets(tensors):
    ahead = tensors // 2
    behind = tensors - 1 - ahead
    offsets = []
    for step in range(ahead):
        offsets.append(ahead - step)
        if step < behind:
            offsets.append(step - behind)
    return offsets + [0]


def ring_order(tensors):
    ring = ring_of(tensors)
    table = [
        [ring[(ring.index(device) + offset) % tensors] for offset in ring_offsets(tensors)]
        for device in range(tensors)
    ]
    return jnp.array(table, jnp.int32)[lax.axis_index("tensor")]


def ring_sums(chunks):
    tensors = lax.axis_size("tensor")
    ring = ring_of(tensors)
    forward = [(ring[i], ring[(i + 1) % tensors]) for i in range(tensors)]
    backward = [(b, a) for a, b in forward]
    sums = {}
    for offset, pieces in zip(ring_offsets(tensors), chunks[:-1]):
        way = offset > 0
        for i, piece in enumerate(pieces):
            if (way, i) in sums:
                piece = (sums[way, i].astype(F32) + piece.astype(F32)).astype(BF)
            sums[way, i] = lax.ppermute(piece, "tensor", forward if way else backward)
    return [
        (sums[True, i], sums[False, i], own) for i, own in enumerate(chunks[-1])
    ]


def total_of(parts):
    return sum(part[...].astype(F32) for part in parts[1:]) + parts[0][...].astype(F32)


def finish_rows(codes, *refs):
    terms, (crossing_rows, kept) = refs[:-2], refs[-2:]
    total = jnp.concatenate([total_of(terms[:3]), total_of(terms[3:])], axis=0)
    rows, lanes = kept.shape
    squares = total[rows:]
    for start in range(0, rows, TILE):
        size = min(TILE, rows - start)
        across = squares[start // lanes : start // lanes + 1, start % lanes : start % lanes + TILE]
        diagonal = iota((size, TILE), 0) == iota((size, TILE), 1)
        column = jnp.sum(jnp.where(diagonal, across, 0.0), axis=1, keepdims=True)
        kept[start : start + size, :] = (
            total[start : start + size] * lax.rsqrt(column / D + 1e-06)
        ).astype(BF)
    sent = crossing_rows.shape[0] - EXTRA
    crossing_rows[:sent, :] = kept[:sent, :]
    wide = min(lanes, codes.shape[1])
    code, count = codes[0:1, :wide], codes[1:2, :wide]
    if wide < lanes:
        code = jnp.concatenate([code, jnp.zeros((1, lanes - wide), jnp.int32)], axis=1)
        count = jnp.concatenate([count, jnp.zeros((1, lanes - wide), jnp.int32)], axis=1)
    lane, line = iota((EXTRA, lanes), 1), iota((EXTRA, lanes), 0)
    used = (lane < count) & (lane < sent)
    notes = jnp.where(used, code // CONTEXT, NOWHERE)
    notes = jnp.where(line == 1, code % CONTEXT, notes)
    notes = jnp.where(line == 2, count // CONTEXT, notes)
    notes = jnp.where(line == 3, count % CONTEXT, notes)
    crossing_rows[sent:, :] = notes.astype(F32).astype(BF)


def finish(codes, terms, sent):
    lanes = terms[0].shape[1]
    rows = terms[0].shape[0] + terms[3].shape[0] - EXTRA
    return pl.pallas_call(
        finish_rows,
        out_shape=[
            jax.ShapeDtypeStruct((sent + EXTRA, lanes), BF),
            jax.ShapeDtypeStruct((rows, lanes), BF),
        ],
        compiler_params=pltpu.CompilerParams(vmem_limit_bytes=VMEM_BYTES),
        name="finish_rows",
    )(codes, *terms)


def routed(route, rows):
    found = jnp.sum(route, axis=1, keepdims=True) > 0.5
    return jnp.where(found, dot(route.astype(BF), rows), ABSENT).astype(BF)


def place_staying(codes, first, second, out):
    capacity = codes.shape[1] - second.shape[0]
    slots, context, lanes = out.shape
    shape = (slots * context, codes.shape[1])
    code, crossing = codes[0:1, :], codes[1:2, :]
    route = (iota(shape, 0) == code) & (iota(shape, 1) >= crossing)
    rows = jnp.concatenate([first[:capacity, :], second[...]], axis=0)
    out[...] = routed(jnp.where(route, 1.0, 0.0), rows).reshape(out.shape)


def place_crossing(received, codes, near, out, most):
    slots, context, lanes = near.shape
    sent = received.shape[0] - EXTRA
    notes = received[sent:, :].astype(F32).astype(jnp.int32)
    code = notes[0:1, :sent] * context + notes[1:2, :sent]
    route = iota((slots * context, sent), 0) == code
    out[:, :context, :] = near[...]
    out[:, context:, :] = routed(jnp.where(route, 1.0, 0.0), received[:sent, :]).reshape(near.shape)
    counts = jnp.maximum(notes[2:3, :sent] * context + notes[3:4, :sent], codes[1:2, :sent])
    most[0] = jnp.max(counts)


def place(kernel, out_shape, out_specs, *operands):
    return pl.pallas_call(
        kernel,
        out_shape=out_shape,
        out_specs=out_specs,
        compiler_params=pltpu.CompilerParams(vmem_limit_bytes=VMEM_BYTES),
        name=kernel.__name__,
    )(*operands)


def rebuild_and_attend(
    arrived, resident, resident_valid, queries, kept, wanted, rebuilt, attended
):
    plane, context, lanes = arrived.shape
    slots, context = 2 * plane, context // 2
    steps, batch, width = queries.shape
    rows = slots * context
    fresh = kept[kept.shape[0] - steps * batch :, :]
    columns = rebuilt.shape[1]
    held = resident.shape[1]
    heads = width // HD
    blocks = arrived[...].reshape(rows, lanes)
    half = half_of(lax.axis_index("inst"))

    def instance_of(slot):
        place = slot >> 1
        there = jnp.where(slot % 2 == 0, half, 1 - half)
        return (place >> 1) * 4 + there * 2 + (place & 1)

    valid = blocks[:, :TILE].astype(F32) < ABSENT / 2
    flags = jnp.where(valid, 1.0, 0.0).astype(BF)
    opening = jnp.where(iota((slots, rows), 1) == iota((slots, rows), 0) * context, 1.0, 0.0)
    living = dot(opening.astype(BF), flags).astype(BF)
    sooner = instance_of(iota((rows, slots), 1)) < instance_of(iota((rows, slots), 0) // context)
    before = jnp.where(sooner, 1.0, 0.0)
    ranking = dot(before.astype(BF), living)
    target = ranking.astype(jnp.int32) * context + iota((rows, TILE), 0) % context
    target = jnp.where(valid, target, -1)
    routes = jnp.concatenate(
        [
            jnp.where(target == iota((rows, TILE), 1) + start, 1.0, 0.0).astype(BF)
            for start in range(0, columns, TILE)
        ],
        axis=1,
    )[:, :columns]
    moved = dot(blocks, routes, ((0,), (0,))).astype(BF)
    rebuilt[...] = moved
    filled = dot(jnp.ones((EXTRA, rows), BF), routes)[:1] > 0.5

    query = jnp.concatenate(
        [queries[s, :, h * HD : (h + 1) * HD] for s in range(steps) for h in range(heads)], axis=0
    )
    count = query.shape[0]
    scale = 1.0 / HD**0.5
    want = wanted[...]

    def request_of(size):
        return iota((count, size), 1) // context

    mask_held = (want == request_of(held)) & (resident_valid[...] > 0)
    mask_moved = (want == request_of(columns) + held // context) & filled
    line, mark = iota((count, steps * batch), 0), iota((count, steps * batch), 1)
    mask_fresh = (line % batch == mark % batch) & (mark // batch <= line // (heads * batch))
    lowest = -1e30
    score_held = jnp.where(mask_held, dot(query, resident[:HD, :]) * scale, lowest)
    score_moved = jnp.where(mask_moved, dot(query, moved[:HD]) * scale, lowest)
    score_fresh = jnp.where(
        mask_fresh, dot(query, fresh[:, :HD], ((1,), (1,))) * scale, lowest
    )
    top = jnp.maximum(
        jnp.maximum(
            jnp.max(score_held, axis=1, keepdims=True), jnp.max(score_moved, axis=1, keepdims=True)
        ),
        jnp.max(score_fresh, axis=1, keepdims=True),
    )
    exp_held = jnp.where(mask_held, jnp.exp(score_held - top), 0.0)
    exp_moved = jnp.where(mask_moved, jnp.exp(score_moved - top), 0.0)
    exp_fresh = jnp.where(mask_fresh, jnp.exp(score_fresh - top), 0.0)
    total = (
        jnp.sum(exp_held, axis=1, keepdims=True)
        + jnp.sum(exp_moved, axis=1, keepdims=True)
        + jnp.sum(exp_fresh, axis=1, keepdims=True)
    )
    across = ((1,), (1,))
    out = dot((exp_held / total).astype(BF), resident[HD:, :], across)
    out = out + dot((exp_moved / total).astype(BF), moved[HD:], across)
    out = out + dot((exp_fresh / total).astype(BF), fresh[:, HD:])
    out = out.astype(BF)
    for s in range(steps):
        for h in range(heads):
            start = (s * heads + h) * batch
            attended[s, :, h * HD : (h + 1) * HD] = out[start : start + batch]


def rebuild(arrived, resident, resident_valid, queries, kept, wanted, columns):
    return pl.pallas_call(
        rebuild_and_attend,
        out_shape=[
            jax.ShapeDtypeStruct((arrived.shape[2], columns), BF),
            jax.ShapeDtypeStruct(queries.shape, BF),
        ],
        compiler_params=pltpu.CompilerParams(vmem_limit_bytes=VMEM_BYTES),
        name="rebuild_and_attend",
    )(arrived, resident, resident_valid, queries, kept, wanted)


def remaining_rows(hidden, gain, weight, codes, target_of, capacity, lanes):
    tensors = lax.axis_size("tensor")
    left = hidden.shape[0] - capacity
    select = (target_of[None, :] == capacity + jnp.arange(left, dtype=jnp.int32)[:, None]).astype(BF)
    wide = jnp.dot(select, hidden, preferred_element_type=F32)
    squares = jnp.sum(wide * wide, axis=1)
    distance = 1
    while distance < tensors:
        pairs = [(i, i ^ distance) for i in range(tensors)]
        squares = squares + lax.ppermute(squares, "tensor", pairs)
        distance *= 2
    parts = jnp.dot((wide * gain).astype(BF), weight, preferred_element_type=F32).astype(BF)
    order = ring_order(tensors)
    chunks = [
        [lax.dynamic_slice_in_dim(parts, order[i] * lanes, lanes, 1)] for i in range(tensors)
    ]
    total = total_of(ring_sums(chunks)[0])
    return (total * lax.rsqrt(squares / D + 1e-06)[:, None]).astype(BF)


def shards(
    hidden_rows,
    kv_weight,
    norm_gain,
    resident_cache,
    queries,
    fresh_hidden,
    move_dest,
    move_len,
    resident_len,
    decode_ids,
):
    requests = move_dest.shape[0]
    leaving = hidden_rows.shape[0]
    context = leaving // requests
    instances = lax.axis_size("inst")
    owned = kv_weight.shape[1] // lax.axis_size("tensor")
    assert owned == 2 * HD and context == CONTEXT
    steps, batch_rows, features = fresh_hidden.shape
    heads = queries.shape[2] // HD
    fresh_rows = steps * batch_rows
    capacity = max(leaving * 23 // 32 // 16, 1) * 16
    sent = max(leaving * 15 // 32 // 16, 1) * 16
    plane = instances // 2
    mine = lax.axis_index("inst").astype(jnp.int32)[None]
    fresh = fresh_hidden.reshape(fresh_rows, features)
    gain = norm_gain[None, :]
    resident_valid = (
        jnp.arange(context, dtype=jnp.int32)[None, :] < resident_len[:, None]
    ).astype(jnp.int32)
    resident_valid = resident_valid.reshape(1, -1)
    wanted = jnp.tile(decode_ids, steps * heads)[:, None]

    chunks, codes = project_chunks(
        hidden_rows, fresh, gain, kv_weight, move_dest, move_len, capacity, owned
    )
    terms = [term for piece in ring_sums(chunks) for term in piece]
    crossing_rows, kept = finish(codes, terms, sent)

    def second_pass():
        cross = half_of(move_dest) != half_of(mine)
        index = jnp.arange(requests, dtype=jnp.int32)
        sooner = (cross[:, None] > cross[None, :]) | (
            (cross[:, None] == cross[None, :]) & (index[:, None] < index[None, :])
        )
        start = jnp.sum(jnp.where(sooner, move_len[:, None], 0), axis=0)
        position = jnp.arange(context, dtype=jnp.int32)[None, :]
        target = jnp.where(position < move_len[:, None], start[:, None] + position, -1)
        return remaining_rows(
            hidden_rows, gain, kv_weight, codes, target.reshape(-1), capacity, owned
        )

    rest = lax.cond(
        jnp.sum(move_len) > capacity,
        second_pass,
        lambda: jnp.zeros((leaving - capacity, owned), BF),
    )

    halves = [(i, i ^ 2) for i in range(instances)]
    planes = [[i for i in range(instances) if half_of(i) == half] for half in range(2)]

    received = lax.ppermute(crossing_rows, "inst", halves)
    near_type = jax.ShapeDtypeStruct((plane, context, owned), BF)
    vmem = pl.BlockSpec(memory_space=pltpu.VMEM)
    near = place(place_staying, near_type, vmem, codes, kept, rest)
    both_type = jax.ShapeDtypeStruct((plane, 2 * context, owned), BF)
    most_type = jax.ShapeDtypeStruct((1,), jnp.int32)
    outgoing, most = place(
        place_crossing,
        (both_type, most_type),
        (vmem, pl.BlockSpec(memory_space=pltpu.SMEM)),
        received,
        codes,
        near,
    )

    def all_crossing():
        rows = jnp.concatenate([kept[:capacity], rest], axis=0)
        rows = lax.ppermute(rows, "inst", halves)
        notes = lax.ppermute(codes, "inst", halves)
        lane = jnp.arange(leaving, dtype=jnp.int32)[None, :]
        slot = jnp.arange(plane * context, dtype=jnp.int32)[:, None]
        route = (slot == notes[0:1]) & (lane < notes[1:2])
        far = routed(route.astype(F32), rows).reshape(near.shape)
        return jnp.concatenate([near, far], axis=1)

    outgoing = lax.cond(most[0] > sent, all_crossing, lambda: outgoing)
    arrived = lax.all_to_all(
        outgoing, "inst", split_axis=0, concat_axis=0, tiled=True, axis_index_groups=planes
    )
    return tuple(
        rebuild(arrived, resident_cache, resident_valid, queries, kept, wanted, leaving)
    )


def solution(mesh):
    in_specs = (
        P("inst", "tensor"),
        P("tensor", None),
        P("tensor"),
        P("tensor", "inst"),
        P(None, "inst", "tensor"),
        P(None, "inst", "tensor"),
        P("inst"),
        P("inst"),
        P("inst"),
        P("inst"),
    )
    out_specs = (P("tensor", "inst"), P(None, "inst", "tensor"))
    return jax.shard_map(shards, mesh=mesh, in_specs=in_specs, out_specs=out_specs, check_vma=False)
```

```python
import functools

import jax
import jax.numpy as jnp
from jax import lax
from jax.experimental import pallas as pl
from jax.experimental.pallas import tpu as pltpu
from jax.sharding import PartitionSpec as P

D = 8192
GROUP = 8
HD = 128
STEPS = 2
TILE = 128
CONTEXT = 16
EXTRA = 16
NOWHERE = 63
ABSENT = 2.0**100
BF = jnp.bfloat16
F32 = jnp.float32
VMEM_BYTES = 32 * 1024 * 1024


def ring_of(tensors):
    return list(range(0, tensors, 2)) + list(range(tensors - 1, 0, -2))


def iota(shape, axis):
    return lax.broadcasted_iota(jnp.int32, shape, axis)


def dot(a, b, contract=((1,), (0,))):
    return lax.dot_general(a, b, (contract, ((), ())), preferred_element_type=F32)


def plane_of(instance):
    return (instance >> 2) * 2 + (instance & 1)


def half_of(instance):
    return (instance >> 1) & 1


def weight_copy(weight, blocks, sems, offset, place):
    tensors, lanes = lax.axis_size("tensor"), blocks.shape[2]
    me = lax.axis_index("tensor")
    at = jnp.where(me % 2 == 0, me // 2, tensors - 1 - me // 2)
    at = (at + offset + tensors) % tensors
    owner = jnp.where(at < (tensors + 1) // 2, 2 * at, 2 * (tensors - at) - 1)
    columns = pl.ds(pl.multiple_of(owner * lanes, lanes), lanes)
    return pltpu.make_async_copy(weight.at[:, columns], blocks.at[place], sems.at[place])


def first_chunks(
    offsets, dest, length, hidden, fresh, gain, weight, out_a, out_b, scaled, extra, codes, blocks, sems
):
    copies = [weight_copy(weight, blocks, sems, offset, i) for i, offset in enumerate(offsets)]
    for copy in copies:
        copy.start()
    requests = dest.shape[1]
    context = hidden.shape[0] // requests
    rows, capacity = scaled.shape[0], scaled.shape[0] - fresh.shape[0]
    half = half_of(lax.axis_index("inst"))

    def upright(line):
        diagonal = iota((requests, requests), 0) == iota((requests, requests), 1)
        return jnp.sum(jnp.where(diagonal, line, 0), axis=1, keepdims=True)

    lengths, dests = length[...], dest[...]
    cross = jnp.where(half_of(dests) != half, 1, 0)
    crossing = jnp.sum(cross * lengths, axis=1, keepdims=True)
    cross_up, lengths_up, dests_up = upright(cross), upright(lengths), upright(dests)
    earlier = iota((requests, requests), 1) < iota((requests, requests), 0)
    sooner = (cross > cross_up) | ((cross == cross_up) & earlier)
    start = jnp.sum(jnp.where(sooner, lengths, 0), axis=1, keepdims=True)
    shape = (requests, hidden.shape[0])
    lane = iota(shape, 1)
    at = lane % context
    here = (lane // context == iota(shape, 0)) & (at < lengths_up)
    target = jnp.sum(jnp.where(here, start + at + 1, 0), axis=0, keepdims=True) - 1
    inside = (lane >= start) & (lane < start + lengths_up)
    code = jnp.where(inside, plane_of(dests_up) * context + lane - start + 1, 0)
    code = jnp.sum(code, axis=0, keepdims=True) - 1
    codes[...] = jnp.where(iota(codes.shape, 0) == 0, code, crossing)
    select = jnp.where(target == iota((capacity, hidden.shape[0]), 0), 1.0, 0.0).astype(BF)
    wide = jnp.concatenate([dot(select, hidden[...]), fresh[...].astype(F32)], axis=0)
    scaled[...] = (wide * gain[...]).astype(BF)
    square = wide * wide
    high = square.astype(BF)
    low = (square - high.astype(F32)).astype(BF)
    lanes = out_a.shape[1]
    ones = jnp.ones((EXTRA, wide.shape[1]), BF)
    total = jnp.zeros((EXTRA, lanes), F32)
    for index, start in enumerate(range(0, rows, lanes)):
        stop = min(start + lanes, rows)
        part = dot(ones, high[start:stop], ((1,), (1,))) + dot(ones, low[start:stop], ((1,), (1,)))
        if stop - start < lanes:
            part = jnp.concatenate([part, jnp.zeros((EXTRA, lanes - stop + start), F32)], axis=1)
        total = jnp.where(iota((EXTRA, lanes), 0) == index, part, total)
    extra[...] = total.astype(BF)
    for place_here, out in enumerate((out_a, out_b)):
        copies[place_here].wait()
        out[:rows, :] = dot(scaled[...], blocks[place_here]).astype(BF)
        out[rows:, :] = extra[...]


def later_chunks(offsets, scaled, extra, weight, *refs):
    outs, (blocks, sems) = refs[:-2], refs[-2:]
    copies = [weight_copy(weight, blocks, sems, offset, i) for i, offset in enumerate(offsets)]
    for copy in copies:
        copy.start()
    rows = scaled.shape[0]
    for place_here, out in enumerate(outs):
        copies[place_here].wait()
        out[:rows, :] = dot(scaled[...], blocks[place_here]).astype(BF)
        out[rows:, :] = extra[...]


def project_chunks(hidden, fresh, gain, weight, dest, length, capacity, lanes):
    rows, depth = capacity + fresh.shape[0], hidden.shape[1]
    chunk = jax.ShapeDtypeStruct((rows + EXTRA, lanes), BF)
    offsets = ring_offsets(lax.axis_size("tensor"))
    vmem = pl.BlockSpec(memory_space=pltpu.VMEM)
    hbm = pl.BlockSpec(memory_space=pltpu.HBM)

    def options(count, name):
        return dict(
            scratch_shapes=[
                pltpu.VMEM((count, depth, lanes), BF),
                pltpu.SemaphoreType.DMA((count,)),
            ],
            compiler_params=pltpu.CompilerParams(vmem_limit_bytes=VMEM_BYTES),
            cost_estimate=pl.CostEstimate(
                flops=2 * rows * depth * lanes * count,
                bytes_accessed=2 * (rows * depth + count * (depth + rows) * lanes),
                transcendentals=0,
            ),
            name=name,
        )

    out_a, out_b, scaled, extra, codes = pl.pallas_call(
        functools.partial(first_chunks, offsets[:2]),
        in_specs=[vmem, vmem, vmem, vmem, vmem, hbm],
        out_shape=[
            chunk,
            chunk,
            jax.ShapeDtypeStruct((rows, depth), BF),
            jax.ShapeDtypeStruct((EXTRA, lanes), BF),
            jax.ShapeDtypeStruct((8, hidden.shape[0]), jnp.int32),
        ],
        **options(2, "first_chunks"),
    )(dest[None, :], length[None, :], hidden, fresh, gain, weight)
    rest = len(offsets) - 2
    later = pl.pallas_call(
        functools.partial(later_chunks, offsets[2:]),
        in_specs=[vmem, vmem, hbm],
        out_shape=[chunk] * rest,
        **options(rest, "later_chunks"),
    )(scaled, extra, weight)
    return [out_a, out_b, *later], codes


def ring_offsets(tensors):
    ahead = tensors // 2
    behind = tensors - 1 - ahead
    offsets = []
    for step in range(ahead):
        offsets.append(ahead - step)
        if step < behind:
            offsets.append(step - behind)
    return offsets + [0]


def ring_order(tensors):
    ring = ring_of(tensors)
    table = [
        [ring[(ring.index(device) + offset) % tensors] for offset in ring_offsets(tensors)]
        for device in range(tensors)
    ]
    return jnp.array(table, jnp.int32)[lax.axis_index("tensor")]


def ring_sums(chunks):
    tensors = lax.axis_size("tensor")
    ring = ring_of(tensors)
    forward = [(ring[i], ring[(i + 1) % tensors]) for i in range(tensors)]
    backward = [(b, a) for a, b in forward]
    sums = {True: None, False: None}
    for offset, chunk in zip(ring_offsets(tensors), chunks[:-1]):
        way = offset > 0
        if sums[way] is not None:
            chunk = (sums[way].astype(F32) + chunk.astype(F32)).astype(BF)
        sums[way] = lax.ppermute(chunk, "tensor", forward if way else backward)
    return sums[True], sums[False], chunks[-1]


def finish_rows(codes, ahead, behind, own, crossing_rows, kept):
    total = ahead[...].astype(F32) + behind[...].astype(F32) + own[...].astype(F32)
    rows, lanes = kept.shape
    squares = total[rows:]
    for start in range(0, rows, TILE):
        size = min(TILE, rows - start)
        across = squares[start // lanes : start // lanes + 1, start % lanes : start % lanes + TILE]
        diagonal = iota((size, TILE), 0) == iota((size, TILE), 1)
        column = jnp.sum(jnp.where(diagonal, across, 0.0), axis=1, keepdims=True)
        kept[start : start + size, :] = (
            total[start : start + size] * lax.rsqrt(column / D + 1e-06)
        ).astype(BF)
    sent = crossing_rows.shape[0] - EXTRA
    crossing_rows[:sent, :] = kept[:sent, :]
    wide = min(lanes, codes.shape[1])
    code, count = codes[0:1, :wide], codes[1:2, :wide]
    if wide < lanes:
        code = jnp.concatenate([code, jnp.zeros((1, lanes - wide), jnp.int32)], axis=1)
        count = jnp.concatenate([count, jnp.zeros((1, lanes - wide), jnp.int32)], axis=1)
    lane, line = iota((EXTRA, lanes), 1), iota((EXTRA, lanes), 0)
    used = (lane < count) & (lane < sent)
    notes = jnp.where(used, code // CONTEXT, NOWHERE)
    notes = jnp.where(line == 1, code % CONTEXT, notes)
    notes = jnp.where(line == 2, count // CONTEXT, notes)
    notes = jnp.where(line == 3, count % CONTEXT, notes)
    crossing_rows[sent:, :] = notes.astype(F32).astype(BF)


def finish(codes, ahead, behind, own, sent):
    rows, lanes = own.shape[0] - EXTRA, own.shape[1]
    return pl.pallas_call(
        finish_rows,
        out_shape=[
            jax.ShapeDtypeStruct((sent + EXTRA, lanes), BF),
            jax.ShapeDtypeStruct((rows, lanes), BF),
        ],
        compiler_params=pltpu.CompilerParams(vmem_limit_bytes=VMEM_BYTES),
        name="finish_rows",
    )(codes, ahead, behind, own)


def routed(route, rows):
    found = jnp.sum(route, axis=1, keepdims=True) > 0.5
    return jnp.where(found, dot(route.astype(BF), rows), ABSENT).astype(BF)


def place_staying(codes, first, second, out):
    capacity = codes.shape[1] - second.shape[0]
    slots, context, lanes = out.shape
    shape = (slots * context, codes.shape[1])
    code, crossing = codes[0:1, :], codes[1:2, :]
    route = (iota(shape, 0) == code) & (iota(shape, 1) >= crossing)
    rows = jnp.concatenate([first[:capacity, :], second[...]], axis=0)
    out[...] = routed(jnp.where(route, 1.0, 0.0), rows).reshape(out.shape)


def place_crossing(received, codes, out, most):
    slots, context, lanes = out.shape
    sent = received.shape[0] - EXTRA
    notes = received[sent:, :].astype(F32).astype(jnp.int32)
    code = notes[0:1, :sent] * context + notes[1:2, :sent]
    route = iota((slots * context, sent), 0) == code
    out[...] = routed(jnp.where(route, 1.0, 0.0), received[:sent, :]).reshape(out.shape)
    counts = jnp.maximum(notes[2:3, :sent] * context + notes[3:4, :sent], codes[1:2, :sent])
    most[0] = jnp.max(counts)


def place(kernel, out_shape, out_specs, weighs, *operands):
    return pl.pallas_call(
        kernel,
        out_shape=out_shape,
        out_specs=out_specs,
        compiler_params=pltpu.CompilerParams(vmem_limit_bytes=VMEM_BYTES),
        cost_estimate=pl.CostEstimate(flops=weighs, bytes_accessed=1 << 20, transcendentals=0),
        name=kernel.__name__,
    )(*operands)


def rebuild_and_attend(
    near, far, resident, resident_valid, queries, kept, wanted, rebuilt, attended
):
    plane, context, lanes = near.shape
    slots = 2 * plane
    steps, batch, width = queries.shape
    rows = slots * context
    fresh = kept[kept.shape[0] - steps * batch :, :]
    columns = rebuilt.shape[1]
    held = resident.shape[1]
    heads = width // HD
    blocks = jnp.concatenate([near[...], far[...]], axis=0).reshape(rows, lanes)
    half = half_of(lax.axis_index("inst"))

    def instance_of(slot):
        place = slot % plane
        there = jnp.where(slot < plane, half, 1 - half)
        return (place >> 1) * 4 + there * 2 + (place & 1)

    valid = blocks[:, :TILE].astype(F32) < ABSENT / 2
    flags = jnp.where(valid, 1.0, 0.0).astype(BF)
    opening = jnp.where(iota((slots, rows), 1) == iota((slots, rows), 0) * context, 1.0, 0.0)
    living = dot(opening.astype(BF), flags).astype(BF)
    sooner = instance_of(iota((rows, slots), 1)) < instance_of(iota((rows, slots), 0) // context)
    before = jnp.where(sooner, 1.0, 0.0)
    ranking = dot(before.astype(BF), living)
    target = ranking.astype(jnp.int32) * context + iota((rows, TILE), 0) % context
    target = jnp.where(valid, target, -1)
    routes = jnp.concatenate(
        [
            jnp.where(target == iota((rows, TILE), 1) + start, 1.0, 0.0).astype(BF)
            for start in range(0, columns, TILE)
        ],
        axis=1,
    )[:, :columns]
    moved = dot(blocks, routes, ((0,), (0,))).astype(BF)
    rebuilt[...] = moved
    filled = dot(jnp.ones((EXTRA, rows), BF), routes)[:1] > 0.5

    query = jnp.concatenate(
        [queries[s, :, h * HD : (h + 1) * HD] for s in range(steps) for h in range(heads)], axis=0
    )
    count = query.shape[0]
    scale = 1.0 / HD**0.5
    want = wanted[...]

    def request_of(size):
        return iota((count, size), 1) // context

    mask_held = (want == request_of(held)) & (resident_valid[...] > 0)
    mask_moved = (want == request_of(columns) + held // context) & filled
    line, mark = iota((count, steps * batch), 0), iota((count, steps * batch), 1)
    mask_fresh = (line % batch == mark % batch) & (mark // batch <= line // (heads * batch))
    lowest = -1e30
    score_held = jnp.where(mask_held, dot(query, resident[:HD, :]) * scale, lowest)
    score_moved = jnp.where(mask_moved, dot(query, moved[:HD]) * scale, lowest)
    score_fresh = jnp.where(
        mask_fresh, dot(query, fresh[:, :HD], ((1,), (1,))) * scale, lowest
    )
    top = jnp.maximum(
        jnp.maximum(
            jnp.max(score_held, axis=1, keepdims=True), jnp.max(score_moved, axis=1, keepdims=True)
        ),
        jnp.max(score_fresh, axis=1, keepdims=True),
    )
    exp_held = jnp.where(mask_held, jnp.exp(score_held - top), 0.0)
    exp_moved = jnp.where(mask_moved, jnp.exp(score_moved - top), 0.0)
    exp_fresh = jnp.where(mask_fresh, jnp.exp(score_fresh - top), 0.0)
    total = (
        jnp.sum(exp_held, axis=1, keepdims=True)
        + jnp.sum(exp_moved, axis=1, keepdims=True)
        + jnp.sum(exp_fresh, axis=1, keepdims=True)
    )
    across = ((1,), (1,))
    out = dot((exp_held / total).astype(BF), resident[HD:, :], across)
    out = out + dot((exp_moved / total).astype(BF), moved[HD:], across)
    out = out + dot((exp_fresh / total).astype(BF), fresh[:, HD:])
    out = out.astype(BF)
    for s in range(steps):
        for h in range(heads):
            start = (s * heads + h) * batch
            attended[s, :, h * HD : (h + 1) * HD] = out[start : start + batch]


def rebuild(near, far, resident, resident_valid, queries, kept, wanted, columns):
    return pl.pallas_call(
        rebuild_and_attend,
        out_shape=[
            jax.ShapeDtypeStruct((near.shape[2], columns), BF),
            jax.ShapeDtypeStruct(queries.shape, BF),
        ],
        compiler_params=pltpu.CompilerParams(vmem_limit_bytes=VMEM_BYTES),
        name="rebuild_and_attend",
    )(near, far, resident, resident_valid, queries, kept, wanted)


def remaining_rows(hidden, gain, weight, codes, target_of, capacity, lanes):
    tensors = lax.axis_size("tensor")
    left = hidden.shape[0] - capacity
    select = (target_of[None, :] == capacity + jnp.arange(left, dtype=jnp.int32)[:, None]).astype(BF)
    wide = jnp.dot(select, hidden, preferred_element_type=F32)
    squares = jnp.sum(wide * wide, axis=1)
    distance = 1
    while distance < tensors:
        pairs = [(i, i ^ distance) for i in range(tensors)]
        squares = squares + lax.ppermute(squares, "tensor", pairs)
        distance *= 2
    parts = jnp.dot((wide * gain).astype(BF), weight, preferred_element_type=F32).astype(BF)
    order = ring_order(tensors)
    chunks = [
        lax.dynamic_slice_in_dim(parts, order[i] * lanes, lanes, 1) for i in range(tensors)
    ]
    ahead, behind, own = ring_sums(chunks)
    total = ahead.astype(F32) + behind.astype(F32) + own.astype(F32)
    return (total * lax.rsqrt(squares / D + 1e-06)[:, None]).astype(BF)


def shards(
    hidden_rows,
    kv_weight,
    norm_gain,
    resident_cache,
    queries,
    fresh_hidden,
    move_dest,
    move_len,
    resident_len,
    decode_ids,
):
    requests = move_dest.shape[0]
    leaving = hidden_rows.shape[0]
    context = leaving // requests
    instances = lax.axis_size("inst")
    owned = kv_weight.shape[1] // lax.axis_size("tensor")
    assert owned == 2 * HD and context == CONTEXT
    steps, batch_rows, features = fresh_hidden.shape
    heads = queries.shape[2] // HD
    fresh_rows = steps * batch_rows
    capacity = max(leaving * 23 // 32 // 16, 1) * 16
    sent = max(leaving * 15 // 32 // 16, 1) * 16
    plane = instances // 2
    mine = lax.axis_index("inst").astype(jnp.int32)[None]
    fresh = fresh_hidden.reshape(fresh_rows, features)
    gain = norm_gain[None, :]
    resident_valid = (
        jnp.arange(context, dtype=jnp.int32)[None, :] < resident_len[:, None]
    ).astype(jnp.int32)
    resident_valid = resident_valid.reshape(1, -1)
    wanted = jnp.tile(decode_ids, steps * heads)[:, None]

    chunks, codes = project_chunks(
        hidden_rows, fresh, gain, kv_weight, move_dest, move_len, capacity, owned
    )
    ahead, behind, own = ring_sums(chunks)
    crossing_rows, kept = finish(codes, ahead, behind, own, sent)

    def second_pass():
        cross = half_of(move_dest) != half_of(mine)
        index = jnp.arange(requests, dtype=jnp.int32)
        sooner = (cross[:, None] > cross[None, :]) | (
            (cross[:, None] == cross[None, :]) & (index[:, None] < index[None, :])
        )
        start = jnp.sum(jnp.where(sooner, move_len[:, None], 0), axis=0)
        position = jnp.arange(context, dtype=jnp.int32)[None, :]
        target = jnp.where(position < move_len[:, None], start[:, None] + position, -1)
        return remaining_rows(
            hidden_rows, gain, kv_weight, codes, target.reshape(-1), capacity, owned
        )

    rest = lax.cond(
        jnp.sum(move_len) > capacity,
        second_pass,
        lambda: jnp.zeros((leaving - capacity, owned), BF),
    )

    halves = [(i, i ^ 2) for i in range(instances)]
    planes = [[i for i in range(instances) if half_of(i) == half] for half in range(2)]

    received = lax.ppermute(crossing_rows, "inst", halves)
    blocks_type = jax.ShapeDtypeStruct((plane, context, owned), BF)
    vmem = pl.BlockSpec(memory_space=pltpu.VMEM)
    staying = place(place_staying, blocks_type, vmem, 1 << 33, codes, kept, rest)
    most_type = jax.ShapeDtypeStruct((1,), jnp.int32)
    crossing, most = place(
        place_crossing,
        (blocks_type, most_type),
        (vmem, pl.BlockSpec(memory_space=pltpu.SMEM)),
        1 << 36,
        received,
        codes,
    )

    def over_plane(rows):
        return lax.all_to_all(
            rows, "inst", split_axis=0, concat_axis=0, tiled=True, axis_index_groups=planes
        )

    def all_crossing():
        rows = jnp.concatenate([kept[:capacity], rest], axis=0)
        rows = lax.ppermute(rows, "inst", halves)
        notes = lax.ppermute(codes, "inst", halves)
        lane = jnp.arange(leaving, dtype=jnp.int32)[None, :]
        slot = jnp.arange(plane * context, dtype=jnp.int32)[:, None]
        route = (slot == notes[0:1]) & (lane < notes[1:2])
        return routed(route.astype(F32), rows).reshape(crossing.shape)

    near = over_plane(staying)
    far = over_plane(lax.cond(most[0] > sent, all_crossing, lambda: crossing))
    return tuple(
        rebuild(near, far, resident_cache, resident_valid, queries, kept, wanted, leaving)
    )


def solution(mesh):
    in_specs = (
        P("inst", "tensor"),
        P("tensor", None),
        P("tensor"),
        P("tensor", "inst"),
        P(None, "inst", "tensor"),
        P(None, "inst", "tensor"),
        P("inst"),
        P("inst"),
        P("inst"),
        P("inst"),
    )
    out_specs = (P("tensor", "inst"), P(None, "inst", "tensor"))
    return jax.shard_map(shards, mesh=mesh, in_specs=in_specs, out_specs=out_specs, check_vma=False)
```

```python
import functools

import jax
import jax.numpy as jnp
from jax import lax
from jax.experimental import pallas as pl
from jax.experimental.pallas import tpu as pltpu
from jax.sharding import PartitionSpec as P

D = 8192
GROUP = 8
HD = 128
STEPS = 2
TILE = 128
CONTEXT = 16
EXTRA = 16
NOWHERE = 63
ABSENT = 2.0**100
BF = jnp.bfloat16
F32 = jnp.float32
VMEM_BYTES = 32 * 1024 * 1024


def ring_of(tensors):
    return list(range(0, tensors, 2)) + list(range(tensors - 1, 0, -2))


def iota(shape, axis):
    return lax.broadcasted_iota(jnp.int32, shape, axis)


def dot(a, b, contract=((1,), (0,))):
    return lax.dot_general(a, b, (contract, ((), ())), preferred_element_type=F32)


def plane_of(instance):
    return (instance >> 2) * 2 + (instance & 1)


def half_of(instance):
    return (instance >> 1) & 1


def weight_copy(weight, blocks, sems, offset, place):
    tensors, lanes = lax.axis_size("tensor"), blocks.shape[2]
    me = lax.axis_index("tensor")
    at = jnp.where(me % 2 == 0, me // 2, tensors - 1 - me // 2)
    at = (at + offset + tensors) % tensors
    owner = jnp.where(at < (tensors + 1) // 2, 2 * at, 2 * (tensors - at) - 1)
    columns = pl.ds(pl.multiple_of(owner * lanes, lanes), lanes)
    return pltpu.make_async_copy(weight.at[:, columns], blocks.at[place], sems.at[place])


def pair_of_chunks(capacity, scaled, extra, codes, block, mirrored, out, mirrored_out):
    rows, lanes = scaled.shape[0], out.shape[1]
    here = dot(scaled[...], block[...])
    there = dot(scaled[...], mirrored[...])
    row = iota((rows, lanes), 0)
    crosses = (row < codes[1:2, :1]) & (row < capacity)
    out[:rows, :] = jnp.where(crosses, there, here).astype(BF)
    mirrored_out[:rows, :] = jnp.where(crosses, here, there).astype(BF)
    out[rows:, :] = extra[...]
    mirrored_out[rows:, :] = extra[...]


def first_chunks(offsets, *refs):
    operands, weight = refs[:5], refs[5]
    outs, (scaled, extra, codes), (blocks, sems) = refs[6:8], refs[8:11], refs[11:13]
    held, held_sems = refs[13:18], refs[18]
    fetches = [
        pltpu.make_async_copy(source, target, held_sems.at[i])
        for i, (source, target) in enumerate(zip(operands, held))
    ]
    for fetch in fetches:
        fetch.start()
    copies = [weight_copy(weight, blocks, sems, offset, i) for i, offset in enumerate(offsets)]
    for copy in copies:
        copy.start()
    dest, length, gain, fresh, hidden = held
    requests = dest.shape[1]
    context = hidden.shape[0] // requests
    rows, capacity = scaled.shape[0], scaled.shape[0] - fresh.shape[0]
    for fetch in fetches[:2]:
        fetch.wait()
    half = half_of(lax.axis_index("inst"))

    def upright(line):
        diagonal = iota((requests, requests), 0) == iota((requests, requests), 1)
        return jnp.sum(jnp.where(diagonal, line, 0), axis=1, keepdims=True)

    lengths, dests = length[...], dest[...]
    cross = jnp.where(half_of(dests) != half, 1, 0)
    crossing = jnp.sum(cross * lengths, axis=1, keepdims=True)
    cross_up, lengths_up, dests_up = upright(cross), upright(lengths), upright(dests)
    earlier = iota((requests, requests), 1) < iota((requests, requests), 0)
    sooner = (cross > cross_up) | ((cross == cross_up) & earlier)
    start = jnp.sum(jnp.where(sooner, lengths, 0), axis=1, keepdims=True)
    shape = (requests, hidden.shape[0])
    lane = iota(shape, 1)
    at = lane % context
    here = (lane // context == iota(shape, 0)) & (at < lengths_up)
    target = jnp.sum(jnp.where(here, start + at + 1, 0), axis=0, keepdims=True) - 1
    inside = (lane >= start) & (lane < start + lengths_up)
    code = jnp.where(inside, plane_of(dests_up) * context + lane - start + 1, 0)
    code = jnp.sum(code, axis=0, keepdims=True) - 1
    codes[...] = jnp.where(iota(codes.shape, 0) == 0, code, crossing)
    select = jnp.where(target == iota((capacity, hidden.shape[0]), 0), 1.0, 0.0).astype(BF)
    for fetch in fetches[2:]:
        fetch.wait()
    wide = jnp.concatenate([dot(select, hidden[...]), fresh[...].astype(F32)], axis=0)
    scaled[...] = (wide * gain[...]).astype(BF)
    square = wide * wide
    narrow = sum(square[:, i : i + TILE] for i in range(TILE, square.shape[1], TILE))
    column = jnp.sum(narrow + square[:, :TILE], axis=1, keepdims=True)
    lanes = extra.shape[1]
    totals = [jnp.zeros((EXTRA, TILE), F32) for _ in range(0, lanes, TILE)]
    for start in range(0, rows, TILE):
        size = min(TILE, rows - start)
        diagonal = iota((size, TILE), 0) == iota((size, TILE), 1)
        line = jnp.where(diagonal, column[start : start + size], 0.0)
        line = jnp.sum(line, axis=0, keepdims=True)
        place_here = start % lanes // TILE
        totals[place_here] = jnp.where(
            iota((EXTRA, TILE), 0) == start // lanes, line, totals[place_here]
        )
    extra[...] = jnp.concatenate(totals, axis=1).astype(BF)
    for copy in copies:
        copy.wait()
    pair_of_chunks(capacity, scaled, extra, codes, blocks.at[0], blocks.at[1], *outs)


def later_chunks(offsets, capacity, scaled, extra, codes, weight, *refs):
    outs, (blocks, sems) = refs[:-2], refs[-2:]
    copies = [weight_copy(weight, blocks, sems, offset, i) for i, offset in enumerate(offsets)]
    for copy in copies:
        copy.start()
    for i in range(0, len(copies), 2):
        copies[i].wait()
        copies[i + 1].wait()
        pair_of_chunks(
            capacity, scaled, extra, codes, blocks.at[i], blocks.at[i + 1], *outs[i : i + 2]
        )


def project_chunks(hidden, fresh, gain, weight, dest, length, capacity, lanes):
    rows, depth = capacity + fresh.shape[0], hidden.shape[1]
    chunk = jax.ShapeDtypeStruct((rows + EXTRA, lanes), BF)
    tensors = lax.axis_size("tensor")
    offsets = ring_offsets(tensors)
    pairs = []
    for offset in offsets:
        if all(offset not in pair for pair in pairs):
            pairs.append((offset, offset - tensors // 2 if offset > 0 else offset + tensors // 2))
    vmem = pl.BlockSpec(memory_space=pltpu.VMEM)
    hbm = pl.BlockSpec(memory_space=pltpu.HBM)

    def options(count, name, *more):
        return dict(
            scratch_shapes=[
                pltpu.VMEM((count, depth, lanes), BF),
                pltpu.SemaphoreType.DMA((count,)),
                *more,
            ],
            compiler_params=pltpu.CompilerParams(vmem_limit_bytes=VMEM_BYTES),
            cost_estimate=pl.CostEstimate(
                flops=2 * rows * depth * lanes * count,
                bytes_accessed=2 * (rows * depth + count * (depth + rows) * lanes),
                transcendentals=0,
            ),
            name=name,
        )

    operands = [dest[None, :], length[None, :], gain, fresh, hidden]
    *first, scaled, extra, codes = pl.pallas_call(
        functools.partial(first_chunks, pairs[0]),
        in_specs=[hbm] * 6,
        out_shape=[
            chunk,
            chunk,
            jax.ShapeDtypeStruct((rows, depth), BF),
            jax.ShapeDtypeStruct((EXTRA, lanes), BF),
            jax.ShapeDtypeStruct((8, hidden.shape[0]), jnp.int32),
        ],
        **options(
            2,
            "first_chunks",
            *(pltpu.VMEM(operand.shape, operand.dtype) for operand in operands),
            pltpu.SemaphoreType.DMA((len(operands),)),
        ),
    )(*operands, weight)
    chunks = dict(zip(pairs[0], first))
    for group, name in ((pairs[1:2], "second_chunks"), (pairs[2:], "later_chunks")):
        group = [offset for pair in group for offset in pair]
        outs = pl.pallas_call(
            functools.partial(later_chunks, group, capacity),
            in_specs=[vmem, vmem, vmem, hbm],
            out_shape=[chunk] * len(group),
            **options(len(group), name),
        )(scaled, extra, codes, weight)
        chunks.update(zip(group, outs))
    return [chunks[offset] for offset in offsets], codes


def ring_offsets(tensors):
    ahead = tensors // 2
    behind = tensors - 1 - ahead
    offsets = []
    for step in range(ahead):
        offsets.append(ahead - step)
        if step < behind:
            offsets.append(step - behind)
    return offsets + [0]


def ring_order(tensors):
    ring = ring_of(tensors)
    table = [
        [ring[(ring.index(device) + offset) % tensors] for offset in ring_offsets(tensors)]
        for device in range(tensors)
    ]
    return jnp.array(table, jnp.int32)[lax.axis_index("tensor")]


def ring_sums(chunks):
    tensors = lax.axis_size("tensor")
    ring = ring_of(tensors)
    forward = [(ring[i], ring[(i + 1) % tensors]) for i in range(tensors)]
    backward = [(b, a) for a, b in forward]
    sums = {True: None, False: None}
    for offset, chunk in zip(ring_offsets(tensors), chunks[:-1]):
        way = offset > 0
        if sums[way] is not None:
            chunk = (sums[way].astype(F32) + chunk.astype(F32)).astype(BF)
        sums[way] = lax.ppermute(chunk, "tensor", forward if way else backward)
    return sums[True], sums[False], chunks[-1]


def finish_rows(codes, ahead, behind, own, crossing_rows, kept):
    total = ahead[...].astype(F32) + behind[...].astype(F32) + own[...].astype(F32)
    rows, lanes = kept.shape
    squares = total[rows:]
    for start in range(0, rows, TILE):
        size = min(TILE, rows - start)
        across = squares[start // lanes : start // lanes + 1, start % lanes : start % lanes + TILE]
        diagonal = iota((size, TILE), 0) == iota((size, TILE), 1)
        column = jnp.sum(jnp.where(diagonal, across, 0.0), axis=1, keepdims=True)
        kept[start : start + size, :] = (
            total[start : start + size] * lax.rsqrt(column / D + 1e-06)
        ).astype(BF)
    sent = crossing_rows.shape[0] - EXTRA
    crossing_rows[:sent, :] = kept[:sent, :]
    wide = min(lanes, codes.shape[1])
    code, count = codes[0:1, :wide], codes[1:2, :wide]
    if wide < lanes:
        code = jnp.concatenate([code, jnp.zeros((1, lanes - wide), jnp.int32)], axis=1)
        count = jnp.concatenate([count, jnp.zeros((1, lanes - wide), jnp.int32)], axis=1)
    lane, line = iota((EXTRA, lanes), 1), iota((EXTRA, lanes), 0)
    used = (lane < count) & (lane < sent)
    notes = jnp.where(used, code // CONTEXT, NOWHERE)
    notes = jnp.where(line == 1, code % CONTEXT, notes)
    notes = jnp.where(line == 2, count // CONTEXT, notes)
    notes = jnp.where(line == 3, count % CONTEXT, notes)
    crossing_rows[sent:, :] = notes.astype(F32).astype(BF)


def finish(codes, ahead, behind, own, sent):
    rows, lanes = own.shape[0] - EXTRA, own.shape[1]
    return pl.pallas_call(
        finish_rows,
        out_shape=[
            jax.ShapeDtypeStruct((sent + EXTRA, lanes), BF),
            jax.ShapeDtypeStruct((rows, lanes), BF),
        ],
        compiler_params=pltpu.CompilerParams(vmem_limit_bytes=VMEM_BYTES),
        name="finish_rows",
    )(codes, ahead, behind, own)


def routed(route, rows):
    found = jnp.sum(route, axis=1, keepdims=True) > 0.5
    return jnp.where(found, dot(route.astype(BF), rows), ABSENT).astype(BF)


def place_staying(codes, first, second, out):
    capacity = codes.shape[1] - second.shape[0]
    slots, context, lanes = out.shape
    shape = (slots * context, codes.shape[1])
    code, crossing = codes[0:1, :], codes[1:2, :]
    route = (iota(shape, 0) == code) & (iota(shape, 1) >= crossing)
    rows = jnp.concatenate([first[:capacity, :], second[...]], axis=0)
    out[...] = routed(jnp.where(route, 1.0, 0.0), rows).reshape(out.shape)


def place_crossing(received, codes, out, most):
    slots, context, lanes = out.shape
    sent = received.shape[0] - EXTRA
    notes = received[sent:, :].astype(F32).astype(jnp.int32)
    code = notes[0:1, :sent] * context + notes[1:2, :sent]
    route = iota((slots * context, sent), 0) == code
    out[...] = routed(jnp.where(route, 1.0, 0.0), received[:sent, :]).reshape(out.shape)
    counts = jnp.maximum(notes[2:3, :sent] * context + notes[3:4, :sent], codes[1:2, :sent])
    most[0] = jnp.max(counts)


def place(kernel, out_shape, out_specs, weighs, *operands):
    return pl.pallas_call(
        kernel,
        out_shape=out_shape,
        out_specs=out_specs,
        compiler_params=pltpu.CompilerParams(vmem_limit_bytes=VMEM_BYTES),
        cost_estimate=pl.CostEstimate(flops=weighs, bytes_accessed=1 << 20, transcendentals=0),
        name=kernel.__name__,
    )(*operands)


def rebuild_and_attend(
    near, far, resident, resident_valid, queries, kept, wanted, rebuilt, attended
):
    plane, context, lanes = near.shape
    slots = 2 * plane
    steps, batch, width = queries.shape
    rows = slots * context
    fresh = kept[kept.shape[0] - steps * batch :, :]
    columns = rebuilt.shape[1]
    held = resident.shape[1]
    heads = width // HD
    blocks = jnp.concatenate([near[...], far[...]], axis=0).reshape(rows, lanes)
    half = half_of(lax.axis_index("inst"))

    def instance_of(slot):
        place = slot % plane
        there = jnp.where(slot < plane, half, 1 - half)
        return (place >> 1) * 4 + there * 2 + (place & 1)

    valid = blocks[:, :TILE].astype(F32) < ABSENT / 2
    flags = jnp.where(valid, 1.0, 0.0).astype(BF)
    opening = jnp.where(iota((slots, rows), 1) == iota((slots, rows), 0) * context, 1.0, 0.0)
    living = dot(opening.astype(BF), flags).astype(BF)
    sooner = instance_of(iota((rows, slots), 1)) < instance_of(iota((rows, slots), 0) // context)
    before = jnp.where(sooner, 1.0, 0.0)
    ranking = dot(before.astype(BF), living)
    target = ranking.astype(jnp.int32) * context + iota((rows, TILE), 0) % context
    target = jnp.where(valid, target, -1)
    routes = jnp.concatenate(
        [
            jnp.where(target == iota((rows, TILE), 1) + start, 1.0, 0.0).astype(BF)
            for start in range(0, columns, TILE)
        ],
        axis=1,
    )[:, :columns]
    moved = dot(blocks, routes, ((0,), (0,))).astype(BF)
    rebuilt[...] = moved
    filled = dot(jnp.ones((EXTRA, rows), BF), routes)[:1] > 0.5

    query = jnp.concatenate(
        [queries[s, :, h * HD : (h + 1) * HD] for s in range(steps) for h in range(heads)], axis=0
    )
    count = query.shape[0]
    scale = 1.0 / HD**0.5
    want = wanted[...]

    def request_of(size):
        return iota((count, size), 1) // context

    mask_held = (want == request_of(held)) & (resident_valid[...] > 0)
    mask_moved = (want == request_of(columns) + held // context) & filled
    line, mark = iota((count, steps * batch), 0), iota((count, steps * batch), 1)
    mask_fresh = (line % batch == mark % batch) & (mark // batch <= line // (heads * batch))
    lowest = -1e30
    score_held = jnp.where(mask_held, dot(query, resident[:HD, :]) * scale, lowest)
    score_moved = jnp.where(mask_moved, dot(query, moved[:HD]) * scale, lowest)
    score_fresh = jnp.where(
        mask_fresh, dot(query, fresh[:, :HD], ((1,), (1,))) * scale, lowest
    )
    top = jnp.maximum(
        jnp.maximum(
            jnp.max(score_held, axis=1, keepdims=True), jnp.max(score_moved, axis=1, keepdims=True)
        ),
        jnp.max(score_fresh, axis=1, keepdims=True),
    )
    exp_held = jnp.where(mask_held, jnp.exp(score_held - top), 0.0)
    exp_moved = jnp.where(mask_moved, jnp.exp(score_moved - top), 0.0)
    exp_fresh = jnp.where(mask_fresh, jnp.exp(score_fresh - top), 0.0)
    total = (
        jnp.sum(exp_held, axis=1, keepdims=True)
        + jnp.sum(exp_moved, axis=1, keepdims=True)
        + jnp.sum(exp_fresh, axis=1, keepdims=True)
    )
    across = ((1,), (1,))
    out = dot((exp_held / total).astype(BF), resident[HD:, :], across)
    out = out + dot((exp_moved / total).astype(BF), moved[HD:], across)
    out = out + dot((exp_fresh / total).astype(BF), fresh[:, HD:])
    out = out.astype(BF)
    for s in range(steps):
        for h in range(heads):
            start = (s * heads + h) * batch
            attended[s, :, h * HD : (h + 1) * HD] = out[start : start + batch]


def rebuild(near, far, resident, resident_valid, queries, kept, wanted, columns):
    return pl.pallas_call(
        rebuild_and_attend,
        out_shape=[
            jax.ShapeDtypeStruct((near.shape[2], columns), BF),
            jax.ShapeDtypeStruct(queries.shape, BF),
        ],
        compiler_params=pltpu.CompilerParams(vmem_limit_bytes=VMEM_BYTES),
        name="rebuild_and_attend",
    )(near, far, resident, resident_valid, queries, kept, wanted)


def remaining_rows(hidden, gain, weight, codes, target_of, capacity, lanes):
    tensors = lax.axis_size("tensor")
    left = hidden.shape[0] - capacity
    select = (target_of[None, :] == capacity + jnp.arange(left, dtype=jnp.int32)[:, None]).astype(BF)
    wide = jnp.dot(select, hidden, preferred_element_type=F32)
    squares = jnp.sum(wide * wide, axis=1)
    distance = 1
    while distance < tensors:
        pairs = [(i, i ^ distance) for i in range(tensors)]
        squares = squares + lax.ppermute(squares, "tensor", pairs)
        distance *= 2
    parts = jnp.dot((wide * gain).astype(BF), weight, preferred_element_type=F32).astype(BF)
    order = ring_order(tensors)
    crosses = capacity + jnp.arange(left, dtype=jnp.int32)[:, None] < codes[1, 0]

    def block_of(owner):
        return lax.dynamic_slice_in_dim(parts, owner * lanes, lanes, 1)

    chunks = [
        jnp.where(crosses, block_of(tensors - 1 - order[i]), block_of(order[i]))
        for i in range(tensors)
    ]
    ahead, behind, own = ring_sums(chunks)
    total = ahead.astype(F32) + behind.astype(F32) + own.astype(F32)
    return (total * lax.rsqrt(squares / D + 1e-06)[:, None]).astype(BF)


def shards(
    hidden_rows,
    kv_weight,
    norm_gain,
    resident_cache,
    queries,
    fresh_hidden,
    move_dest,
    move_len,
    resident_len,
    decode_ids,
):
    requests = move_dest.shape[0]
    leaving = hidden_rows.shape[0]
    context = leaving // requests
    instances = lax.axis_size("inst")
    owned = kv_weight.shape[1] // lax.axis_size("tensor")
    assert owned == 2 * HD and context == CONTEXT
    steps, batch_rows, features = fresh_hidden.shape
    heads = queries.shape[2] // HD
    fresh_rows = steps * batch_rows
    capacity = max(leaving * 23 // 32 // 16, 1) * 16
    sent = max(leaving * 15 // 32 // 16, 1) * 16
    plane = instances // 2
    mine = lax.axis_index("inst").astype(jnp.int32)[None]
    fresh = fresh_hidden.reshape(fresh_rows, features)
    gain = norm_gain[None, :]
    resident_valid = (
        jnp.arange(context, dtype=jnp.int32)[None, :] < resident_len[:, None]
    ).astype(jnp.int32)
    resident_valid = resident_valid.reshape(1, -1)
    wanted = jnp.tile(decode_ids, steps * heads)[:, None]

    chunks, codes = project_chunks(
        hidden_rows, fresh, gain, kv_weight, move_dest, move_len, capacity, owned
    )
    ahead, behind, own = ring_sums(chunks)
    crossing_rows, kept = finish(codes, ahead, behind, own, sent)

    def second_pass():
        cross = half_of(move_dest) != half_of(mine)
        index = jnp.arange(requests, dtype=jnp.int32)
        sooner = (cross[:, None] > cross[None, :]) | (
            (cross[:, None] == cross[None, :]) & (index[:, None] < index[None, :])
        )
        start = jnp.sum(jnp.where(sooner, move_len[:, None], 0), axis=0)
        position = jnp.arange(context, dtype=jnp.int32)[None, :]
        target = jnp.where(position < move_len[:, None], start[:, None] + position, -1)
        return remaining_rows(
            hidden_rows, gain, kv_weight, codes, target.reshape(-1), capacity, owned
        )

    rest = lax.cond(
        jnp.sum(move_len) > capacity,
        second_pass,
        lambda: jnp.zeros((leaving - capacity, owned), BF),
    )

    tensors = lax.axis_size("tensor")
    halves = [
        (i * tensors + t, (i ^ 2) * tensors + tensors - 1 - t)
        for i in range(instances)
        for t in range(tensors)
    ]
    planes = [[i for i in range(instances) if half_of(i) == half] for half in range(2)]

    received = lax.ppermute(crossing_rows, ("inst", "tensor"), halves)
    blocks_type = jax.ShapeDtypeStruct((plane, context, owned), BF)
    vmem = pl.BlockSpec(memory_space=pltpu.VMEM)
    staying = place(place_staying, blocks_type, vmem, 1 << 33, codes, kept, rest)
    most_type = jax.ShapeDtypeStruct((1,), jnp.int32)
    crossing, most = place(
        place_crossing,
        (blocks_type, most_type),
        (vmem, pl.BlockSpec(memory_space=pltpu.SMEM)),
        1 << 36,
        received,
        codes,
    )

    def over_plane(rows):
        return lax.all_to_all(
            rows, "inst", split_axis=0, concat_axis=0, tiled=True, axis_index_groups=planes
        )

    def all_crossing():
        rows = jnp.concatenate([kept[:capacity], rest], axis=0)
        rows = lax.ppermute(rows, ("inst", "tensor"), halves)
        notes = lax.ppermute(codes, ("inst", "tensor"), halves)
        lane = jnp.arange(leaving, dtype=jnp.int32)[None, :]
        slot = jnp.arange(plane * context, dtype=jnp.int32)[:, None]
        route = (slot == notes[0:1]) & (lane < notes[1:2])
        return routed(route.astype(F32), rows).reshape(crossing.shape)

    near = over_plane(staying)
    far = over_plane(lax.cond(most[0] > sent, all_crossing, lambda: crossing))
    return tuple(
        rebuild(near, far, resident_cache, resident_valid, queries, kept, wanted, leaving)
    )


def solution(mesh):
    in_specs = (
        P("inst", "tensor"),
        P("tensor", None),
        P("tensor"),
        P("tensor", "inst"),
        P(None, "inst", "tensor"),
        P(None, "inst", "tensor"),
        P("inst"),
        P("inst"),
        P("inst"),
        P("inst"),
    )
    out_specs = (P("tensor", "inst"), P(None, "inst", "tensor"))
    return jax.shard_map(shards, mesh=mesh, in_specs=in_specs, out_specs=out_specs, check_vma=False)
```

```python
import functools

import jax
import jax.numpy as jnp
from jax import lax
from jax.experimental import pallas as pl
from jax.experimental.pallas import tpu as pltpu
from jax.sharding import PartitionSpec as P

D = 8192
GROUP = 8
HD = 128
STEPS = 2
TILE = 128
CONTEXT = 16
EXTRA = 16
NOWHERE = 63
ABSENT = 2.0**100
BF = jnp.bfloat16
F32 = jnp.float32
VMEM_BYTES = 32 * 1024 * 1024


def ring_of(tensors):
    return list(range(0, tensors, 2)) + list(range(tensors - 1, 0, -2))


def iota(shape, axis):
    return lax.broadcasted_iota(jnp.int32, shape, axis)


def dot(a, b, contract=((1,), (0,))):
    return lax.dot_general(a, b, (contract, ((), ())), preferred_element_type=F32)


def plane_of(instance):
    return (instance >> 2) * 2 + (instance & 1)


def half_of(instance):
    return (instance >> 1) & 1


def weight_copy(weight, blocks, sems, offset, place):
    tensors, lanes = lax.axis_size("tensor"), blocks.shape[2]
    me = lax.axis_index("tensor")
    at = jnp.where(me % 2 == 0, me // 2, tensors - 1 - me // 2)
    at = (at + offset + tensors) % tensors
    owner = jnp.where(at < (tensors + 1) // 2, 2 * at, 2 * (tensors - at) - 1)
    columns = pl.ds(pl.multiple_of(owner * lanes, lanes), lanes)
    return pltpu.make_async_copy(weight.at[:, columns], blocks.at[place], sems.at[place])


def pair_of_chunks(capacity, scaled, extra, codes, block, mirrored, out, mirrored_out):
    rows, lanes = scaled.shape[0], out.shape[1]
    here = dot(scaled[...], block[...])
    there = dot(scaled[...], mirrored[...])
    row = iota((rows, lanes), 0)
    crosses = (row < codes[1:2, :1]) & (row < capacity)
    out[:rows, :] = jnp.where(crosses, there, here).astype(BF)
    mirrored_out[:rows, :] = jnp.where(crosses, here, there).astype(BF)
    out[rows:, :] = extra[...]
    mirrored_out[rows:, :] = extra[...]


def first_chunks(offsets, *refs):
    operands, weight = refs[:5], refs[5]
    outs, (scaled, extra, codes), (blocks, sems) = refs[6:8], refs[8:11], refs[11:13]
    held, held_sems = refs[13:18], refs[18]
    fetches = [
        pltpu.make_async_copy(source, target, held_sems.at[i])
        for i, (source, target) in enumerate(zip(operands, held))
    ]
    for fetch in fetches:
        fetch.start()
    copies = [weight_copy(weight, blocks, sems, offset, i) for i, offset in enumerate(offsets)]
    for copy in copies:
        copy.start()
    dest, length, gain, fresh, hidden = held
    requests = dest.shape[1]
    context = hidden.shape[0] // requests
    rows, capacity = scaled.shape[0], scaled.shape[0] - fresh.shape[0]
    for fetch in fetches[:2]:
        fetch.wait()
    half = half_of(lax.axis_index("inst"))

    def upright(line):
        diagonal = iota((requests, requests), 0) == iota((requests, requests), 1)
        return jnp.sum(jnp.where(diagonal, line, 0), axis=1, keepdims=True)

    lengths, dests = length[...], dest[...]
    cross = jnp.where(half_of(dests) != half, 1, 0)
    crossing = jnp.sum(cross * lengths, axis=1, keepdims=True)
    cross_up, lengths_up, dests_up = upright(cross), upright(lengths), upright(dests)
    earlier = iota((requests, requests), 1) < iota((requests, requests), 0)
    sooner = (cross > cross_up) | ((cross == cross_up) & earlier)
    start = jnp.sum(jnp.where(sooner, lengths, 0), axis=1, keepdims=True)
    shape = (requests, hidden.shape[0])
    lane = iota(shape, 1)
    at = lane % context
    here = (lane // context == iota(shape, 0)) & (at < lengths_up)
    target = jnp.sum(jnp.where(here, start + at + 1, 0), axis=0, keepdims=True) - 1
    inside = (lane >= start) & (lane < start + lengths_up)
    code = jnp.where(inside, plane_of(dests_up) * context + lane - start + 1, 0)
    code = jnp.sum(code, axis=0, keepdims=True) - 1
    codes[...] = jnp.where(iota(codes.shape, 0) == 0, code, crossing)
    select = jnp.where(target == iota((capacity, hidden.shape[0]), 0), 1.0, 0.0).astype(BF)
    for fetch in fetches[2:]:
        fetch.wait()
    wide = jnp.concatenate([dot(select, hidden[...]), fresh[...].astype(F32)], axis=0)
    scaled[...] = (wide * gain[...]).astype(BF)
    square = wide * wide
    narrow = sum(square[:, i : i + TILE] for i in range(TILE, square.shape[1], TILE))
    column = jnp.sum(narrow + square[:, :TILE], axis=1, keepdims=True)
    lanes = extra.shape[1]
    totals = [jnp.zeros((EXTRA, TILE), F32) for _ in range(0, lanes, TILE)]
    for start in range(0, rows, TILE):
        size = min(TILE, rows - start)
        diagonal = iota((size, TILE), 0) == iota((size, TILE), 1)
        line = jnp.where(diagonal, column[start : start + size], 0.0)
        line = jnp.sum(line, axis=0, keepdims=True)
        place_here = start % lanes // TILE
        totals[place_here] = jnp.where(
            iota((EXTRA, TILE), 0) == start // lanes, line, totals[place_here]
        )
    extra[...] = jnp.concatenate(totals, axis=1).astype(BF)
    for copy in copies:
        copy.wait()
    pair_of_chunks(capacity, scaled, extra, codes, blocks.at[0], blocks.at[1], *outs)


def later_chunks(offsets, capacity, scaled, extra, codes, weight, *refs):
    outs, (blocks, sems) = refs[:-2], refs[-2:]
    copies = [weight_copy(weight, blocks, sems, offset, i) for i, offset in enumerate(offsets)]
    for copy in copies:
        copy.start()
    for i in range(0, len(copies), 2):
        copies[i].wait()
        copies[i + 1].wait()
        pair_of_chunks(
            capacity, scaled, extra, codes, blocks.at[i], blocks.at[i + 1], *outs[i : i + 2]
        )


def project_chunks(hidden, fresh, gain, weight, dest, length, capacity, lanes):
    rows, depth = capacity + fresh.shape[0], hidden.shape[1]
    chunk = jax.ShapeDtypeStruct((rows + EXTRA, lanes), BF)
    tensors = lax.axis_size("tensor")
    offsets = ring_offsets(tensors)
    pairs = []
    for offset in offsets:
        if all(offset not in pair for pair in pairs):
            pairs.append((offset, offset - tensors // 2 if offset > 0 else offset + tensors // 2))
    vmem = pl.BlockSpec(memory_space=pltpu.VMEM)
    hbm = pl.BlockSpec(memory_space=pltpu.HBM)

    def options(count, name, *more):
        return dict(
            scratch_shapes=[
                pltpu.VMEM((count, depth, lanes), BF),
                pltpu.SemaphoreType.DMA((count,)),
                *more,
            ],
            compiler_params=pltpu.CompilerParams(vmem_limit_bytes=VMEM_BYTES),
            cost_estimate=pl.CostEstimate(
                flops=2 * rows * depth * lanes * count,
                bytes_accessed=2 * (rows * depth + count * (depth + rows) * lanes),
                transcendentals=0,
            ),
            name=name,
        )

    operands = [dest[None, :], length[None, :], gain, fresh, hidden]
    *first, scaled, extra, codes = pl.pallas_call(
        functools.partial(first_chunks, pairs[0]),
        in_specs=[hbm] * 6,
        out_shape=[
            chunk,
            chunk,
            jax.ShapeDtypeStruct((rows, depth), BF),
            jax.ShapeDtypeStruct((EXTRA, lanes), BF),
            jax.ShapeDtypeStruct((8, hidden.shape[0]), jnp.int32),
        ],
        **options(
            2,
            "first_chunks",
            *(pltpu.VMEM(operand.shape, operand.dtype) for operand in operands),
            pltpu.SemaphoreType.DMA((len(operands),)),
        ),
    )(*operands, weight)
    chunks = dict(zip(pairs[0], first))
    for group, name in ((pairs[1:2], "second_chunks"), (pairs[2:], "later_chunks")):
        group = [offset for pair in group for offset in pair]
        outs = pl.pallas_call(
            functools.partial(later_chunks, group, capacity),
            in_specs=[vmem, vmem, vmem, hbm],
            out_shape=[chunk] * len(group),
            **options(len(group), name),
        )(scaled, extra, codes, weight)
        chunks.update(zip(group, outs))
    return [chunks[offset] for offset in offsets], codes


def ring_offsets(tensors):
    ahead = tensors // 2
    behind = tensors - 1 - ahead
    offsets = []
    for step in range(ahead):
        offsets.append(ahead - step)
        if step < behind:
            offsets.append(step - behind)
    return offsets + [0]


def ring_order(tensors):
    ring = ring_of(tensors)
    table = [
        [ring[(ring.index(device) + offset) % tensors] for offset in ring_offsets(tensors)]
        for device in range(tensors)
    ]
    return jnp.array(table, jnp.int32)[lax.axis_index("tensor")]


def ring_sums(chunks):
    tensors = lax.axis_size("tensor")
    ring = ring_of(tensors)
    forward = [(ring[i], ring[(i + 1) % tensors]) for i in range(tensors)]
    backward = [(b, a) for a, b in forward]
    sums = {True: None, False: None}
    for offset, chunk in zip(ring_offsets(tensors), chunks[:-1]):
        way = offset > 0
        if sums[way] is not None:
            chunk = (sums[way].astype(F32) + chunk.astype(F32)).astype(BF)
        sums[way] = lax.ppermute(chunk, "tensor", forward if way else backward)
    return sums[True], sums[False], chunks[-1]


def finish_rows(codes, ahead, behind, own, crossing_rows, kept):
    total = ahead[...].astype(F32) + behind[...].astype(F32) + own[...].astype(F32)
    rows, lanes = kept.shape
    squares = total[rows:]
    for start in range(0, rows, TILE):
        size = min(TILE, rows - start)
        across = squares[start // lanes : start // lanes + 1, start % lanes : start % lanes + TILE]
        diagonal = iota((size, TILE), 0) == iota((size, TILE), 1)
        column = jnp.sum(jnp.where(diagonal, across, 0.0), axis=1, keepdims=True)
        kept[start : start + size, :] = (
            total[start : start + size] * lax.rsqrt(column / D + 1e-06)
        ).astype(BF)
    sent = crossing_rows.shape[0] - EXTRA
    crossing_rows[:sent, :] = kept[:sent, :]
    wide = min(lanes, codes.shape[1])
    code, count = codes[0:1, :wide], codes[1:2, :wide]
    if wide < lanes:
        code = jnp.concatenate([code, jnp.zeros((1, lanes - wide), jnp.int32)], axis=1)
        count = jnp.concatenate([count, jnp.zeros((1, lanes - wide), jnp.int32)], axis=1)
    lane, line = iota((EXTRA, lanes), 1), iota((EXTRA, lanes), 0)
    used = (lane < count) & (lane < sent)
    notes = jnp.where(used, code // CONTEXT, NOWHERE)
    notes = jnp.where(line == 1, code % CONTEXT, notes)
    notes = jnp.where(line == 2, count // CONTEXT, notes)
    notes = jnp.where(line == 3, count % CONTEXT, notes)
    crossing_rows[sent:, :] = notes.astype(F32).astype(BF)


def finish(codes, ahead, behind, own, sent):
    rows, lanes = own.shape[0] - EXTRA, own.shape[1]
    return pl.pallas_call(
        finish_rows,
        out_shape=[
            jax.ShapeDtypeStruct((sent + EXTRA, lanes), BF),
            jax.ShapeDtypeStruct((rows, lanes), BF),
        ],
        compiler_params=pltpu.CompilerParams(vmem_limit_bytes=VMEM_BYTES),
        name="finish_rows",
    )(codes, ahead, behind, own)


def routed(route, rows):
    found = jnp.sum(route, axis=1, keepdims=True) > 0.5
    return jnp.where(found, dot(route.astype(BF), rows), ABSENT).astype(BF)


def place_staying(codes, first, second, out):
    capacity = codes.shape[1] - second.shape[0]
    slots, context, lanes = out.shape
    shape = (slots * context, codes.shape[1])
    code, crossing = codes[0:1, :], codes[1:2, :]
    route = (iota(shape, 0) == code) & (iota(shape, 1) >= crossing)
    rows = jnp.concatenate([first[:capacity, :], second[...]], axis=0)
    out[...] = routed(jnp.where(route, 1.0, 0.0), rows).reshape(out.shape)


def place_crossing(received, codes, near, out, most):
    slots, context, lanes = near.shape
    sent = received.shape[0] - EXTRA
    notes = received[sent:, :].astype(F32).astype(jnp.int32)
    code = notes[0:1, :sent] * context + notes[1:2, :sent]
    route = iota((slots * context, sent), 0) == code
    out[:, :context, :] = near[...]
    out[:, context:, :] = routed(jnp.where(route, 1.0, 0.0), received[:sent, :]).reshape(near.shape)
    counts = jnp.maximum(notes[2:3, :sent] * context + notes[3:4, :sent], codes[1:2, :sent])
    most[0] = jnp.max(counts)


def place(kernel, out_shape, out_specs, *operands):
    return pl.pallas_call(
        kernel,
        out_shape=out_shape,
        out_specs=out_specs,
        compiler_params=pltpu.CompilerParams(vmem_limit_bytes=VMEM_BYTES),
        name=kernel.__name__,
    )(*operands)


def rebuild_and_attend(
    arrived, resident, resident_valid, queries, kept, wanted, rebuilt, attended
):
    plane, context, lanes = arrived.shape
    slots, context = 2 * plane, context // 2
    steps, batch, width = queries.shape
    rows = slots * context
    fresh = kept[kept.shape[0] - steps * batch :, :]
    columns = rebuilt.shape[1]
    held = resident.shape[1]
    heads = width // HD
    blocks = arrived[...].reshape(rows, lanes)
    half = half_of(lax.axis_index("inst"))

    def instance_of(slot):
        place = slot >> 1
        there = jnp.where(slot % 2 == 0, half, 1 - half)
        return (place >> 1) * 4 + there * 2 + (place & 1)

    valid = blocks[:, :TILE].astype(F32) < ABSENT / 2
    flags = jnp.where(valid, 1.0, 0.0).astype(BF)
    opening = jnp.where(iota((slots, rows), 1) == iota((slots, rows), 0) * context, 1.0, 0.0)
    living = dot(opening.astype(BF), flags).astype(BF)
    sooner = instance_of(iota((rows, slots), 1)) < instance_of(iota((rows, slots), 0) // context)
    before = jnp.where(sooner, 1.0, 0.0)
    ranking = dot(before.astype(BF), living)
    target = ranking.astype(jnp.int32) * context + iota((rows, TILE), 0) % context
    target = jnp.where(valid, target, -1)
    routes = jnp.concatenate(
        [
            jnp.where(target == iota((rows, TILE), 1) + start, 1.0, 0.0).astype(BF)
            for start in range(0, columns, TILE)
        ],
        axis=1,
    )[:, :columns]
    moved = dot(blocks, routes, ((0,), (0,))).astype(BF)
    rebuilt[...] = moved
    filled = dot(jnp.ones((EXTRA, rows), BF), routes)[:1] > 0.5

    query = jnp.concatenate(
        [queries[s, :, h * HD : (h + 1) * HD] for s in range(steps) for h in range(heads)], axis=0
    )
    count = query.shape[0]
    scale = 1.0 / HD**0.5
    want = wanted[...]

    def request_of(size):
        return iota((count, size), 1) // context

    mask_held = (want == request_of(held)) & (resident_valid[...] > 0)
    mask_moved = (want == request_of(columns) + held // context) & filled
    line, mark = iota((count, steps * batch), 0), iota((count, steps * batch), 1)
    mask_fresh = (line % batch == mark % batch) & (mark // batch <= line // (heads * batch))
    lowest = -1e30
    score_held = jnp.where(mask_held, dot(query, resident[:HD, :]) * scale, lowest)
    score_moved = jnp.where(mask_moved, dot(query, moved[:HD]) * scale, lowest)
    score_fresh = jnp.where(
        mask_fresh, dot(query, fresh[:, :HD], ((1,), (1,))) * scale, lowest
    )
    top = jnp.maximum(
        jnp.maximum(
            jnp.max(score_held, axis=1, keepdims=True), jnp.max(score_moved, axis=1, keepdims=True)
        ),
        jnp.max(score_fresh, axis=1, keepdims=True),
    )
    exp_held = jnp.where(mask_held, jnp.exp(score_held - top), 0.0)
    exp_moved = jnp.where(mask_moved, jnp.exp(score_moved - top), 0.0)
    exp_fresh = jnp.where(mask_fresh, jnp.exp(score_fresh - top), 0.0)
    total = (
        jnp.sum(exp_held, axis=1, keepdims=True)
        + jnp.sum(exp_moved, axis=1, keepdims=True)
        + jnp.sum(exp_fresh, axis=1, keepdims=True)
    )
    across = ((1,), (1,))
    out = dot((exp_held / total).astype(BF), resident[HD:, :], across)
    out = out + dot((exp_moved / total).astype(BF), moved[HD:], across)
    out = out + dot((exp_fresh / total).astype(BF), fresh[:, HD:])
    out = out.astype(BF)
    for s in range(steps):
        for h in range(heads):
            start = (s * heads + h) * batch
            attended[s, :, h * HD : (h + 1) * HD] = out[start : start + batch]


def rebuild(arrived, resident, resident_valid, queries, kept, wanted, columns):
    return pl.pallas_call(
        rebuild_and_attend,
        out_shape=[
            jax.ShapeDtypeStruct((arrived.shape[2], columns), BF),
            jax.ShapeDtypeStruct(queries.shape, BF),
        ],
        compiler_params=pltpu.CompilerParams(vmem_limit_bytes=VMEM_BYTES),
        name="rebuild_and_attend",
    )(arrived, resident, resident_valid, queries, kept, wanted)


def remaining_rows(hidden, gain, weight, codes, target_of, capacity, lanes):
    tensors = lax.axis_size("tensor")
    left = hidden.shape[0] - capacity
    select = (target_of[None, :] == capacity + jnp.arange(left, dtype=jnp.int32)[:, None]).astype(BF)
    wide = jnp.dot(select, hidden, preferred_element_type=F32)
    squares = jnp.sum(wide * wide, axis=1)
    distance = 1
    while distance < tensors:
        pairs = [(i, i ^ distance) for i in range(tensors)]
        squares = squares + lax.ppermute(squares, "tensor", pairs)
        distance *= 2
    parts = jnp.dot((wide * gain).astype(BF), weight, preferred_element_type=F32).astype(BF)
    order = ring_order(tensors)
    crosses = capacity + jnp.arange(left, dtype=jnp.int32)[:, None] < codes[1, 0]

    def block_of(owner):
        return lax.dynamic_slice_in_dim(parts, owner * lanes, lanes, 1)

    chunks = [
        jnp.where(crosses, block_of(tensors - 1 - order[i]), block_of(order[i]))
        for i in range(tensors)
    ]
    ahead, behind, own = ring_sums(chunks)
    total = ahead.astype(F32) + behind.astype(F32) + own.astype(F32)
    return (total * lax.rsqrt(squares / D + 1e-06)[:, None]).astype(BF)


def shards(
    hidden_rows,
    kv_weight,
    norm_gain,
    resident_cache,
    queries,
    fresh_hidden,
    move_dest,
    move_len,
    resident_len,
    decode_ids,
):
    requests = move_dest.shape[0]
    leaving = hidden_rows.shape[0]
    context = leaving // requests
    instances = lax.axis_size("inst")
    owned = kv_weight.shape[1] // lax.axis_size("tensor")
    assert owned == 2 * HD and context == CONTEXT
    steps, batch_rows, features = fresh_hidden.shape
    heads = queries.shape[2] // HD
    fresh_rows = steps * batch_rows
    capacity = max(leaving * 23 // 32 // 16, 1) * 16
    sent = max(leaving * 15 // 32 // 16, 1) * 16
    plane = instances // 2
    mine = lax.axis_index("inst").astype(jnp.int32)[None]
    fresh = fresh_hidden.reshape(fresh_rows, features)
    gain = norm_gain[None, :]
    resident_valid = (
        jnp.arange(context, dtype=jnp.int32)[None, :] < resident_len[:, None]
    ).astype(jnp.int32)
    resident_valid = resident_valid.reshape(1, -1)
    wanted = jnp.tile(decode_ids, steps * heads)[:, None]

    chunks, codes = project_chunks(
        hidden_rows, fresh, gain, kv_weight, move_dest, move_len, capacity, owned
    )
    ahead, behind, own = ring_sums(chunks)
    crossing_rows, kept = finish(codes, ahead, behind, own, sent)

    def second_pass():
        cross = half_of(move_dest) != half_of(mine)
        index = jnp.arange(requests, dtype=jnp.int32)
        sooner = (cross[:, None] > cross[None, :]) | (
            (cross[:, None] == cross[None, :]) & (index[:, None] < index[None, :])
        )
        start = jnp.sum(jnp.where(sooner, move_len[:, None], 0), axis=0)
        position = jnp.arange(context, dtype=jnp.int32)[None, :]
        target = jnp.where(position < move_len[:, None], start[:, None] + position, -1)
        return remaining_rows(
            hidden_rows, gain, kv_weight, codes, target.reshape(-1), capacity, owned
        )

    rest = lax.cond(
        jnp.sum(move_len) > capacity,
        second_pass,
        lambda: jnp.zeros((leaving - capacity, owned), BF),
    )

    tensors = lax.axis_size("tensor")
    halves = [
        (i * tensors + t, (i ^ 2) * tensors + tensors - 1 - t)
        for i in range(instances)
        for t in range(tensors)
    ]
    planes = [[i for i in range(instances) if half_of(i) == half] for half in range(2)]

    received = lax.ppermute(crossing_rows, ("inst", "tensor"), halves)
    blocks_type = jax.ShapeDtypeStruct((plane, context, owned), BF)
    vmem = pl.BlockSpec(memory_space=pltpu.VMEM)
    near = place(place_staying, blocks_type, vmem, codes, kept, rest)
    both_type = jax.ShapeDtypeStruct((plane, 2 * context, owned), BF)
    most_type = jax.ShapeDtypeStruct((1,), jnp.int32)
    outgoing, most = place(
        place_crossing,
        (both_type, most_type),
        (vmem, pl.BlockSpec(memory_space=pltpu.SMEM)),
        received,
        codes,
        near,
    )

    def all_crossing():
        rows = jnp.concatenate([kept[:capacity], rest], axis=0)
        rows = lax.ppermute(rows, ("inst", "tensor"), halves)
        notes = lax.ppermute(codes, ("inst", "tensor"), halves)
        lane = jnp.arange(leaving, dtype=jnp.int32)[None, :]
        slot = jnp.arange(plane * context, dtype=jnp.int32)[:, None]
        route = (slot == notes[0:1]) & (lane < notes[1:2])
        far = routed(route.astype(F32), rows).reshape(near.shape)
        return jnp.concatenate([near, far], axis=1)

    outgoing = lax.cond(most[0] > sent, all_crossing, lambda: outgoing)
    arrived = lax.all_to_all(
        outgoing, "inst", split_axis=0, concat_axis=0, tiled=True, axis_index_groups=planes
    )
    return tuple(
        rebuild(arrived, resident_cache, resident_valid, queries, kept, wanted, leaving)
    )


def solution(mesh):
    in_specs = (
        P("inst", "tensor"),
        P("tensor", None),
        P("tensor"),
        P("tensor", "inst"),
        P(None, "inst", "tensor"),
        P(None, "inst", "tensor"),
        P("inst"),
        P("inst"),
        P("inst"),
        P("inst"),
    )
    out_specs = (P("tensor", "inst"), P(None, "inst", "tensor"))
    return jax.shard_map(shards, mesh=mesh, in_specs=in_specs, out_specs=out_specs, check_vma=False)
```

```python
import functools

import jax
import jax.numpy as jnp
from jax import lax
from jax.experimental import pallas as pl
from jax.experimental.pallas import tpu as pltpu
from jax.sharding import PartitionSpec as P

D = 8192
GROUP = 8
HD = 128
STEPS = 2
TILE = 128
CONTEXT = 16
EXTRA = 16
NOWHERE = 63
ABSENT = 2.0**100
BF = jnp.bfloat16
F32 = jnp.float32
VMEM_BYTES = 32 * 1024 * 1024


def ring_of(tensors):
    return list(range(0, tensors, 2)) + list(range(tensors - 1, 0, -2))


def iota(shape, axis):
    return lax.broadcasted_iota(jnp.int32, shape, axis)


def dot(a, b, contract=((1,), (0,))):
    return lax.dot_general(a, b, (contract, ((), ())), preferred_element_type=F32)


def plane_of(instance):
    return (instance >> 2) * 2 + (instance & 1)


def core_of(instance):
    return instance & 1


def half_of(instance):
    return (instance >> 1) & 1


def weight_copy(weight, blocks, sems, offset, place):
    tensors, lanes = lax.axis_size("tensor"), blocks.shape[2]
    me = lax.axis_index("tensor")
    at = jnp.where(me % 2 == 0, me // 2, tensors - 1 - me // 2)
    sense = 1 - 2 * core_of(lax.axis_index("inst"))
    at = (at + sense * offset + tensors) % tensors
    owner = jnp.where(at < (tensors + 1) // 2, 2 * at, 2 * (tensors - at) - 1)
    columns = pl.ds(pl.multiple_of(owner * lanes, lanes), lanes)
    return pltpu.make_async_copy(weight.at[:, columns], blocks.at[place], sems.at[place])


def pair_of_chunks(capacity, scaled, extra, codes, block, mirrored, out, mirrored_out):
    rows, lanes = scaled.shape[0], out.shape[1]
    here = dot(scaled[...], block[...])
    there = dot(scaled[...], mirrored[...])
    row = iota((rows, lanes), 0)
    crosses = (row < codes[1:2, :1]) & (row < capacity)
    out[:rows, :] = jnp.where(crosses, there, here).astype(BF)
    mirrored_out[:rows, :] = jnp.where(crosses, here, there).astype(BF)
    out[rows:, :] = extra[...]
    mirrored_out[rows:, :] = extra[...]


def first_chunks(offsets, *refs):
    operands, weight = refs[:5], refs[5]
    outs, (scaled, extra, codes), (blocks, sems) = refs[6:8], refs[8:11], refs[11:13]
    held, held_sems = refs[13:18], refs[18]
    fetches = [
        pltpu.make_async_copy(source, target, held_sems.at[i])
        for i, (source, target) in enumerate(zip(operands, held))
    ]
    for fetch in fetches:
        fetch.start()
    copies = [weight_copy(weight, blocks, sems, offset, i) for i, offset in enumerate(offsets)]
    for copy in copies:
        copy.start()
    dest, length, gain, fresh, hidden = held
    requests = dest.shape[1]
    context = hidden.shape[0] // requests
    rows, capacity = scaled.shape[0], scaled.shape[0] - fresh.shape[0]
    for fetch in fetches[:2]:
        fetch.wait()
    half = half_of(lax.axis_index("inst"))

    def upright(line):
        diagonal = iota((requests, requests), 0) == iota((requests, requests), 1)
        return jnp.sum(jnp.where(diagonal, line, 0), axis=1, keepdims=True)

    lengths, dests = length[...], dest[...]
    cross = jnp.where(half_of(dests) != half, 1, 0)
    crossing = jnp.sum(cross * lengths, axis=1, keepdims=True)
    cross_up, lengths_up, dests_up = upright(cross), upright(lengths), upright(dests)
    earlier = iota((requests, requests), 1) < iota((requests, requests), 0)
    sooner = (cross > cross_up) | ((cross == cross_up) & earlier)
    start = jnp.sum(jnp.where(sooner, lengths, 0), axis=1, keepdims=True)
    shape = (requests, hidden.shape[0])
    lane = iota(shape, 1)
    at = lane % context
    here = (lane // context == iota(shape, 0)) & (at < lengths_up)
    target = jnp.sum(jnp.where(here, start + at + 1, 0), axis=0, keepdims=True) - 1
    inside = (lane >= start) & (lane < start + lengths_up)
    code = jnp.where(inside, plane_of(dests_up) * context + lane - start + 1, 0)
    code = jnp.sum(code, axis=0, keepdims=True) - 1
    codes[...] = jnp.where(iota(codes.shape, 0) == 0, code, crossing)
    select = jnp.where(target == iota((capacity, hidden.shape[0]), 0), 1.0, 0.0).astype(BF)
    for fetch in fetches[2:]:
        fetch.wait()
    wide = jnp.concatenate([dot(select, hidden[...]), fresh[...].astype(F32)], axis=0)
    scaled[...] = (wide * gain[...]).astype(BF)
    square = wide * wide
    narrow = sum(square[:, i : i + TILE] for i in range(TILE, square.shape[1], TILE))
    column = jnp.sum(narrow + square[:, :TILE], axis=1, keepdims=True)
    lanes = extra.shape[1]
    totals = [jnp.zeros((EXTRA, TILE), F32) for _ in range(0, lanes, TILE)]
    for start in range(0, rows, TILE):
        size = min(TILE, rows - start)
        diagonal = iota((size, TILE), 0) == iota((size, TILE), 1)
        line = jnp.where(diagonal, column[start : start + size], 0.0)
        line = jnp.sum(line, axis=0, keepdims=True)
        place_here = start % lanes // TILE
        totals[place_here] = jnp.where(
            iota((EXTRA, TILE), 0) == start // lanes, line, totals[place_here]
        )
    extra[...] = jnp.concatenate(totals, axis=1).astype(BF)
    for copy in copies:
        copy.wait()
    pair_of_chunks(capacity, scaled, extra, codes, blocks.at[0], blocks.at[1], *outs)


def later_chunks(offsets, capacity, scaled, extra, codes, weight, *refs):
    outs, (blocks, sems) = refs[:-2], refs[-2:]
    copies = [weight_copy(weight, blocks, sems, offset, i) for i, offset in enumerate(offsets)]
    for copy in copies:
        copy.start()
    for i in range(0, len(copies), 2):
        copies[i].wait()
        copies[i + 1].wait()
        pair_of_chunks(
            capacity, scaled, extra, codes, blocks.at[i], blocks.at[i + 1], *outs[i : i + 2]
        )


def project_chunks(hidden, fresh, gain, weight, dest, length, capacity, lanes):
    rows, depth = capacity + fresh.shape[0], hidden.shape[1]
    chunk = jax.ShapeDtypeStruct((rows + EXTRA, lanes), BF)
    tensors = lax.axis_size("tensor")
    offsets = ring_offsets(tensors)
    pairs = []
    for offset in offsets:
        if all(offset not in pair for pair in pairs):
            pairs.append((offset, offset - tensors // 2 if offset > 0 else offset + tensors // 2))
    vmem = pl.BlockSpec(memory_space=pltpu.VMEM)
    hbm = pl.BlockSpec(memory_space=pltpu.HBM)

    def options(count, name, *more):
        return dict(
            scratch_shapes=[
                pltpu.VMEM((count, depth, lanes), BF),
                pltpu.SemaphoreType.DMA((count,)),
                *more,
            ],
            compiler_params=pltpu.CompilerParams(vmem_limit_bytes=VMEM_BYTES),
            cost_estimate=pl.CostEstimate(
                flops=2 * rows * depth * lanes * count,
                bytes_accessed=2 * (rows * depth + count * (depth + rows) * lanes),
                transcendentals=0,
            ),
            name=name,
        )

    operands = [dest[None, :], length[None, :], gain, fresh, hidden]
    *first, scaled, extra, codes = pl.pallas_call(
        functools.partial(first_chunks, pairs[0]),
        in_specs=[hbm] * 6,
        out_shape=[
            chunk,
            chunk,
            jax.ShapeDtypeStruct((rows, depth), BF),
            jax.ShapeDtypeStruct((EXTRA, lanes), BF),
            jax.ShapeDtypeStruct((8, hidden.shape[0]), jnp.int32),
        ],
        **options(
            2,
            "first_chunks",
            *(pltpu.VMEM(operand.shape, operand.dtype) for operand in operands),
            pltpu.SemaphoreType.DMA((len(operands),)),
        ),
    )(*operands, weight)
    chunks = dict(zip(pairs[0], first))
    for group, name in ((pairs[1:2], "second_chunks"), (pairs[2:], "later_chunks")):
        group = [offset for pair in group for offset in pair]
        outs = pl.pallas_call(
            functools.partial(later_chunks, group, capacity),
            in_specs=[vmem, vmem, vmem, hbm],
            out_shape=[chunk] * len(group),
            **options(len(group), name),
        )(scaled, extra, codes, weight)
        chunks.update(zip(group, outs))
    return [chunks[offset] for offset in offsets], codes


def ring_offsets(tensors):
    ahead = tensors // 2
    behind = tensors - 1 - ahead
    offsets = []
    for step in range(ahead):
        offsets.append(ahead - step)
        if step < behind:
            offsets.append(step - behind)
    return offsets + [0]


def ring_order(tensors):
    ring = ring_of(tensors)
    offsets = jnp.array(ring_offsets(tensors), jnp.int32)
    at = jnp.array([ring.index(i) for i in range(tensors)], jnp.int32)[lax.axis_index("tensor")]
    sense = 1 - 2 * core_of(lax.axis_index("inst"))
    return jnp.array(ring, jnp.int32)[(at + sense * offsets + tensors) % tensors]


def ring_sums(chunks):
    tensors = lax.axis_size("tensor")
    ring = ring_of(tensors)
    links = [(ring[i], ring[(i + 1) % tensors]) for i in range(tensors)]
    forward, backward = [], []
    for instance in range(lax.axis_size("inst")):
        ways = (forward, backward) if core_of(instance) == 0 else (backward, forward)
        for a, b in links:
            a, b = instance * tensors + a, instance * tensors + b
            ways[0].append((a, b))
            ways[1].append((b, a))
    sums = {True: None, False: None}
    for offset, chunk in zip(ring_offsets(tensors), chunks[:-1]):
        way = offset > 0
        if sums[way] is not None:
            chunk = (sums[way].astype(F32) + chunk.astype(F32)).astype(BF)
        sums[way] = lax.ppermute(chunk, ("inst", "tensor"), forward if way else backward)
    return sums[True], sums[False], chunks[-1]


def finish_rows(codes, ahead, behind, own, crossing_rows, kept):
    total = ahead[...].astype(F32) + behind[...].astype(F32) + own[...].astype(F32)
    rows, lanes = kept.shape
    squares = total[rows:]
    for start in range(0, rows, TILE):
        size = min(TILE, rows - start)
        across = squares[start // lanes : start // lanes + 1, start % lanes : start % lanes + TILE]
        diagonal = iota((size, TILE), 0) == iota((size, TILE), 1)
        column = jnp.sum(jnp.where(diagonal, across, 0.0), axis=1, keepdims=True)
        kept[start : start + size, :] = (
            total[start : start + size] * lax.rsqrt(column / D + 1e-06)
        ).astype(BF)
    sent = crossing_rows.shape[0] - EXTRA
    crossing_rows[:sent, :] = kept[:sent, :]
    wide = min(lanes, codes.shape[1])
    code, count = codes[0:1, :wide], codes[1:2, :wide]
    if wide < lanes:
        code = jnp.concatenate([code, jnp.zeros((1, lanes - wide), jnp.int32)], axis=1)
        count = jnp.concatenate([count, jnp.zeros((1, lanes - wide), jnp.int32)], axis=1)
    lane, line = iota((EXTRA, lanes), 1), iota((EXTRA, lanes), 0)
    used = (lane < count) & (lane < sent)
    notes = jnp.where(used, code // CONTEXT, NOWHERE)
    notes = jnp.where(line == 1, code % CONTEXT, notes)
    notes = jnp.where(line == 2, count // CONTEXT, notes)
    notes = jnp.where(line == 3, count % CONTEXT, notes)
    crossing_rows[sent:, :] = notes.astype(F32).astype(BF)


def finish(codes, ahead, behind, own, sent):
    rows, lanes = own.shape[0] - EXTRA, own.shape[1]
    return pl.pallas_call(
        finish_rows,
        out_shape=[
            jax.ShapeDtypeStruct((sent + EXTRA, lanes), BF),
            jax.ShapeDtypeStruct((rows, lanes), BF),
        ],
        compiler_params=pltpu.CompilerParams(vmem_limit_bytes=VMEM_BYTES),
        name="finish_rows",
    )(codes, ahead, behind, own)


def routed(route, rows):
    found = jnp.sum(route, axis=1, keepdims=True) > 0.5
    return jnp.where(found, dot(route.astype(BF), rows), ABSENT).astype(BF)


def place_staying(codes, first, second, out):
    capacity = codes.shape[1] - second.shape[0]
    slots, context, lanes = out.shape
    shape = (slots * context, codes.shape[1])
    code, crossing = codes[0:1, :], codes[1:2, :]
    route = (iota(shape, 0) == code) & (iota(shape, 1) >= crossing)
    rows = jnp.concatenate([first[:capacity, :], second[...]], axis=0)
    out[...] = routed(jnp.where(route, 1.0, 0.0), rows).reshape(out.shape)


def place_crossing(received, codes, near, out, most):
    slots, context, lanes = near.shape
    sent = received.shape[0] - EXTRA
    notes = received[sent:, :].astype(F32).astype(jnp.int32)
    code = notes[0:1, :sent] * context + notes[1:2, :sent]
    route = iota((slots * context, sent), 0) == code
    out[:, :context, :] = near[...]
    out[:, context:, :] = routed(jnp.where(route, 1.0, 0.0), received[:sent, :]).reshape(near.shape)
    counts = jnp.maximum(notes[2:3, :sent] * context + notes[3:4, :sent], codes[1:2, :sent])
    most[0] = jnp.max(counts)


def place(kernel, out_shape, out_specs, *operands):
    return pl.pallas_call(
        kernel,
        out_shape=out_shape,
        out_specs=out_specs,
        compiler_params=pltpu.CompilerParams(vmem_limit_bytes=VMEM_BYTES),
        name=kernel.__name__,
    )(*operands)


def rebuild_and_attend(
    arrived, resident, resident_valid, queries, kept, wanted, rebuilt, attended
):
    plane, context, lanes = arrived.shape
    slots, context = 2 * plane, context // 2
    steps, batch, width = queries.shape
    rows = slots * context
    fresh = kept[kept.shape[0] - steps * batch :, :]
    columns = rebuilt.shape[1]
    held = resident.shape[1]
    heads = width // HD
    blocks = arrived[...].reshape(rows, lanes)
    half = half_of(lax.axis_index("inst"))

    def instance_of(slot):
        place = slot >> 1
        there = jnp.where(slot % 2 == 0, half, 1 - half)
        return (place >> 1) * 4 + there * 2 + (place & 1)

    valid = blocks[:, :TILE].astype(F32) < ABSENT / 2
    flags = jnp.where(valid, 1.0, 0.0).astype(BF)
    opening = jnp.where(iota((slots, rows), 1) == iota((slots, rows), 0) * context, 1.0, 0.0)
    living = dot(opening.astype(BF), flags).astype(BF)
    sooner = instance_of(iota((rows, slots), 1)) < instance_of(iota((rows, slots), 0) // context)
    before = jnp.where(sooner, 1.0, 0.0)
    ranking = dot(before.astype(BF), living)
    target = ranking.astype(jnp.int32) * context + iota((rows, TILE), 0) % context
    target = jnp.where(valid, target, -1)
    routes = jnp.concatenate(
        [
            jnp.where(target == iota((rows, TILE), 1) + start, 1.0, 0.0).astype(BF)
            for start in range(0, columns, TILE)
        ],
        axis=1,
    )[:, :columns]
    moved = dot(blocks, routes, ((0,), (0,))).astype(BF)
    rebuilt[...] = moved
    filled = dot(jnp.ones((EXTRA, rows), BF), routes)[:1] > 0.5

    query = jnp.concatenate(
        [queries[s, :, h * HD : (h + 1) * HD] for s in range(steps) for h in range(heads)], axis=0
    )
    count = query.shape[0]
    scale = 1.0 / HD**0.5
    want = wanted[...]

    def request_of(size):
        return iota((count, size), 1) // context

    mask_held = (want == request_of(held)) & (resident_valid[...] > 0)
    mask_moved = (want == request_of(columns) + held // context) & filled
    line, mark = iota((count, steps * batch), 0), iota((count, steps * batch), 1)
    mask_fresh = (line % batch == mark % batch) & (mark // batch <= line // (heads * batch))
    lowest = -1e30
    score_held = jnp.where(mask_held, dot(query, resident[:HD, :]) * scale, lowest)
    score_moved = jnp.where(mask_moved, dot(query, moved[:HD]) * scale, lowest)
    score_fresh = jnp.where(
        mask_fresh, dot(query, fresh[:, :HD], ((1,), (1,))) * scale, lowest
    )
    top = jnp.maximum(
        jnp.maximum(
            jnp.max(score_held, axis=1, keepdims=True), jnp.max(score_moved, axis=1, keepdims=True)
        ),
        jnp.max(score_fresh, axis=1, keepdims=True),
    )
    exp_held = jnp.where(mask_held, jnp.exp(score_held - top), 0.0)
    exp_moved = jnp.where(mask_moved, jnp.exp(score_moved - top), 0.0)
    exp_fresh = jnp.where(mask_fresh, jnp.exp(score_fresh - top), 0.0)
    total = (
        jnp.sum(exp_held, axis=1, keepdims=True)
        + jnp.sum(exp_moved, axis=1, keepdims=True)
        + jnp.sum(exp_fresh, axis=1, keepdims=True)
    )
    across = ((1,), (1,))
    out = dot((exp_held / total).astype(BF), resident[HD:, :], across)
    out = out + dot((exp_moved / total).astype(BF), moved[HD:], across)
    out = out + dot((exp_fresh / total).astype(BF), fresh[:, HD:])
    out = out.astype(BF)
    for s in range(steps):
        for h in range(heads):
            start = (s * heads + h) * batch
            attended[s, :, h * HD : (h + 1) * HD] = out[start : start + batch]


def rebuild(arrived, resident, resident_valid, queries, kept, wanted, columns):
    return pl.pallas_call(
        rebuild_and_attend,
        out_shape=[
            jax.ShapeDtypeStruct((arrived.shape[2], columns), BF),
            jax.ShapeDtypeStruct(queries.shape, BF),
        ],
        compiler_params=pltpu.CompilerParams(vmem_limit_bytes=VMEM_BYTES),
        name="rebuild_and_attend",
    )(arrived, resident, resident_valid, queries, kept, wanted)


def remaining_rows(hidden, gain, weight, codes, target_of, capacity, lanes):
    tensors = lax.axis_size("tensor")
    left = hidden.shape[0] - capacity
    select = (target_of[None, :] == capacity + jnp.arange(left, dtype=jnp.int32)[:, None]).astype(BF)
    wide = jnp.dot(select, hidden, preferred_element_type=F32)
    squares = jnp.sum(wide * wide, axis=1)
    distance = 1
    while distance < tensors:
        pairs = [(i, i ^ distance) for i in range(tensors)]
        squares = squares + lax.ppermute(squares, "tensor", pairs)
        distance *= 2
    parts = jnp.dot((wide * gain).astype(BF), weight, preferred_element_type=F32).astype(BF)
    order = ring_order(tensors)
    crosses = capacity + jnp.arange(left, dtype=jnp.int32)[:, None] < codes[1, 0]

    def block_of(owner):
        return lax.dynamic_slice_in_dim(parts, owner * lanes, lanes, 1)

    chunks = [
        jnp.where(crosses, block_of(tensors - 1 - order[i]), block_of(order[i]))
        for i in range(tensors)
    ]
    ahead, behind, own = ring_sums(chunks)
    total = ahead.astype(F32) + behind.astype(F32) + own.astype(F32)
    return (total * lax.rsqrt(squares / D + 1e-06)[:, None]).astype(BF)


def shards(
    hidden_rows,
    kv_weight,
    norm_gain,
    resident_cache,
    queries,
    fresh_hidden,
    move_dest,
    move_len,
    resident_len,
    decode_ids,
):
    requests = move_dest.shape[0]
    leaving = hidden_rows.shape[0]
    context = leaving // requests
    instances = lax.axis_size("inst")
    owned = kv_weight.shape[1] // lax.axis_size("tensor")
    assert owned == 2 * HD and context == CONTEXT
    steps, batch_rows, features = fresh_hidden.shape
    heads = queries.shape[2] // HD
    fresh_rows = steps * batch_rows
    capacity = max(leaving * 23 // 32 // 16, 1) * 16
    sent = max(leaving * 15 // 32 // 16, 1) * 16
    plane = instances // 2
    mine = lax.axis_index("inst").astype(jnp.int32)[None]
    fresh = fresh_hidden.reshape(fresh_rows, features)
    gain = norm_gain[None, :]
    resident_valid = (
        jnp.arange(context, dtype=jnp.int32)[None, :] < resident_len[:, None]
    ).astype(jnp.int32)
    resident_valid = resident_valid.reshape(1, -1)
    wanted = jnp.tile(decode_ids, steps * heads)[:, None]

    chunks, codes = project_chunks(
        hidden_rows, fresh, gain, kv_weight, move_dest, move_len, capacity, owned
    )
    ahead, behind, own = ring_sums(chunks)
    crossing_rows, kept = finish(codes, ahead, behind, own, sent)

    def second_pass():
        cross = half_of(move_dest) != half_of(mine)
        index = jnp.arange(requests, dtype=jnp.int32)
        sooner = (cross[:, None] > cross[None, :]) | (
            (cross[:, None] == cross[None, :]) & (index[:, None] < index[None, :])
        )
        start = jnp.sum(jnp.where(sooner, move_len[:, None], 0), axis=0)
        position = jnp.arange(context, dtype=jnp.int32)[None, :]
        target = jnp.where(position < move_len[:, None], start[:, None] + position, -1)
        return remaining_rows(
            hidden_rows, gain, kv_weight, codes, target.reshape(-1), capacity, owned
        )

    rest = lax.cond(
        jnp.sum(move_len) > capacity,
        second_pass,
        lambda: jnp.zeros((leaving - capacity, owned), BF),
    )

    tensors = lax.axis_size("tensor")
    halves = [
        (i * tensors + t, (i ^ 2) * tensors + tensors - 1 - t)
        for i in range(instances)
        for t in range(tensors)
    ]
    planes = [[i for i in range(instances) if half_of(i) == half] for half in range(2)]

    received = lax.ppermute(crossing_rows, ("inst", "tensor"), halves)
    blocks_type = jax.ShapeDtypeStruct((plane, context, owned), BF)
    vmem = pl.BlockSpec(memory_space=pltpu.VMEM)
    near = place(place_staying, blocks_type, vmem, codes, kept, rest)
    both_type = jax.ShapeDtypeStruct((plane, 2 * context, owned), BF)
    most_type = jax.ShapeDtypeStruct((1,), jnp.int32)
    outgoing, most = place(
        place_crossing,
        (both_type, most_type),
        (vmem, pl.BlockSpec(memory_space=pltpu.SMEM)),
        received,
        codes,
        near,
    )

    def all_crossing():
        rows = jnp.concatenate([kept[:capacity], rest], axis=0)
        rows = lax.ppermute(rows, ("inst", "tensor"), halves)
        notes = lax.ppermute(codes, ("inst", "tensor"), halves)
        lane = jnp.arange(leaving, dtype=jnp.int32)[None, :]
        slot = jnp.arange(plane * context, dtype=jnp.int32)[:, None]
        route = (slot == notes[0:1]) & (lane < notes[1:2])
        far = routed(route.astype(F32), rows).reshape(near.shape)
        return jnp.concatenate([near, far], axis=1)

    outgoing = lax.cond(most[0] > sent, all_crossing, lambda: outgoing)
    arrived = lax.all_to_all(
        outgoing, "inst", split_axis=0, concat_axis=0, tiled=True, axis_index_groups=planes
    )
    return tuple(
        rebuild(arrived, resident_cache, resident_valid, queries, kept, wanted, leaving)
    )


def solution(mesh):
    in_specs = (
        P("inst", "tensor"),
        P("tensor", None),
        P("tensor"),
        P("tensor", "inst"),
        P(None, "inst", "tensor"),
        P(None, "inst", "tensor"),
        P("inst"),
        P("inst"),
        P("inst"),
        P("inst"),
    )
    out_specs = (P("tensor", "inst"), P(None, "inst", "tensor"))
    return jax.shard_map(shards, mesh=mesh, in_specs=in_specs, out_specs=out_specs, check_vma=False)
```

```python
import functools

import jax
import jax.numpy as jnp
from jax import lax
from jax.experimental import pallas as pl
from jax.experimental.pallas import tpu as pltpu
from jax.sharding import PartitionSpec as P

D = 8192
GROUP = 8
HD = 128
STEPS = 2
TILE = 128
CONTEXT = 16
EXTRA = 16
NOWHERE = 63
ABSENT = 2.0**100
BF = jnp.bfloat16
F32 = jnp.float32
VMEM_BYTES = 32 * 1024 * 1024


def ring_of(tensors):
    return list(range(0, tensors, 2)) + list(range(tensors - 1, 0, -2))


def iota(shape, axis):
    return lax.broadcasted_iota(jnp.int32, shape, axis)


def dot(a, b, contract=((1,), (0,))):
    return lax.dot_general(a, b, (contract, ((), ())), preferred_element_type=F32)


def plane_of(instance):
    return (instance >> 2) * 2 + (instance & 1)


def core_of(instance):
    return instance & 1


def half_of(instance):
    return (instance >> 1) & 1


def weight_copy(weight, blocks, sems, offset, place):
    tensors, lanes = lax.axis_size("tensor"), blocks.shape[2]
    me = lax.axis_index("tensor")
    at = jnp.where(me % 2 == 0, me // 2, tensors - 1 - me // 2)
    sense = 1 - 2 * core_of(lax.axis_index("inst"))
    at = (at + sense * offset + tensors) % tensors
    owner = jnp.where(at < (tensors + 1) // 2, 2 * at, 2 * (tensors - at) - 1)
    columns = pl.ds(pl.multiple_of(owner * lanes, lanes), lanes)
    return pltpu.make_async_copy(weight.at[:, columns], blocks.at[place], sems.at[place])


def pair_of_chunks(capacity, scaled, extra, codes, block, mirrored, out, mirrored_out):
    rows, lanes = scaled.shape[0], out.shape[1]
    here = dot(scaled[...], block[...])
    there = dot(scaled[...], mirrored[...])
    row = iota((rows, lanes), 0)
    crosses = (row < codes[1:2, :1]) & (row < capacity)
    out[:rows, :] = jnp.where(crosses, there, here).astype(BF)
    mirrored_out[:rows, :] = jnp.where(crosses, here, there).astype(BF)
    out[rows:, :] = extra[...]
    mirrored_out[rows:, :] = extra[...]


def first_chunks(offsets, *refs):
    operands, weight = refs[:5], refs[5]
    outs, (scaled, extra, codes), (blocks, sems) = refs[6:8], refs[8:11], refs[11:13]
    held, held_sems = refs[13:18], refs[18]
    fetches = [
        pltpu.make_async_copy(source, target, held_sems.at[i])
        for i, (source, target) in enumerate(zip(operands, held))
    ]
    for fetch in fetches:
        fetch.start()
    copies = [weight_copy(weight, blocks, sems, offset, i) for i, offset in enumerate(offsets)]
    for copy in copies:
        copy.start()
    dest, length, gain, fresh, hidden = held
    requests = dest.shape[1]
    context = hidden.shape[0] // requests
    rows, capacity = scaled.shape[0], scaled.shape[0] - fresh.shape[0]
    for fetch in fetches[:2]:
        fetch.wait()
    half = half_of(lax.axis_index("inst"))

    def upright(line):
        diagonal = iota((requests, requests), 0) == iota((requests, requests), 1)
        return jnp.sum(jnp.where(diagonal, line, 0), axis=1, keepdims=True)

    lengths, dests = length[...], dest[...]
    cross = jnp.where(half_of(dests) != half, 1, 0)
    crossing = jnp.sum(cross * lengths, axis=1, keepdims=True)
    cross_up, lengths_up, dests_up = upright(cross), upright(lengths), upright(dests)
    earlier = iota((requests, requests), 1) < iota((requests, requests), 0)
    sooner = (cross > cross_up) | ((cross == cross_up) & earlier)
    start = jnp.sum(jnp.where(sooner, lengths, 0), axis=1, keepdims=True)
    shape = (requests, hidden.shape[0])
    lane = iota(shape, 1)
    at = lane % context
    here = (lane // context == iota(shape, 0)) & (at < lengths_up)
    target = jnp.sum(jnp.where(here, start + at + 1, 0), axis=0, keepdims=True) - 1
    inside = (lane >= start) & (lane < start + lengths_up)
    code = jnp.where(inside, plane_of(dests_up) * context + lane - start + 1, 0)
    code = jnp.sum(code, axis=0, keepdims=True) - 1
    codes[...] = jnp.where(iota(codes.shape, 0) == 0, code, crossing)
    select = jnp.where(target == iota((capacity, hidden.shape[0]), 0), 1.0, 0.0).astype(BF)
    for fetch in fetches[2:]:
        fetch.wait()
    wide = jnp.concatenate([dot(select, hidden[...]), fresh[...].astype(F32)], axis=0)
    scaled[...] = (wide * gain[...]).astype(BF)
    square = wide * wide
    narrow = sum(square[:, i : i + TILE] for i in range(TILE, square.shape[1], TILE))
    column = jnp.sum(narrow + square[:, :TILE], axis=1, keepdims=True)
    lanes = extra.shape[1]
    totals = [jnp.zeros((EXTRA, TILE), F32) for _ in range(0, lanes, TILE)]
    for start in range(0, rows, TILE):
        size = min(TILE, rows - start)
        diagonal = iota((size, TILE), 0) == iota((size, TILE), 1)
        line = jnp.where(diagonal, column[start : start + size], 0.0)
        line = jnp.sum(line, axis=0, keepdims=True)
        place_here = start % lanes // TILE
        totals[place_here] = jnp.where(
            iota((EXTRA, TILE), 0) == start // lanes, line, totals[place_here]
        )
    extra[...] = jnp.concatenate(totals, axis=1).astype(BF)
    for copy in copies:
        copy.wait()
    pair_of_chunks(capacity, scaled, extra, codes, blocks.at[0], blocks.at[1], *outs)


def later_chunks(offsets, capacity, scaled, extra, codes, weight, *refs):
    outs, (blocks, sems) = refs[:-2], refs[-2:]
    copies = [weight_copy(weight, blocks, sems, offset, i) for i, offset in enumerate(offsets)]
    for copy in copies:
        copy.start()
    for i in range(0, len(copies), 2):
        copies[i].wait()
        copies[i + 1].wait()
        pair_of_chunks(
            capacity, scaled, extra, codes, blocks.at[i], blocks.at[i + 1], *outs[i : i + 2]
        )


def project_chunks(hidden, fresh, gain, weight, dest, length, capacity, lanes):
    rows, depth = capacity + fresh.shape[0], hidden.shape[1]
    chunk = jax.ShapeDtypeStruct((rows + EXTRA, lanes), BF)
    tensors = lax.axis_size("tensor")
    offsets = ring_offsets(tensors)
    pairs = []
    for offset in offsets:
        if all(offset not in pair for pair in pairs):
            pairs.append((offset, offset - tensors // 2 if offset > 0 else offset + tensors // 2))
    vmem = pl.BlockSpec(memory_space=pltpu.VMEM)
    hbm = pl.BlockSpec(memory_space=pltpu.HBM)

    def options(count, name, *more):
        return dict(
            scratch_shapes=[
                pltpu.VMEM((count, depth, lanes), BF),
                pltpu.SemaphoreType.DMA((count,)),
                *more,
            ],
            compiler_params=pltpu.CompilerParams(vmem_limit_bytes=VMEM_BYTES),
            cost_estimate=pl.CostEstimate(
                flops=2 * rows * depth * lanes * count,
                bytes_accessed=2 * (rows * depth + count * (depth + rows) * lanes),
                transcendentals=0,
            ),
            name=name,
        )

    operands = [dest[None, :], length[None, :], gain, fresh, hidden]
    *first, scaled, extra, codes = pl.pallas_call(
        functools.partial(first_chunks, pairs[0]),
        in_specs=[hbm] * 6,
        out_shape=[
            chunk,
            chunk,
            jax.ShapeDtypeStruct((rows, depth), BF),
            jax.ShapeDtypeStruct((EXTRA, lanes), BF),
            jax.ShapeDtypeStruct((8, hidden.shape[0]), jnp.int32),
        ],
        **options(
            2,
            "first_chunks",
            *(pltpu.VMEM(operand.shape, operand.dtype) for operand in operands),
            pltpu.SemaphoreType.DMA((len(operands),)),
        ),
    )(*operands, weight)
    chunks = dict(zip(pairs[0], first))
    for group, name in ((pairs[1:2], "second_chunks"), (pairs[2:], "later_chunks")):
        group = [offset for pair in group for offset in pair]
        outs = pl.pallas_call(
            functools.partial(later_chunks, group, capacity),
            in_specs=[vmem, vmem, vmem, hbm],
            out_shape=[chunk] * len(group),
            **options(len(group), name),
        )(scaled, extra, codes, weight)
        chunks.update(zip(group, outs))
    return [chunks[offset] for offset in offsets], codes


def ring_offsets(tensors):
    ahead = tensors // 2
    behind = tensors - 1 - ahead
    offsets = []
    for step in range(ahead):
        offsets.append(ahead - step)
        if step < behind:
            offsets.append(step - behind)
    return offsets + [0]


def ring_order(tensors):
    ring = ring_of(tensors)
    offsets = jnp.array(ring_offsets(tensors), jnp.int32)
    at = jnp.array([ring.index(i) for i in range(tensors)], jnp.int32)[lax.axis_index("tensor")]
    sense = 1 - 2 * core_of(lax.axis_index("inst"))
    return jnp.array(ring, jnp.int32)[(at + sense * offsets + tensors) % tensors]


def ring_sums(chunks):
    tensors = lax.axis_size("tensor")
    ring = ring_of(tensors)
    links = [(ring[i], ring[(i + 1) % tensors]) for i in range(tensors)]
    forward, backward = [], []
    for instance in range(lax.axis_size("inst")):
        ways = (forward, backward) if core_of(instance) == 0 else (backward, forward)
        for a, b in links:
            a, b = instance * tensors + a, instance * tensors + b
            ways[0].append((a, b))
            ways[1].append((b, a))
    sums = {True: None, False: None}
    for offset, chunk in zip(ring_offsets(tensors), chunks[:-1]):
        way = offset > 0
        if sums[way] is not None:
            chunk = (sums[way].astype(F32) + chunk.astype(F32)).astype(BF)
        sums[way] = lax.ppermute(chunk, ("inst", "tensor"), forward if way else backward)
    return sums[True], sums[False], chunks[-1]


def finish_rows(codes, ahead, behind, own, crossing_rows, kept):
    total = ahead[...].astype(F32) + behind[...].astype(F32) + own[...].astype(F32)
    rows, lanes = kept.shape
    squares = total[rows:]
    for start in range(0, rows, TILE):
        size = min(TILE, rows - start)
        across = squares[start // lanes : start // lanes + 1, start % lanes : start % lanes + TILE]
        diagonal = iota((size, TILE), 0) == iota((size, TILE), 1)
        column = jnp.sum(jnp.where(diagonal, across, 0.0), axis=1, keepdims=True)
        kept[start : start + size, :] = (
            total[start : start + size] * lax.rsqrt(column / D + 1e-06)
        ).astype(BF)
    sent = crossing_rows.shape[0] - EXTRA
    crossing_rows[:sent, :] = kept[:sent, :]
    wide = min(lanes, codes.shape[1])
    code, count = codes[0:1, :wide], codes[1:2, :wide]
    if wide < lanes:
        code = jnp.concatenate([code, jnp.zeros((1, lanes - wide), jnp.int32)], axis=1)
        count = jnp.concatenate([count, jnp.zeros((1, lanes - wide), jnp.int32)], axis=1)
    lane, line = iota((EXTRA, lanes), 1), iota((EXTRA, lanes), 0)
    used = (lane < count) & (lane < sent)
    notes = jnp.where(used, code // CONTEXT, NOWHERE)
    notes = jnp.where(line == 1, code % CONTEXT, notes)
    notes = jnp.where(line == 2, count // CONTEXT, notes)
    notes = jnp.where(line == 3, count % CONTEXT, notes)
    crossing_rows[sent:, :] = notes.astype(F32).astype(BF)


def finish(codes, ahead, behind, own, sent):
    rows, lanes = own.shape[0] - EXTRA, own.shape[1]
    return pl.pallas_call(
        finish_rows,
        out_shape=[
            jax.ShapeDtypeStruct((sent + EXTRA, lanes), BF),
            jax.ShapeDtypeStruct((rows, lanes), BF),
        ],
        compiler_params=pltpu.CompilerParams(vmem_limit_bytes=VMEM_BYTES),
        name="finish_rows",
    )(codes, ahead, behind, own)


def routed(route, rows):
    found = jnp.sum(route, axis=1, keepdims=True) > 0.5
    return jnp.where(found, dot(route.astype(BF), rows), ABSENT).astype(BF)


def place_staying(codes, first, second, out):
    capacity = codes.shape[1] - second.shape[0]
    slots, context, lanes = out.shape
    shape = (slots * context, codes.shape[1])
    code, crossing = codes[0:1, :], codes[1:2, :]
    route = (iota(shape, 0) == code) & (iota(shape, 1) >= crossing)
    rows = jnp.concatenate([first[:capacity, :], second[...]], axis=0)
    out[...] = routed(jnp.where(route, 1.0, 0.0), rows).reshape(out.shape)


def place_crossing(received, codes, near, out, most):
    slots, context, lanes = near.shape
    sent = received.shape[0] - EXTRA
    notes = received[sent:, :].astype(F32).astype(jnp.int32)
    code = notes[0:1, :sent] * context + notes[1:2, :sent]
    route = iota((slots * context, sent), 0) == code
    out[:, :context, :] = near[...]
    out[:, context:, :] = routed(jnp.where(route, 1.0, 0.0), received[:sent, :]).reshape(near.shape)
    counts = jnp.maximum(notes[2:3, :sent] * context + notes[3:4, :sent], codes[1:2, :sent])
    most[0] = jnp.max(counts)


def place(kernel, out_shape, out_specs, *operands):
    return pl.pallas_call(
        kernel,
        out_shape=out_shape,
        out_specs=out_specs,
        compiler_params=pltpu.CompilerParams(vmem_limit_bytes=VMEM_BYTES),
        name=kernel.__name__,
    )(*operands)


def rebuild_and_attend(
    arrived, resident, resident_valid, queries, kept, wanted, rebuilt, attended
):
    plane, context, lanes = arrived.shape
    slots, context = 2 * plane, context // 2
    steps, batch, width = queries.shape
    rows = slots * context
    fresh = kept[kept.shape[0] - steps * batch :, :]
    columns = rebuilt.shape[1]
    held = resident.shape[1]
    heads = width // HD
    blocks = arrived[...].reshape(rows, lanes)
    half = half_of(lax.axis_index("inst"))

    def instance_of(slot):
        place = slot >> 1
        there = jnp.where(slot % 2 == 0, half, 1 - half)
        return (place >> 1) * 4 + there * 2 + (place & 1)

    valid = blocks[:, :TILE].astype(F32) < ABSENT / 2
    flags = jnp.where(valid, 1.0, 0.0).astype(BF)
    opening = jnp.where(iota((slots, rows), 1) == iota((slots, rows), 0) * context, 1.0, 0.0)
    living = dot(opening.astype(BF), flags).astype(BF)
    sooner = instance_of(iota((rows, slots), 1)) < instance_of(iota((rows, slots), 0) // context)
    before = jnp.where(sooner, 1.0, 0.0)
    ranking = dot(before.astype(BF), living)
    target = ranking.astype(jnp.int32) * context + iota((rows, TILE), 0) % context
    target = jnp.where(valid, target, -1)
    routes = jnp.concatenate(
        [
            jnp.where(target == iota((rows, TILE), 1) + start, 1.0, 0.0)
            for start in range(0, columns, TILE)
        ],
        axis=1,
    )[:, :columns]
    filled = jnp.sum(routes, axis=0, keepdims=True) > 0.5
    moved = dot(blocks, routes.astype(BF), ((0,), (0,))).astype(BF)
    rebuilt[...] = moved

    query = jnp.concatenate(
        [queries[s, :, h * HD : (h + 1) * HD] for s in range(steps) for h in range(heads)], axis=0
    )
    count = query.shape[0]
    scale = 1.0 / HD**0.5
    want = wanted[...]

    def request_of(size):
        return iota((count, size), 1) // context

    mask_held = (want == request_of(held)) & (resident_valid[...] > 0)
    mask_moved = (want == request_of(columns) + held // context) & filled
    line, mark = iota((count, steps * batch), 0), iota((count, steps * batch), 1)
    mask_fresh = (line % batch == mark % batch) & (mark // batch <= line // (heads * batch))
    lowest = -1e30
    score_held = jnp.where(mask_held, dot(query, resident[:HD, :]) * scale, lowest)
    score_moved = jnp.where(mask_moved, dot(query, moved[:HD]) * scale, lowest)
    score_fresh = jnp.where(
        mask_fresh, dot(query, fresh[:, :HD], ((1,), (1,))) * scale, lowest
    )
    top = jnp.maximum(
        jnp.maximum(
            jnp.max(score_held, axis=1, keepdims=True), jnp.max(score_moved, axis=1, keepdims=True)
        ),
        jnp.max(score_fresh, axis=1, keepdims=True),
    )
    exp_held = jnp.where(mask_held, jnp.exp(score_held - top), 0.0)
    exp_moved = jnp.where(mask_moved, jnp.exp(score_moved - top), 0.0)
    exp_fresh = jnp.where(mask_fresh, jnp.exp(score_fresh - top), 0.0)
    total = (
        jnp.sum(exp_held, axis=1, keepdims=True)
        + jnp.sum(exp_moved, axis=1, keepdims=True)
        + jnp.sum(exp_fresh, axis=1, keepdims=True)
    )
    share = 1.0 / total
    across = ((1,), (1,))
    out = dot((exp_held * share).astype(BF), resident[HD:, :], across)
    out = out + dot((exp_moved * share).astype(BF), moved[HD:], across)
    out = out + dot((exp_fresh * share).astype(BF), fresh[:, HD:])
    out = out.astype(BF)
    for s in range(steps):
        for h in range(heads):
            start = (s * heads + h) * batch
            attended[s, :, h * HD : (h + 1) * HD] = out[start : start + batch]


def rebuild(arrived, resident, resident_valid, queries, kept, wanted, columns):
    return pl.pallas_call(
        rebuild_and_attend,
        out_shape=[
            jax.ShapeDtypeStruct((arrived.shape[2], columns), BF),
            jax.ShapeDtypeStruct(queries.shape, BF),
        ],
        compiler_params=pltpu.CompilerParams(vmem_limit_bytes=VMEM_BYTES),
        name="rebuild_and_attend",
    )(arrived, resident, resident_valid, queries, kept, wanted)


def remaining_rows(hidden, gain, weight, codes, target_of, capacity, lanes):
    tensors = lax.axis_size("tensor")
    left = hidden.shape[0] - capacity
    select = (target_of[None, :] == capacity + jnp.arange(left, dtype=jnp.int32)[:, None]).astype(BF)
    wide = jnp.dot(select, hidden, preferred_element_type=F32)
    squares = jnp.sum(wide * wide, axis=1)
    distance = 1
    while distance < tensors:
        pairs = [(i, i ^ distance) for i in range(tensors)]
        squares = squares + lax.ppermute(squares, "tensor", pairs)
        distance *= 2
    parts = jnp.dot((wide * gain).astype(BF), weight, preferred_element_type=F32).astype(BF)
    order = ring_order(tensors)
    crosses = capacity + jnp.arange(left, dtype=jnp.int32)[:, None] < codes[1, 0]

    def block_of(owner):
        return lax.dynamic_slice_in_dim(parts, owner * lanes, lanes, 1)

    chunks = [
        jnp.where(crosses, block_of(tensors - 1 - order[i]), block_of(order[i]))
        for i in range(tensors)
    ]
    ahead, behind, own = ring_sums(chunks)
    total = ahead.astype(F32) + behind.astype(F32) + own.astype(F32)
    return (total * lax.rsqrt(squares / D + 1e-06)[:, None]).astype(BF)


def shards(
    hidden_rows,
    kv_weight,
    norm_gain,
    resident_cache,
    queries,
    fresh_hidden,
    move_dest,
    move_len,
    resident_len,
    decode_ids,
):
    requests = move_dest.shape[0]
    leaving = hidden_rows.shape[0]
    context = leaving // requests
    instances = lax.axis_size("inst")
    owned = kv_weight.shape[1] // lax.axis_size("tensor")
    assert owned == 2 * HD and context == CONTEXT
    steps, batch_rows, features = fresh_hidden.shape
    heads = queries.shape[2] // HD
    fresh_rows = steps * batch_rows
    capacity = max(leaving * 23 // 32 // 16, 1) * 16
    sent = max(leaving * 15 // 32 // 16, 1) * 16
    plane = instances // 2
    mine = lax.axis_index("inst").astype(jnp.int32)[None]
    fresh = fresh_hidden.reshape(fresh_rows, features)
    gain = norm_gain[None, :]
    resident_valid = (
        jnp.arange(context, dtype=jnp.int32)[None, :] < resident_len[:, None]
    ).astype(jnp.int32)
    resident_valid = resident_valid.reshape(1, -1)
    wanted = jnp.tile(decode_ids, steps * heads)[:, None]

    chunks, codes = project_chunks(
        hidden_rows, fresh, gain, kv_weight, move_dest, move_len, capacity, owned
    )
    ahead, behind, own = ring_sums(chunks)
    crossing_rows, kept = finish(codes, ahead, behind, own, sent)

    def second_pass():
        cross = half_of(move_dest) != half_of(mine)
        index = jnp.arange(requests, dtype=jnp.int32)
        sooner = (cross[:, None] > cross[None, :]) | (
            (cross[:, None] == cross[None, :]) & (index[:, None] < index[None, :])
        )
        start = jnp.sum(jnp.where(sooner, move_len[:, None], 0), axis=0)
        position = jnp.arange(context, dtype=jnp.int32)[None, :]
        target = jnp.where(position < move_len[:, None], start[:, None] + position, -1)
        return remaining_rows(
            hidden_rows, gain, kv_weight, codes, target.reshape(-1), capacity, owned
        )

    rest = lax.cond(
        jnp.sum(move_len) > capacity,
        second_pass,
        lambda: jnp.zeros((leaving - capacity, owned), BF),
    )

    tensors = lax.axis_size("tensor")
    halves = [
        (i * tensors + t, (i ^ 2) * tensors + tensors - 1 - t)
        for i in range(instances)
        for t in range(tensors)
    ]
    planes = [[i for i in range(instances) if half_of(i) == half] for half in range(2)]

    received = lax.ppermute(crossing_rows, ("inst", "tensor"), halves)
    blocks_type = jax.ShapeDtypeStruct((plane, context, owned), BF)
    vmem = pl.BlockSpec(memory_space=pltpu.VMEM)
    near = place(place_staying, blocks_type, vmem, codes, kept, rest)
    both_type = jax.ShapeDtypeStruct((plane, 2 * context, owned), BF)
    most_type = jax.ShapeDtypeStruct((1,), jnp.int32)
    outgoing, most = place(
        place_crossing,
        (both_type, most_type),
        (vmem, pl.BlockSpec(memory_space=pltpu.SMEM)),
        received,
        codes,
        near,
    )

    def all_crossing():
        rows = jnp.concatenate([kept[:capacity], rest], axis=0)
        rows = lax.ppermute(rows, ("inst", "tensor"), halves)
        notes = lax.ppermute(codes, ("inst", "tensor"), halves)
        lane = jnp.arange(leaving, dtype=jnp.int32)[None, :]
        slot = jnp.arange(plane * context, dtype=jnp.int32)[:, None]
        route = (slot == notes[0:1]) & (lane < notes[1:2])
        far = routed(route.astype(F32), rows).reshape(near.shape)
        return jnp.concatenate([near, far], axis=1)

    outgoing = lax.cond(most[0] > sent, all_crossing, lambda: outgoing)
    arrived = lax.all_to_all(
        outgoing, "inst", split_axis=0, concat_axis=0, tiled=True, axis_index_groups=planes
    )
    return tuple(
        rebuild(arrived, resident_cache, resident_valid, queries, kept, wanted, leaving)
    )


def solution(mesh):
    in_specs = (
        P("inst", "tensor"),
        P("tensor", None),
        P("tensor"),
        P("tensor", "inst"),
        P(None, "inst", "tensor"),
        P(None, "inst", "tensor"),
        P("inst"),
        P("inst"),
        P("inst"),
        P("inst"),
    )
    out_specs = (P("tensor", "inst"), P(None, "inst", "tensor"))
    return jax.shard_map(shards, mesh=mesh, in_specs=in_specs, out_specs=out_specs, check_vma=False)
```

```python
import functools

import jax
import jax.numpy as jnp
from jax import lax
from jax.experimental import pallas as pl
from jax.experimental.pallas import tpu as pltpu
from jax.sharding import PartitionSpec as P

D = 8192
GROUP = 8
HD = 128
STEPS = 2
TILE = 128
CONTEXT = 16
EXTRA = 16
NOWHERE = 63
ABSENT = 2.0**100
BF = jnp.bfloat16
F32 = jnp.float32
VMEM_BYTES = 32 * 1024 * 1024


def ring_of(tensors):
    return list(range(0, tensors, 2)) + list(range(tensors - 1, 0, -2))


def iota(shape, axis):
    return lax.broadcasted_iota(jnp.int32, shape, axis)


def dot(a, b, contract=((1,), (0,))):
    return lax.dot_general(a, b, (contract, ((), ())), preferred_element_type=F32)


def plane_of(instance):
    return (instance >> 2) * 2 + (instance & 1)


def core_of(instance):
    return instance & 1


def half_of(instance):
    return (instance >> 1) & 1


def weight_copy(weight, blocks, sems, offset, place):
    tensors, lanes = lax.axis_size("tensor"), blocks.shape[2]
    me = lax.axis_index("tensor")
    at = jnp.where(me % 2 == 0, me // 2, tensors - 1 - me // 2)
    sense = 1 - 2 * core_of(lax.axis_index("inst"))
    at = (at + sense * offset + tensors) % tensors
    owner = jnp.where(at < (tensors + 1) // 2, 2 * at, 2 * (tensors - at) - 1)
    columns = pl.ds(pl.multiple_of(owner * lanes, lanes), lanes)
    return pltpu.make_async_copy(weight.at[:, columns], blocks.at[place], sems.at[place])


def pair_of_chunks(capacity, scaled, extra, codes, block, mirrored, out, mirrored_out):
    rows, lanes = scaled.shape[0], out.shape[1]
    here = dot(scaled[...], block[...])
    there = dot(scaled[...], mirrored[...])
    row = iota((rows, lanes), 0)
    crosses = (row < codes[1:2, :1]) & (row < capacity)
    out[:rows, :] = jnp.where(crosses, there, here).astype(BF)
    mirrored_out[:rows, :] = jnp.where(crosses, here, there).astype(BF)
    out[rows:, :] = extra[...]
    mirrored_out[rows:, :] = extra[...]


def first_chunks(offsets, *refs):
    operands, weight = refs[:5], refs[5]
    outs, (scaled, extra, codes), (blocks, sems) = refs[6:8], refs[8:11], refs[11:13]
    held, held_sems = refs[13:18], refs[18]
    fetches = [
        pltpu.make_async_copy(source, target, held_sems.at[i])
        for i, (source, target) in enumerate(zip(operands, held))
    ]
    for fetch in fetches:
        fetch.start()
    copies = [weight_copy(weight, blocks, sems, offset, i) for i, offset in enumerate(offsets)]
    for copy in copies:
        copy.start()
    dest, length, gain, fresh, hidden = held
    requests = dest.shape[1]
    context = hidden.shape[0] // requests
    rows, capacity = scaled.shape[0], scaled.shape[0] - fresh.shape[0]
    for fetch in fetches[:2]:
        fetch.wait()
    half = half_of(lax.axis_index("inst"))

    def upright(line):
        diagonal = iota((requests, requests), 0) == iota((requests, requests), 1)
        return jnp.sum(jnp.where(diagonal, line, 0), axis=1, keepdims=True)

    lengths, dests = length[...], dest[...]
    cross = jnp.where(half_of(dests) != half, 1, 0)
    crossing = jnp.sum(cross * lengths, axis=1, keepdims=True)
    cross_up, lengths_up, dests_up = upright(cross), upright(lengths), upright(dests)
    earlier = iota((requests, requests), 1) < iota((requests, requests), 0)
    sooner = (cross > cross_up) | ((cross == cross_up) & earlier)
    start = jnp.sum(jnp.where(sooner, lengths, 0), axis=1, keepdims=True)
    shape = (requests, hidden.shape[0])
    lane = iota(shape, 1)
    at = lane % context
    here = (lane // context == iota(shape, 0)) & (at < lengths_up)
    target = jnp.sum(jnp.where(here, start + at + 1, 0), axis=0, keepdims=True) - 1
    inside = (lane >= start) & (lane < start + lengths_up)
    code = jnp.where(inside, plane_of(dests_up) * context + lane - start + 1, 0)
    code = jnp.sum(code, axis=0, keepdims=True) - 1
    codes[...] = jnp.where(iota(codes.shape, 0) == 0, code, crossing)
    select = jnp.where(target == iota((capacity, hidden.shape[0]), 0), 1.0, 0.0).astype(BF)
    for fetch in fetches[2:]:
        fetch.wait()
    wide = jnp.concatenate([dot(select, hidden[...]), fresh[...].astype(F32)], axis=0)
    scaled[...] = (wide * gain[...]).astype(BF)
    square = wide * wide
    narrow = sum(square[:, i : i + TILE] for i in range(TILE, square.shape[1], TILE))
    column = jnp.sum(narrow + square[:, :TILE], axis=1, keepdims=True)
    lanes = extra.shape[1]
    totals = [jnp.zeros((EXTRA, TILE), F32) for _ in range(0, lanes, TILE)]
    for start in range(0, rows, TILE):
        size = min(TILE, rows - start)
        diagonal = iota((size, TILE), 0) == iota((size, TILE), 1)
        line = jnp.where(diagonal, column[start : start + size], 0.0)
        line = jnp.sum(line, axis=0, keepdims=True)
        place_here = start % lanes // TILE
        totals[place_here] = jnp.where(
            iota((EXTRA, TILE), 0) == start // lanes, line, totals[place_here]
        )
    extra[...] = jnp.concatenate(totals, axis=1).astype(BF)
    for copy in copies:
        copy.wait()
    pair_of_chunks(capacity, scaled, extra, codes, blocks.at[0], blocks.at[1], *outs)


def later_chunks(offsets, capacity, scaled, extra, codes, weight, *refs):
    outs, (blocks, sems) = refs[:-2], refs[-2:]
    copies = [weight_copy(weight, blocks, sems, offset, i) for i, offset in enumerate(offsets)]
    for copy in copies:
        copy.start()
    for i in range(0, len(copies), 2):
        copies[i].wait()
        copies[i + 1].wait()
        pair_of_chunks(
            capacity, scaled, extra, codes, blocks.at[i], blocks.at[i + 1], *outs[i : i + 2]
        )


def project_chunks(hidden, fresh, gain, weight, dest, length, capacity, lanes):
    rows, depth = capacity + fresh.shape[0], hidden.shape[1]
    chunk = jax.ShapeDtypeStruct((rows + EXTRA, lanes), BF)
    tensors = lax.axis_size("tensor")
    offsets = ring_offsets(tensors)
    pairs = []
    for offset in offsets:
        if all(offset not in pair for pair in pairs):
            pairs.append((offset, offset - tensors // 2 if offset > 0 else offset + tensors // 2))
    vmem = pl.BlockSpec(memory_space=pltpu.VMEM)
    hbm = pl.BlockSpec(memory_space=pltpu.HBM)

    def options(count, name, *more):
        return dict(
            scratch_shapes=[
                pltpu.VMEM((count, depth, lanes), BF),
                pltpu.SemaphoreType.DMA((count,)),
                *more,
            ],
            compiler_params=pltpu.CompilerParams(vmem_limit_bytes=VMEM_BYTES),
            cost_estimate=pl.CostEstimate(
                flops=2 * rows * depth * lanes * count,
                bytes_accessed=2 * (rows * depth + count * (depth + rows) * lanes),
                transcendentals=0,
            ),
            name=name,
        )

    operands = [dest[None, :], length[None, :], gain, fresh, hidden]
    *first, scaled, extra, codes = pl.pallas_call(
        functools.partial(first_chunks, pairs[0]),
        in_specs=[hbm] * 6,
        out_shape=[
            chunk,
            chunk,
            jax.ShapeDtypeStruct((rows, depth), BF),
            jax.ShapeDtypeStruct((EXTRA, lanes), BF),
            jax.ShapeDtypeStruct((8, hidden.shape[0]), jnp.int32),
        ],
        **options(
            2,
            "first_chunks",
            *(pltpu.VMEM(operand.shape, operand.dtype) for operand in operands),
            pltpu.SemaphoreType.DMA((len(operands),)),
        ),
    )(*operands, weight)
    chunks = dict(zip(pairs[0], first))
    for group, name in ((pairs[1:2], "second_chunks"), (pairs[2:], "later_chunks")):
        group = [offset for pair in group for offset in pair]
        outs = pl.pallas_call(
            functools.partial(later_chunks, group, capacity),
            in_specs=[vmem, vmem, vmem, hbm],
            out_shape=[chunk] * len(group),
            **options(len(group), name),
        )(scaled, extra, codes, weight)
        chunks.update(zip(group, outs))
    return [chunks[offset] for offset in offsets], codes


def ring_offsets(tensors):
    ahead = tensors // 2
    behind = tensors - 1 - ahead
    offsets = []
    for step in range(ahead):
        offsets.append(ahead - step)
        if step < behind:
            offsets.append(step - behind)
    return offsets + [0]


def ring_order(tensors):
    ring = ring_of(tensors)
    offsets = jnp.array(ring_offsets(tensors), jnp.int32)
    at = jnp.array([ring.index(i) for i in range(tensors)], jnp.int32)[lax.axis_index("tensor")]
    sense = 1 - 2 * core_of(lax.axis_index("inst"))
    return jnp.array(ring, jnp.int32)[(at + sense * offsets + tensors) % tensors]


def ring_sums(chunks):
    tensors = lax.axis_size("tensor")
    ring = ring_of(tensors)
    links = [(ring[i], ring[(i + 1) % tensors]) for i in range(tensors)]
    forward, backward = [], []
    for instance in range(lax.axis_size("inst")):
        ways = (forward, backward) if core_of(instance) == 0 else (backward, forward)
        for a, b in links:
            a, b = instance * tensors + a, instance * tensors + b
            ways[0].append((a, b))
            ways[1].append((b, a))
    sums = {True: None, False: None}
    for offset, chunk in zip(ring_offsets(tensors), chunks[:-1]):
        way = offset > 0
        if sums[way] is not None:
            chunk = (sums[way].astype(F32) + chunk.astype(F32)).astype(BF)
        sums[way] = lax.ppermute(chunk, ("inst", "tensor"), forward if way else backward)
    return sums[True], sums[False], chunks[-1]


def finish_rows(codes, ahead, behind, own, crossing_rows, kept):
    total = ahead[...].astype(F32) + behind[...].astype(F32) + own[...].astype(F32)
    rows, lanes = kept.shape
    squares = total[rows:]
    for start in range(0, rows, TILE):
        size = min(TILE, rows - start)
        across = squares[start // lanes : start // lanes + 1, start % lanes : start % lanes + TILE]
        diagonal = iota((size, TILE), 0) == iota((size, TILE), 1)
        column = jnp.sum(jnp.where(diagonal, across, 0.0), axis=1, keepdims=True)
        kept[start : start + size, :] = (
            total[start : start + size] * lax.rsqrt(column / D + 1e-06)
        ).astype(BF)
    sent = crossing_rows.shape[0] - EXTRA
    crossing_rows[:sent, :] = kept[:sent, :]
    wide = min(lanes, codes.shape[1])
    code, count = codes[0:1, :wide], codes[1:2, :wide]
    if wide < lanes:
        code = jnp.concatenate([code, jnp.zeros((1, lanes - wide), jnp.int32)], axis=1)
        count = jnp.concatenate([count, jnp.zeros((1, lanes - wide), jnp.int32)], axis=1)
    lane, line = iota((EXTRA, lanes), 1), iota((EXTRA, lanes), 0)
    used = (lane < count) & (lane < sent)
    notes = jnp.where(used, code // CONTEXT, NOWHERE)
    notes = jnp.where(line == 1, code % CONTEXT, notes)
    notes = jnp.where(line == 2, count // CONTEXT, notes)
    notes = jnp.where(line == 3, count % CONTEXT, notes)
    crossing_rows[sent:, :] = notes.astype(F32).astype(BF)


def finish(codes, ahead, behind, own, sent):
    rows, lanes = own.shape[0] - EXTRA, own.shape[1]
    return pl.pallas_call(
        finish_rows,
        out_shape=[
            jax.ShapeDtypeStruct((sent + EXTRA, lanes), BF),
            jax.ShapeDtypeStruct((rows, lanes), BF),
        ],
        compiler_params=pltpu.CompilerParams(vmem_limit_bytes=VMEM_BYTES),
        name="finish_rows",
    )(codes, ahead, behind, own)


def routed(route, rows):
    narrow = route.astype(BF)
    found = dot(narrow, jnp.ones((route.shape[1], rows.shape[1]), BF))
    return jnp.where(found > 0.5, dot(narrow, rows), ABSENT).astype(BF)


def place_staying(codes, first, second, out):
    capacity = codes.shape[1] - second.shape[0]
    slots, context, lanes = out.shape
    shape = (slots * context, codes.shape[1])
    code, crossing = codes[0:1, :], codes[1:2, :]
    route = (iota(shape, 0) == code) & (iota(shape, 1) >= crossing)
    rows = jnp.concatenate([first[:capacity, :], second[...]], axis=0)
    out[...] = routed(jnp.where(route, 1.0, 0.0), rows).reshape(out.shape)


def place_crossing(received, codes, near, out, most):
    slots, context, lanes = near.shape
    sent = received.shape[0] - EXTRA
    notes = received[sent:, :].astype(F32).astype(jnp.int32)
    code = notes[0:1, :sent] * context + notes[1:2, :sent]
    route = iota((slots * context, sent), 0) == code
    out[:, :context, :] = near[...]
    out[:, context:, :] = routed(jnp.where(route, 1.0, 0.0), received[:sent, :]).reshape(near.shape)
    counts = jnp.maximum(notes[2:3, :sent] * context + notes[3:4, :sent], codes[1:2, :sent])
    most[0] = jnp.max(counts)


def place(kernel, out_shape, out_specs, *operands):
    return pl.pallas_call(
        kernel,
        out_shape=out_shape,
        out_specs=out_specs,
        compiler_params=pltpu.CompilerParams(vmem_limit_bytes=VMEM_BYTES),
        name=kernel.__name__,
    )(*operands)


def rebuild_and_attend(
    arrived, resident, resident_valid, queries, kept, wanted, rebuilt, attended
):
    plane, context, lanes = arrived.shape
    slots, context = 2 * plane, context // 2
    steps, batch, width = queries.shape
    rows = slots * context
    fresh = kept[kept.shape[0] - steps * batch :, :]
    columns = rebuilt.shape[1]
    held = resident.shape[1]
    heads = width // HD
    blocks = arrived[...].reshape(rows, lanes)
    half = half_of(lax.axis_index("inst"))

    def instance_of(slot):
        place = slot >> 1
        there = jnp.where(slot % 2 == 0, half, 1 - half)
        return (place >> 1) * 4 + there * 2 + (place & 1)

    valid = blocks[:, :TILE].astype(F32) < ABSENT / 2
    flags = jnp.where(valid, 1.0, 0.0).astype(BF)
    opening = jnp.where(iota((slots, rows), 1) == iota((slots, rows), 0) * context, 1.0, 0.0)
    living = dot(opening.astype(BF), flags).astype(BF)
    sooner = instance_of(iota((rows, slots), 1)) < instance_of(iota((rows, slots), 0) // context)
    before = jnp.where(sooner, 1.0, 0.0)
    ranking = dot(before.astype(BF), living)
    target = ranking.astype(jnp.int32) * context + iota((rows, TILE), 0) % context
    target = jnp.where(valid, target, -1)
    routes = jnp.concatenate(
        [
            jnp.where(target == iota((rows, TILE), 1) + start, 1.0, 0.0)
            for start in range(0, columns, TILE)
        ],
        axis=1,
    )[:, :columns]
    filled = jnp.sum(routes, axis=0, keepdims=True) > 0.5
    moved = dot(blocks, routes.astype(BF), ((0,), (0,))).astype(BF)
    rebuilt[...] = moved

    query = jnp.concatenate(
        [queries[s, :, h * HD : (h + 1) * HD] for s in range(steps) for h in range(heads)], axis=0
    )
    count = query.shape[0]
    scale = 1.0 / HD**0.5
    want = wanted[...]

    def request_of(size):
        return iota((count, size), 1) // context

    mask_held = (want == request_of(held)) & (resident_valid[...] > 0)
    mask_moved = (want == request_of(columns) + held // context) & filled
    line, mark = iota((count, steps * batch), 0), iota((count, steps * batch), 1)
    mask_fresh = (line % batch == mark % batch) & (mark // batch <= line // (heads * batch))
    lowest = -1e30
    score_held = jnp.where(mask_held, dot(query, resident[:HD, :]) * scale, lowest)
    score_moved = jnp.where(mask_moved, dot(query, moved[:HD]) * scale, lowest)
    score_fresh = jnp.where(
        mask_fresh, dot(query, fresh[:, :HD], ((1,), (1,))) * scale, lowest
    )
    top = jnp.maximum(
        jnp.maximum(
            jnp.max(score_held, axis=1, keepdims=True), jnp.max(score_moved, axis=1, keepdims=True)
        ),
        jnp.max(score_fresh, axis=1, keepdims=True),
    )
    exp_held = jnp.where(mask_held, jnp.exp(score_held - top), 0.0)
    exp_moved = jnp.where(mask_moved, jnp.exp(score_moved - top), 0.0)
    exp_fresh = jnp.where(mask_fresh, jnp.exp(score_fresh - top), 0.0)
    total = (
        jnp.sum(exp_held, axis=1, keepdims=True)
        + jnp.sum(exp_moved, axis=1, keepdims=True)
        + jnp.sum(exp_fresh, axis=1, keepdims=True)
    )
    share = 1.0 / total
    across = ((1,), (1,))
    out = dot((exp_held * share).astype(BF), resident[HD:, :], across)
    out = out + dot((exp_moved * share).astype(BF), moved[HD:], across)
    out = out + dot((exp_fresh * share).astype(BF), fresh[:, HD:])
    out = out.astype(BF)
    for s in range(steps):
        for h in range(heads):
            start = (s * heads + h) * batch
            attended[s, :, h * HD : (h + 1) * HD] = out[start : start + batch]


def rebuild(arrived, resident, resident_valid, queries, kept, wanted, columns):
    return pl.pallas_call(
        rebuild_and_attend,
        out_shape=[
            jax.ShapeDtypeStruct((arrived.shape[2], columns), BF),
            jax.ShapeDtypeStruct(queries.shape, BF),
        ],
        compiler_params=pltpu.CompilerParams(vmem_limit_bytes=VMEM_BYTES),
        name="rebuild_and_attend",
    )(arrived, resident, resident_valid, queries, kept, wanted)


def remaining_rows(hidden, gain, weight, codes, target_of, capacity, lanes):
    tensors = lax.axis_size("tensor")
    left = hidden.shape[0] - capacity
    select = (target_of[None, :] == capacity + jnp.arange(left, dtype=jnp.int32)[:, None]).astype(BF)
    wide = jnp.dot(select, hidden, preferred_element_type=F32)
    squares = jnp.sum(wide * wide, axis=1)
    distance = 1
    while distance < tensors:
        pairs = [(i, i ^ distance) for i in range(tensors)]
        squares = squares + lax.ppermute(squares, "tensor", pairs)
        distance *= 2
    parts = jnp.dot((wide * gain).astype(BF), weight, preferred_element_type=F32).astype(BF)
    order = ring_order(tensors)
    crosses = capacity + jnp.arange(left, dtype=jnp.int32)[:, None] < codes[1, 0]

    def block_of(owner):
        return lax.dynamic_slice_in_dim(parts, owner * lanes, lanes, 1)

    chunks = [
        jnp.where(crosses, block_of(tensors - 1 - order[i]), block_of(order[i]))
        for i in range(tensors)
    ]
    ahead, behind, own = ring_sums(chunks)
    total = ahead.astype(F32) + behind.astype(F32) + own.astype(F32)
    return (total * lax.rsqrt(squares / D + 1e-06)[:, None]).astype(BF)


def shards(
    hidden_rows,
    kv_weight,
    norm_gain,
    resident_cache,
    queries,
    fresh_hidden,
    move_dest,
    move_len,
    resident_len,
    decode_ids,
):
    requests = move_dest.shape[0]
    leaving = hidden_rows.shape[0]
    context = leaving // requests
    instances = lax.axis_size("inst")
    owned = kv_weight.shape[1] // lax.axis_size("tensor")
    assert owned == 2 * HD and context == CONTEXT
    steps, batch_rows, features = fresh_hidden.shape
    heads = queries.shape[2] // HD
    fresh_rows = steps * batch_rows
    capacity = max(leaving * 23 // 32 // 16, 1) * 16
    sent = max(leaving * 15 // 32 // 16, 1) * 16
    plane = instances // 2
    mine = lax.axis_index("inst").astype(jnp.int32)[None]
    fresh = fresh_hidden.reshape(fresh_rows, features)
    gain = norm_gain[None, :]
    resident_valid = (
        jnp.arange(context, dtype=jnp.int32)[None, :] < resident_len[:, None]
    ).astype(jnp.int32)
    resident_valid = resident_valid.reshape(1, -1)
    wanted = jnp.tile(decode_ids, steps * heads)[:, None]

    chunks, codes = project_chunks(
        hidden_rows, fresh, gain, kv_weight, move_dest, move_len, capacity, owned
    )
    ahead, behind, own = ring_sums(chunks)
    crossing_rows, kept = finish(codes, ahead, behind, own, sent)

    def second_pass():
        cross = half_of(move_dest) != half_of(mine)
        index = jnp.arange(requests, dtype=jnp.int32)
        sooner = (cross[:, None] > cross[None, :]) | (
            (cross[:, None] == cross[None, :]) & (index[:, None] < index[None, :])
        )
        start = jnp.sum(jnp.where(sooner, move_len[:, None], 0), axis=0)
        position = jnp.arange(context, dtype=jnp.int32)[None, :]
        target = jnp.where(position < move_len[:, None], start[:, None] + position, -1)
        return remaining_rows(
            hidden_rows, gain, kv_weight, codes, target.reshape(-1), capacity, owned
        )

    rest = lax.cond(
        jnp.sum(move_len) > capacity,
        second_pass,
        lambda: jnp.zeros((leaving - capacity, owned), BF),
    )

    tensors = lax.axis_size("tensor")
    halves = [
        (i * tensors + t, (i ^ 2) * tensors + tensors - 1 - t)
        for i in range(instances)
        for t in range(tensors)
    ]
    planes = [[i for i in range(instances) if half_of(i) == half] for half in range(2)]

    received = lax.ppermute(crossing_rows, ("inst", "tensor"), halves)
    blocks_type = jax.ShapeDtypeStruct((plane, context, owned), BF)
    vmem = pl.BlockSpec(memory_space=pltpu.VMEM)
    near = place(place_staying, blocks_type, vmem, codes, kept, rest)
    both_type = jax.ShapeDtypeStruct((plane, 2 * context, owned), BF)
    most_type = jax.ShapeDtypeStruct((1,), jnp.int32)
    outgoing, most = place(
        place_crossing,
        (both_type, most_type),
        (vmem, pl.BlockSpec(memory_space=pltpu.SMEM)),
        received,
        codes,
        near,
    )

    def all_crossing():
        rows = jnp.concatenate([kept[:capacity], rest], axis=0)
        rows = lax.ppermute(rows, ("inst", "tensor"), halves)
        notes = lax.ppermute(codes, ("inst", "tensor"), halves)
        lane = jnp.arange(leaving, dtype=jnp.int32)[None, :]
        slot = jnp.arange(plane * context, dtype=jnp.int32)[:, None]
        route = (slot == notes[0:1]) & (lane < notes[1:2])
        far = routed(route.astype(F32), rows).reshape(near.shape)
        return jnp.concatenate([near, far], axis=1)

    outgoing = lax.cond(most[0] > sent, all_crossing, lambda: outgoing)
    arrived = lax.all_to_all(
        outgoing, "inst", split_axis=0, concat_axis=0, tiled=True, axis_index_groups=planes
    )
    return tuple(
        rebuild(arrived, resident_cache, resident_valid, queries, kept, wanted, leaving)
    )


def solution(mesh):
    in_specs = (
        P("inst", "tensor"),
        P("tensor", None),
        P("tensor"),
        P("tensor", "inst"),
        P(None, "inst", "tensor"),
        P(None, "inst", "tensor"),
        P("inst"),
        P("inst"),
        P("inst"),
        P("inst"),
    )
    out_specs = (P("tensor", "inst"), P(None, "inst", "tensor"))
    return jax.shard_map(shards, mesh=mesh, in_specs=in_specs, out_specs=out_specs, check_vma=False)
```
